32 devices in a mesh: clip: 8 (over z, x), seg: 4 (over y, core).
Axes of the slice: x: 2, y: 2, z: 4, core: 2. Of those that a mesh axis runs over, the one named last changes fastest.
Arguments:
- frames: bfloat16 [32, 4, 5, 48, 48, 3], P('clip', 'seg'), may hold values from -6 to 6
- features: bfloat16 [32, 4, 8, 8, 2048], P('clip', 'seg'), may hold values from -6 to 6
- res_group: int32 [32], replicated, may hold values from 0 to 2
- stem_weight: bfloat16 [7, 7, 3, 64], replicated, may hold values from -0.5 to 0.5
- diff_weight: bfloat16 [3, 3, 12, 64], replicated, may hold values from -1.75 to 1.75
- stem_gain: float32 [64], replicated, may hold values from 0.1 to 1.9
- stem_bias: float32 [64], replicated, may hold values from -0.5 to 0.5
- w_reduce: bfloat16 [2048, 512], replicated, may hold values from -0.125 to 0.125
- gain_one: float32 [512], replicated, may hold values from 0.1 to 1.9
- bias_one: float32 [512], replicated, may hold values from -0.5 to 0.5
- w_spatial: bfloat16 [3, 3, 512, 512], replicated, may hold values from -0.09375 to 0.09375
- gain_two: float32 [512], replicated, may hold values from 0.1 to 1.9
- bias_two: float32 [512], replicated, may hold values from -0.5 to 0.5
- w_expand: bfloat16 [512, 2048], replicated, may hold values from -0.25 to 0.25
- gain_three: float32 [2048], replicated, may hold values from 0.1 to 1.9
- bias_three: float32 [2048], replicated, may hold values from -0.5 to 0.5
- w_squeeze: bfloat16 [2048, 128], replicated, may hold values from -0.125 to 0.125
- w_fine: bfloat16 [3, 3, 128, 128], replicated, may hold values from -0.1875 to 0.1875
- w_coarse: bfloat16 [3, 3, 128, 128], replicated, may hold values from -0.1875 to 0.1875
- w_excite: bfloat16 [128, 2048], replicated, may hold values from -0.25 to 0.25
- stem_cotangent: bfloat16 [32, 4, 24, 24, 64], P('clip', 'seg'), may hold values from -6 to 6
- block_cotangent: bfloat16 [32, 4, 8, 8, 2048], P('clip', 'seg'), may hold values from -6 to 6
Outputs:
- stem_out: bfloat16 [32, 4, 24, 24, 64], P('clip', 'seg')
- block_out: bfloat16 [32, 4, 8, 8, 2048], P('clip', 'seg')
- grad_features: bfloat16 [32, 4, 8, 8, 2048], P('clip', 'seg')
- grad_stem_weight: float32 [7, 7, 3, 64], replicated
- grad_diff_weight: float32 [3, 3, 12, 64], replicated
- grad_stem_gain: float32 [64], replicated
- grad_stem_bias: float32 [64], replicated
- grad_w_reduce: float32 [2048, 512], replicated
- grad_gain_one: float32 [512], replicated
- grad_bias_one: float32 [512], replicated
- grad_w_spatial: float32 [3, 3, 512, 512], replicated
- grad_gain_two: float32 [512], replicated
- grad_bias_two: float32 [512], replicated
- grad_w_expand: float32 [512, 2048], replicated
- grad_gain_three: float32 [2048], replicated
- grad_bias_three: float32 [2048], replicated
- grad_w_squeeze: float32 [2048, 128], replicated
- grad_w_fine: float32 [3, 3, 128, 128], replicated
- grad_w_coarse: float32 [3, 3, 128, 128], replicated
- grad_w_excite: float32 [128, 2048], replicated
The draws below stay inside these ranges and needn't reach their ends.
Inputs may be any that keep to these rules, and one draw needn't show every extreme that they name: `res_group`: groups 0, 1, 2 have valid feature grids of 5, 7, 8 cells on a side, placed at the grid's first rows and columns.
All inputs are finite; a program needn't handle non-finite values.
Results may differ from the reference program's by a relative error of at most 0.015.
Values may be sent and summed in bfloat16 or wider, within the bound.
A program may use at most 192 MiB of HBM per device.

```python
import jax
import jax.numpy as jnp
from jax import lax

STEM = 64
WIDE = 2048
MID = 512
RED = 128
IMG = 48
GRID = 8
FRAMES = 5
SEG = 4
CLIPS = 32


def touch_ends(array, stream_key, least, high):
    dims = array.shape
    index_at = [jax.random.randint(jax.random.fold_in(stream_key, axis), (), 0, dims[axis]) for axis in range(len(dims))]
    array = array.at[tuple(index_at)].set(least)
    longest = dims.index(max(dims))
    index_at[longest] = (index_at[longest] + 1) % dims[longest]
    return array.at[tuple(index_at)].set(high)


def levels(own_key, shape, pieces, low, largest):
    factor_of, own = 1.0, jax.random.fold_in(own_key, 6)
    for position, blocks in pieces:
        heights = jnp.exp(jax.random.uniform(jax.random.fold_in(own, position), (blocks,), jnp.float32, low / len(pieces), largest / len(pieces)))
        factor_of = factor_of * jnp.repeat(heights, shape[position] // blocks).reshape([-1 if axis == position else 1 for axis in range(len(shape))])
    return factor_of


def noise(stream_key, shape, deviation, bound, split=(), kind=jnp.bfloat16):
    level = levels(stream_key, shape, split, -0.22, 0.18) if split else 1.0
    array = jax.random.normal(stream_key, shape, jnp.float32) * deviation * level
    return jnp.minimum(jnp.maximum(array, -bound), bound).astype(kind)


def setup_inputs(seed: int = 0) -> dict:
    arg_keys = jax.random.split(jax.random.key(seed), 23)
    return {
        "frames": noise(arg_keys[0], (CLIPS, SEG, FRAMES, IMG, IMG, 3), 1.0, 6.0, ((0, 8), (1, 4))),
        "features": noise(arg_keys[1], (CLIPS, SEG, GRID, GRID, WIDE), 1.0, 6.0, ((0, 8), (1, 4))),
        "res_group": touch_ends(jax.random.randint(arg_keys[2], (CLIPS,), 0, 3), jax.random.fold_in(arg_keys[2], 1), 0, 2).astype(jnp.int32),
        "stem_weight": noise(arg_keys[3], (7, 7, 3, STEM), 147 ** -0.5, 0.5),
        "diff_weight": noise(arg_keys[4], (3, 3, 12, STEM), 12 ** -0.5, 1.75),
        "stem_gain": jnp.clip(1.0 + 0.18 * jax.random.normal(arg_keys[5], (STEM,), jnp.float32), 0.1, 1.9),
        "stem_bias": jnp.clip(jax.random.uniform(arg_keys[6], (STEM,), jnp.float32, -0.5, 0.5), -0.5, 0.5),
        "w_reduce": noise(arg_keys[7], (WIDE, MID), WIDE ** -0.5, 0.125),
        "gain_one": jnp.clip(1.0 + 0.18 * jax.random.normal(arg_keys[8], (MID,), jnp.float32), 0.1, 1.9),
        "bias_one": jnp.clip(jax.random.uniform(arg_keys[9], (MID,), jnp.float32, -0.5, 0.5), -0.5, 0.5),
        "w_spatial": noise(arg_keys[10], (3, 3, MID, MID), (9 * MID) ** -0.5, 0.09375),
        "gain_two": jnp.clip(1.0 + 0.18 * jax.random.normal(arg_keys[11], (MID,), jnp.float32), 0.1, 1.9),
        "bias_two": jnp.clip(jax.random.uniform(arg_keys[12], (MID,), jnp.float32, -0.5, 0.5), -0.5, 0.5),
        "w_expand": noise(arg_keys[13], (MID, WIDE), MID ** -0.5, 0.25),
        "gain_three": jnp.clip(1.0 + 0.18 * jax.random.normal(arg_keys[14], (WIDE,), jnp.float32), 0.1, 1.9),
        "bias_three": jnp.clip(jax.random.uniform(arg_keys[15], (WIDE,), jnp.float32, -0.5, 0.5), -0.5, 0.5),
        "w_squeeze": noise(arg_keys[16], (WIDE, RED), WIDE ** -0.5, 0.125),
        "w_fine": noise(arg_keys[17], (3, 3, RED, RED), (9 * RED) ** -0.5, 0.1875),
        "w_coarse": noise(arg_keys[18], (3, 3, RED, RED), (9 * RED) ** -0.5, 0.1875),
        "w_excite": noise(arg_keys[19], (RED, WIDE), (4 * RED) ** -0.5, 0.25),
        "stem_cotangent": noise(arg_keys[20], (CLIPS, SEG, IMG // 2, IMG // 2, STEM), 1.0, 6.0, ((0, 8), (1, 4))),
        "block_cotangent": noise(arg_keys[21], (CLIPS, SEG, GRID, GRID, WIDE), 1.0, 6.0, ((0, 8), (1, 4))),
    }


@jax.custom_vjp
def low(v):
    return lax.optimization_barrier(v.astype(jnp.bfloat16)).astype(jnp.float32)

@jax.custom_vjp
def low_back(v):
    return v

def low_keep(v):
    return (low(v), None)

def low_pass(kept, grad):
    return (grad,)

def back_keep(v):
    return (v, None)

def back_low(kept, grad):
    return (low(grad),)
low.defvjp(low_keep, low_pass)
low_back.defvjp(back_keep, back_low)

def silu_act(values):
    return values * jax.nn.sigmoid(values)

def convolve(image, kernel, stride):
    return lax.conv_general_dilated(image, kernel, (stride, stride), 'SAME', dimension_numbers=('NHWC', 'HWIO', 'NHWC'), precision=lax.Precision.HIGHEST)

def project(values, weight):
    return jnp.einsum('abcdk,kn->abcdn', values, weight, precision=lax.Precision.HIGHEST)

def block_pool(image, factor):
    total, height, breadth, chans = image.shape
    return lax.optimization_barrier(jnp.mean(image.reshape(total, height // factor, factor, breadth // factor, factor, chans), axis=(2, 4)))

def upsample(image):
    return jnp.repeat(jnp.repeat(image, 2, axis=1), 2, axis=2)

def local_moments(values, mask):
    axes = tuple(range(values.ndim - 1))
    weighted = values * mask
    return (lax.optimization_barrier(jnp.sum(weighted, axis=axes)), lax.optimization_barrier(jnp.sum(weighted * values, axis=axes)))

def normalize(values, sums, count, gain, bias):
    mean = sums[0] / count
    spread = sums[1] / count - mean * mean
    return (values - mean) * lax.rsqrt(spread + 1e-05) * gain + bias

def spatial(values, weight):
    lead = values.shape
    flat = values.reshape(lead[0] * lead[1], lead[2], lead[3], lead[4])
    return convolve(flat, weight, 1).reshape(lead[0], lead[1], lead[2], lead[3], weight.shape[3])

def multi_scale(diff, w_fine, w_coarse):
    lead = diff.shape
    flat = diff.reshape(lead[0] * lead[1], lead[2], lead[3], lead[4])
    fine = convolve(flat, w_fine, 1)
    coarse = upsample(convolve(low(block_pool(flat, 2)), w_coarse, 1))
    return (fine + coarse).reshape(lead)

def make_mask(groups, grid):
    side = 5 + 2 * groups - groups // 2
    cells = jnp.arange(grid, dtype=jnp.int32)
    inside = (cells[None, :] < side[:, None]).astype(jnp.float32)
    return inside[:, None, :, None, None] * inside[:, None, None, :, None]

def stem_front(frames, stem_weight, diff_weight):
    images = frames.shape[0] * frames.shape[1]
    side = frames.shape[3]
    centre = frames[:, :, 2].reshape(images, side, side, 3)
    diffs = jnp.moveaxis(frames[:, :, 1:] - frames[:, :, :-1], 2, 4).reshape(images, side, side, 12)
    pooled = low(block_pool(diffs, 4))
    motion = upsample(convolve(pooled, diff_weight, 1))
    return low_back(convolve(centre, stem_weight, 2) + motion)

def reference(frames, features, res_group, stem_weight, diff_weight, stem_gain, stem_bias, w_reduce, gain_one, bias_one, w_spatial, gain_two, bias_two, w_expand, gain_three, bias_three, w_squeeze, w_fine, w_coarse, w_excite, stem_cotangent, block_cotangent):
    frames32 = frames.astype(jnp.float32)
    mask = make_mask(res_group, GRID)
    count = jnp.sum(mask) * SEG
    params = tuple((item.astype(jnp.float32) for item in (stem_weight, diff_weight, stem_gain, stem_bias, w_reduce, gain_one, bias_one, w_spatial, gain_two, bias_two, w_expand, gain_three, bias_three, w_squeeze, w_fine, w_coarse, w_excite)))

    def whole(weights, feats):
        s_weight, d_weight, s_gain, s_bias, reduce_w, g_one, b_one, spatial_w, g_two, b_two, expand_w, g_three, b_three, squeeze_w, fine_w, coarse_w, excite_w = weights
        pre = stem_front(frames32, s_weight, d_weight)
        stem_count = float(pre.shape[0] * pre.shape[1] * pre.shape[2])
        stem_norm = normalize(pre, local_moments(pre, 1.0), stem_count, s_gain, s_bias)
        stem_result = silu_act(stem_norm).reshape(frames.shape[0], frames.shape[1], pre.shape[1], pre.shape[2], pre.shape[3])
        inputs = feats * mask
        first = low_back(project(inputs, reduce_w))
        hidden = low(silu_act(normalize(first, local_moments(first, mask), count, g_one, b_one)) * mask)
        second = low_back(spatial(hidden, spatial_w))
        hidden = low(silu_act(normalize(second, local_moments(second, mask), count, g_two, b_two)) * mask)
        third = low_back(project(hidden, expand_w))
        branch = normalize(third, local_moments(third, mask), count, g_three, b_three) * mask
        squeezed = low(project(low(branch), squeeze_w))
        earlier = jnp.pad(squeezed[:, :-1], ((0, 0), (1, 0), (0, 0), (0, 0), (0, 0)))
        later = jnp.pad(squeezed[:, 1:], ((0, 0), (0, 1), (0, 0), (0, 0), (0, 0)))
        motion = multi_scale(low(later - squeezed), fine_w, coarse_w) + multi_scale(low(earlier - squeezed), fine_w, coarse_w)
        gate = jax.nn.sigmoid(project(low(motion), excite_w))
        block_result = silu_act(inputs + branch * (1.0 + gate)) * mask
        return (stem_result, block_result)
    (stem_result, block_result), pullback = jax.vjp(whole, params, features.astype(jnp.float32))
    grads, grad_feats = pullback((stem_cotangent.astype(jnp.float32), block_cotangent.astype(jnp.float32)))
    return (stem_result.astype(jnp.bfloat16), block_result.astype(jnp.bfloat16), grad_feats.astype(jnp.bfloat16), grads[0], grads[1], grads[2], grads[3], grads[4], grads[5], grads[6], grads[7], grads[8], grads[9], grads[10], grads[11], grads[12], grads[13], grads[14], grads[15], grads[16])
```

```python
from functools import partial
from types import SimpleNamespace

import jax
import jax.numpy as jnp
from jax import lax
from jax.experimental import pallas as pl
from jax.experimental.pallas import tpu as pltpu
from jax.sharding import PartitionSpec as P

MESH = pl.DeviceIdType.MESH
F32, BF16 = jnp.float32, jnp.bfloat16
LANES = 128
BLOCK = 64
PAD = 16
TAPS = [(di, dj) for di in (-1, 0, 1) for dj in (-1, 0, 1)]


def dot(a, b):
    return lax.dot_general(a, b, (((1,), (0,)), ((), ())), preferred_element_type=F32)


def dot_bt(a, b):
    return lax.dot_general(a, b, (((1,), (1,)), ((), ())), preferred_element_type=F32)


def dot_at(a, b):
    return lax.dot_general(a, b, (((0,), (0,)), ((), ())), preferred_element_type=F32)


def columns(total, body, step=LANES):
    def go(j, carry):
        body(pl.multiple_of(j * step, step), j)
        return carry

    lax.fori_loop(0, total // step, go, 0)


def lanes(start, size=LANES):
    return pl.ds(start, size)


def fold(block):
    return block.reshape(block.shape[0] // 8, 8, LANES).sum(axis=0)


def total_of(part):
    return jnp.sum(part, axis=0, keepdims=True)


class Sems:
    def __init__(self, ref):
        self.ref, self.used = ref, 0

    def take(self):
        self.used += 1
        return self.ref.at[self.used - 1]


class Place:
    def __init__(self, clips, segs):
        self.clips, self.segs = clips, segs
        self.clip, self.seg = lax.axis_index("clip"), lax.axis_index("seg")
        self.near = 2 * segs
        self.far = clips // 2
        self.near_me = lax.rem(self.clip, 2) * segs + self.seg
        self.far_me = self.clip // 2

    def near_device(self, t):
        return ((self.clip // 2) * 2 + t // self.segs, lax.rem(t, self.segs))

    def far_device(self, t):
        return (t * 2 + lax.rem(self.clip, 2), self.seg)

    def bit(self, axis, stride):
        mine = self.seg if axis == "seg" else self.clip
        bit = lax.rem(mine // stride, 2)
        other = mine + stride * (1 - 2 * bit)
        return bit, (self.clip, other) if axis == "seg" else (other, self.seg)

    def greet(self):
        sem = pltpu.get_barrier_semaphore()

        def near(k, carry):
            pl.semaphore_signal(
                sem, inc=1, device_id=self.near_device(lax.rem(self.near_me + k, self.near)), device_id_type=MESH
            )
            return carry

        def far(k, carry):
            pl.semaphore_signal(
                sem, inc=1, device_id=self.far_device(lax.rem(self.far_me + k, self.far)), device_id_type=MESH
            )
            return carry

        lax.fori_loop(1, self.near, near, 0)
        lax.fori_loop(1, self.far, far, 0)
        pl.semaphore_wait(sem, self.near + self.far - 2)


def remote(src, dst, sends, recvs, device):
    copy = pltpu.make_async_remote_copy(
        src_ref=src,
        dst_ref=dst,
        send_sem=sends.take(),
        recv_sem=recvs.take(),
        device_id=device,
        device_id_type=MESH,
    )
    copy.start()
    return copy


class Sums:
    def __init__(self, place, near_buf, far_buf, result, sends, recvs):
        self.place, self.near_buf, self.far_buf, self.result = place, near_buf, far_buf, result
        self.sends, self.recvs = sends, recvs

    def put(self, row, at, value):
        self.near_buf[self.place.near_me, row : row + 1, lanes(at, value.shape[1])] = value

    def _send(self, buf, me, count, device):
        mine = buf.at[me]
        return [remote(mine, mine, self.sends, self.recvs, device(lax.rem(me + k, count))) for k in range(1, count)]

    def _add(self, buf, count):
        value = buf[0]
        for k in range(1, count):
            value = value + buf[k]
        return value

    def start(self):
        p = self.place
        self.copies = self._send(self.near_buf, p.near_me, p.near, p.near_device)

    def middle(self):
        p = self.place
        for copy in self.copies:
            copy.wait()
        self.far_buf[p.far_me] = self._add(self.near_buf, p.near)
        self.copies = self._send(self.far_buf, p.far_me, p.far, p.far_device)

    def finish(self):
        for copy in self.copies:
            copy.wait()
        self.result[...] = self._add(self.far_buf, self.place.far)


def bit_order(clips, segs, kind):
    seg = [("seg", 1 << k) for k in range(segs.bit_length() - 1)]
    clip = [("clip", 1 << k) for k in range(clips.bit_length() - 1)]
    if kind == 0:
        return seg[:1] + clip[:1] + seg[1:] + clip[1:]
    return seg + clip


def halvings(rows, order):
    steps = []
    for _ in order:
        half = rows // 2
        if rows % 2 == 0 and half % 16 == 0:
            steps.append((rows, half, True))
            rows = half
        else:
            steps.append((rows, rows, False))
    return steps


class Job:
    def __init__(self, place, grads, landing, packed, base, rows, order, land, local, sends, recvs):
        self.grads, self.landing, self.packed = grads, landing, packed
        self.local, self.sends, self.recvs = local, sends, recvs
        self.steps = []
        at = base
        for (axis, stride), (size, sent, halved) in zip(order, halvings(rows, order)):
            bit, device = place.bit(axis, stride)
            if halved:
                keep, away = at + bit * sent, at + (1 - bit) * sent
            else:
                keep, away = at, at
            self.steps.append((keep, away, sent, halved, device, land))
            land += sent
            at = keep
        self.land_end = land
        self.at = 0

    def _rows(self, ref, start, size):
        return ref.at[pl.ds(pl.multiple_of(start, 16), size)]

    def scatter_start(self):
        keep, away, size, halved, device, land = self.steps[self.at]
        self.copy = remote(
            self._rows(self.grads, away, size), self._rows(self.landing, land, size), self.sends, self.recvs, device
        )

    def scatter_finish(self):
        keep, away, size, halved, device, land = self.steps[self.at]
        self.copy.wait()
        block = 32 if size % 32 == 0 else 16

        def add(k, carry):
            mine = pl.ds(pl.multiple_of(keep + k * block, 16), block)
            theirs = pl.ds(pl.multiple_of(land + k * block, 16), block)
            self.grads[mine] = (self.grads[mine].astype(F32) + self.landing[theirs].astype(F32)).astype(BF16)
            return carry

        lax.fori_loop(0, size // block, add, 0)
        self.at += 1

    def own_start(self):
        keep, away, size, halved, device, land = self.steps[-1]
        self.copy = pltpu.make_async_copy(
            self._rows(self.grads, keep, size), self._rows(self.packed, keep, size), self.local.take()
        )
        self.copy.start()

    def own_finish(self):
        self.copy.wait()

    def gather_start(self):
        keep, away, size, halved, device, land = self.steps[self.at - 1]
        self.copy = None
        if halved:
            mine = self._rows(self.packed, keep, size)
            self.copy = remote(mine, mine, self.sends, self.recvs, device)

    def gather_finish(self):
        self.at -= 1
        if self.copy is not None:
            self.copy.wait()


def landing_rows(rows, order):
    return sum(sent for _, sent, _ in halvings(rows, order))


class Stem:
    KERNEL = 7
    COLOURS = 3

    def __init__(self, R, S, images, side, count):
        self.R, self.S, self.images, self.side, self.count = R, S, images, side, count
        self.cells = side // 2
        self.pairs = self.cells // 2
        self.band = side * 8
        self.fine = self.COLOURS * self.band
        self.half_rows = images * self.pairs
        self.depth = S.xx.shape[1]
        self.spread = (self.depth - self.fine) // 3

    def _table(self, q):
        per = self.S.grads.shape[1] // LANES
        return q // per * self.depth, lanes(q % per * LANES)

    def tables(self):
        R, S = self.R, self.S
        table, wt, wd = S.grads, S.wt, S.wd
        tall = 32
        used = self.depth * self.pairs * LANES // table.shape[1]

        def clear(k, carry):
            table[pl.ds(pl.multiple_of(k * tall, tall), tall)] = jnp.zeros((tall, table.shape[1]), BF16)
            return carry

        lax.fori_loop(0, used // tall, clear, 0)
        wt[...] = jnp.zeros(wt.shape, F32)
        wd[...] = jnp.zeros(wd.shape, F32)
        weights = R.stem_w[...].astype(F32)
        for ki in range(self.KERNEL):
            for c in range(self.COLOURS):
                for kj in range(self.KERNEL):
                    at = c * 64 + kj * 8 + ki
                    wt[at : at + 1, 0:64] = weights[ki * self.COLOURS + c, kj : kj + 1]
        for c in range(self.COLOURS):
            for p in range(5):
                block = jnp.zeros((16, LANES), F32)
                if p < 4:
                    block = block + wt[c * 64 + 16 * p : c * 64 + 16 * p + 16, :]
                if p > 0:
                    high = wt[c * 64 + 16 * p - 16 : c * 64 + 16 * p, :]
                    block = block + pltpu.roll(high, 64, 1)
                block = block.astype(BF16)
                for q in range(self.pairs):
                    j = 4 * q - 2 + 2 * p
                    if 0 <= j < self.side:
                        top, at = self._table(q)
                        top = top + c * self.band + j * 8
                        table[top : top + 16, at] = block
        weights = R.diff_w[...].astype(F32)
        for t in range(9):
            wd[t * 16 : t * 16 + weights.shape[1], 0:64] = weights[t]
        for ki in range(3):
            for kj in range(3):
                block = wd[(ki * 3 + kj) * 16 : (ki * 3 + kj) * 16 + 16, :]
                block = (block + pltpu.roll(block, 64, 1)).astype(BF16)
                for q in range(self.pairs):
                    j = q + kj - 1
                    if 0 <= j < self.pairs:
                        top, at = self._table(q)
                        top = top + self.fine + ki * self.spread + j * 16
                        table[top : top + 16, at] = block

    def patches(self):
        S, side, images = self.S, self.side, self.images
        frames, padded, taps, xx = S.frames, S.padded, S.stem_taps, S.xx
        tall = padded.shape[0] // images
        padded[...] = jnp.zeros(padded.shape, F32)
        taps[...] = jnp.zeros(taps.shape, F32)
        row = lax.broadcasted_iota(jnp.int32, (taps.shape[1], self.band), 0)
        lane = lax.broadcasted_iota(jnp.int32, (taps.shape[1], self.band), 1)
        place = jnp.where(row == lax.rem(lane, 8) * 64 + lane // 8, 1.0, 0.0).astype(BF16)
        for c in range(self.COLOURS):
            for img in range(images):
                plane = frames[(img * 5 + 2) * self.COLOURS + c].astype(F32)
                padded[img * tall + 2 : img * tall + 2 + side, 0:side] = plane
            for ki in range(self.KERNEL):
                for parity in range(2):
                    for img in range(images):
                        start = img * tall + 2 * parity + ki
                        piece = padded[pl.ds(start, self.pairs, stride=4), 0:64]
                        top = parity * self.half_rows + img * self.pairs
                        taps[top : top + self.pairs, ki * 64 : ki * 64 + 64] = piece
            xx[:, lanes(c * self.band, self.band)] = dot(taps[...].astype(BF16), place).astype(BF16)
        row = lax.broadcasted_iota(jnp.int32, (side, self.spread), 0)
        lane = lax.broadcasted_iota(jnp.int32, (side, self.spread), 1)
        inside = row // 4 == lane // 16
        channel = lax.rem(lane, 16)
        total = None
        for f in range(5):
            for c in range(self.COLOURS):
                sign = jnp.zeros((side, self.spread), F32)
                if f > 0:
                    sign = sign + jnp.where(channel == (f - 1) * self.COLOURS + c, 1.0, 0.0)
                if f < 4:
                    sign = sign - jnp.where(channel == f * self.COLOURS + c, 1.0, 0.0)
                sign = jnp.where(inside, sign, 0.0).astype(BF16)
                planes = jnp.concatenate(
                    [frames[(img * 5 + f) * self.COLOURS + c] for img in range(images)], axis=0
                )
                part = dot(planes, sign)
                total = part if total is None else total + part
        for h in range(self.spread // LANES):
            S.columns[h] = total[:, h * LANES : (h + 1) * LANES]
        pooled = None
        for k in range(4):
            parts = [
                S.columns[h, pl.ds(k, self.half_rows, stride=4), :] for h in range(self.spread // LANES)
            ]
            part = jnp.concatenate(parts, axis=1)
            pooled = part if pooled is None else pooled + part
        pooled = (pooled * 0.0625).astype(BF16).astype(F32)
        row = lax.rem(lax.broadcasted_iota(jnp.int32, pooled.shape, 0), self.pairs)
        for ki in range(3):
            rolled = pltpu.roll(pooled, (1 - ki) % self.half_rows, 0)
            ok = (row + ki - 1 >= 0) & (row + ki - 1 < self.pairs)
            rolled = jnp.where(ok, rolled, 0.0).astype(BF16)
            at = lanes(self.fine + ki * self.spread, self.spread)
            xx[0 : self.half_rows, at] = rolled
            xx[self.half_rows :, at] = rolled

    def forward(self, sums, at):
        S, per = self.S, self.S.grads.shape[1]
        for n in range(self.pairs * LANES // per):
            S.pre[:, lanes(n * per, per)] = dot(S.xx[...], S.grads[n * self.depth : (n + 1) * self.depth, :])
        s = q = jnp.zeros((8, LANES), F32)
        for k in range(self.pairs):
            v = S.pre[:, lanes(k * LANES)]
            s, q = s + fold(v), q + fold(v * v)
        self._put(sums, at, s, q)

    def _put(self, sums, at, s, q):
        for row, part in enumerate((s, q)):
            part = total_of(part)
            sums.put(row, at, part + pltpu.roll(part, 64, 1))

    def _norm(self):
        S, inv = self.S, 1.0 / self.count
        mean = S.stem_stat[0:1, :] * inv
        root = lax.rsqrt(S.stem_stat[1:2, :] * inv - mean * mean + 1e-05)
        gain, bias = self.R.stem_gain[...], self.R.stem_bias[...]
        scale = root * jnp.concatenate([gain, gain], axis=1)
        return scale, jnp.concatenate([bias, bias], axis=1) - mean * scale, mean, root

    def rear(self, stat, sums, at):
        S = self.S
        S.stem_stat[...] = stat
        scale, shift, mean, root = self._norm()
        step = 2 * self.cells
        S.stem_wide[:, 0:64] = S.stem_cot[...].astype(F32)
        s = q = jnp.zeros((8, LANES), F32)
        for k in range(self.pairs):
            pre = S.pre[:, lanes(k * LANES)]
            cot = []
            for parity in range(2):
                pieces = [
                    S.stem_wide[pl.ds(parity * self.cells + 2 * k + i, self.half_rows, stride=step), 0:64]
                    for i in range(2)
                ]
                cot.append(jnp.concatenate(pieces, axis=1))
            y = pre * scale + shift
            sg = jax.nn.sigmoid(y)
            out = y * sg
            g = jnp.concatenate(cot, axis=0) * (sg + out * (1.0 - sg))
            S.gpre[:, lanes(k * LANES)] = g
            s, q = s + fold(g), q + fold(g * ((pre - mean) * root))
            swapped = pltpu.roll(out, 64, 1)
            for parity in range(2):
                rows = slice(parity * self.half_rows, (parity + 1) * self.half_rows)
                for i, half in enumerate((out, swapped)):
                    where = pl.ds(parity * self.cells + 2 * k + i, self.half_rows, stride=step)
                    S.stem_wide[where, :] = half[rows]
        S.stem_cot[...] = S.stem_wide[:, 0:64].astype(BF16)
        self._put(sums, at, s, q)

    def back(self, stat, top):
        S, inv = self.S, 1.0 / self.count
        scale, _, mean, root = self._norm()
        gb, gg = stat[0:1, :] * inv, stat[1:2, :] * inv
        bands, spots = S.bands, S.spots
        bands[...] = jnp.zeros(bands.shape, F32)
        spots[...] = jnp.zeros(spots.shape, F32)
        for k in range(self.pairs):
            hat = (S.pre[:, lanes(k * LANES)] - mean) * root
            g = (scale * (S.gpre[:, lanes(k * LANES)] - gb - hat * gg)).astype(BF16)
            S.prod[...] = dot_at(S.xx[...], g)
            for c in range(self.COLOURS):
                for p in range(5):
                    j = 4 * k - 2 + 2 * p
                    if 0 <= j < self.side:
                        here = slice((c * 5 + p) * 16, (c * 5 + p) * 16 + 16)
                        start = c * self.band + j * 8
                        bands[here] = bands[here] + S.prod[start : start + 16]
            for ki in range(3):
                for kj in range(3):
                    j = k + kj - 1
                    if 0 <= j < self.pairs:
                        here = slice((ki * 3 + kj) * 16, (ki * 3 + kj) * 16 + 16)
                        start = self.fine + ki * self.spread + j * 16
                        spots[here] = spots[here] + S.prod[start : start + 16]
        low = lax.broadcasted_iota(jnp.int32, (8, LANES), 1) < 64
        for c in range(self.COLOURS):
            for kj in range(self.KERNEL):
                first = bands[c * 80 + kj * 8 : c * 80 + kj * 8 + 8]
                other = bands[c * 80 + kj * 8 + 16 : c * 80 + kj * 8 + 24]
                at = (c * self.KERNEL + kj) * 8
                S.wt[at : at + 8] = jnp.where(low, first + pltpu.roll(other, 64, 1), 0.0)
        grads = S.grads
        grads[top : top + LANES, :] = jnp.zeros((LANES, grads.shape[1]), BF16)
        rest = S.wt.shape[0] - LANES
        used = self.COLOURS * self.KERNEL * 8
        S.wt[used:] = jnp.zeros((S.wt.shape[0] - used, LANES), F32)
        grads[top : top + LANES, lanes(0)] = S.wt[0:LANES].astype(BF16)
        grads[top : top + rest, lanes(LANES)] = S.wt[LANES:].astype(BF16)
        both = spots[...] + pltpu.roll(spots[...], 64, 1)
        grads[top : top + LANES, lanes(2 * LANES)] = both[0:LANES].astype(BF16)
        grads[top : top + 16, lanes(3 * LANES)] = both[LANES:].astype(BF16)


class Layout:
    def __init__(self, wide, mid, red):
        self.excite = 0
        self.scales = self.excite + red * wide // mid
        self.scale_taps = mid // red
        groups = -(-2 * len(TAPS) // self.scale_taps)
        self.squeeze = self.scales + groups * red
        self.expand = self.squeeze + wide * red // mid
        self.spatial = self.expand + wide
        self.reduce = self.spatial + len(TAPS) * mid
        self.stem = self.reduce + wide
        self.rows = self.stem + LANES


def job_list(lay, mid):
    early = lay.expand - lay.excite
    jobs = [[(0, 1024, 0), (1024, early - 1024, 1)]]
    half = (lay.spatial - lay.expand) // 2
    jobs.append([(lay.expand, half, 0), (lay.expand + half, half, 1)])
    spatial, at, kind = [], lay.spatial, 0
    while at < lay.reduce:
        size = min(1024, lay.reduce - at)
        spatial.append((at, size, kind))
        at, kind = at + size, 1 - kind
    jobs.append(spatial)
    half = (lay.stem - lay.reduce) // 2
    jobs.append([(lay.reduce, half, 0), (lay.reduce + half, half, 1), (lay.stem, lay.rows - lay.stem, 0)])
    return jobs


def block_kernel(clips, segs, grid, names, sc_names, *refs):
    R = SimpleNamespace(**dict(zip(names, refs[: len(names)])))
    S = SimpleNamespace(**dict(zip(sc_names, refs[len(names) :])))
    rows, wide = S.x.shape
    mid, red = S.f1.shape[1], S.sq.shape[1]
    cells = grid * grid
    images = rows // cells
    lay = Layout(wide, mid, red)
    blocks = range(0, rows, BLOCK)
    ntap = len(TAPS)
    place = Place(clips, segs)
    local, sends, recvs = Sems(S.local), Sems(S.send), Sems(S.recv)

    wfine = S.wfc.at[pl.ds(0, ntap * red)]
    wcoarse = S.wfc.at[pl.ds(ntap * red, ntap * red)]

    def load(src, dst):
        copy = pltpu.make_async_copy(src, dst, local.take())
        copy.start()
        return copy

    loads = SimpleNamespace(
        x=load(R.x, S.x),
        frames=load(R.frames, S.frames),
        wr=load(R.wr, S.wr),
        ws=load(R.ws, S.ws),
        we=load(R.we, S.we),
        wq=load(R.wq, S.wq),
        wf=load(R.wf, wfine),
        wc=load(R.wc, wcoarse),
        wx=load(R.wx, S.wx),
        cot=load(R.cot, S.cot),
        stem_cot=load(R.stem_cot, S.stem_cot),
    )

    place.greet()

    groups = R.groups
    total_groups = groups.shape[0]

    def side_of(group):
        return 5 + 2 * group - group // 2

    def area(k, acc):
        side = side_of(groups[k])
        return acc + side * side

    count = lax.fori_loop(0, total_groups, area, jnp.int32(0)) * segs
    inv = 1.0 / jnp.full((1, LANES), count.astype(F32), F32)
    cell = lax.broadcasted_iota(jnp.int32, (cells, LANES), 0)
    ci, cj = cell // grid, lax.rem(cell, grid)
    for img in range(images):
        side = side_of(groups[place.clip * images + img])
        S.mask[img * cells : (img + 1) * cells] = jnp.where((ci < side) & (cj < side), 1.0, 0.0).astype(F32)
    half = grid // 2
    small = lax.rem(cell, half * half)
    si, sj = small // half, lax.rem(small, half)
    for t, (di, dj) in enumerate(TAPS):
        ok = (ci + di >= 0) & (ci + di < grid) & (cj + dj >= 0) & (cj + dj < grid)
        S.tap[t] = jnp.where(ok, 1.0, 0.0).astype(F32)
        ok = (si + di >= 0) & (si + di < half) & (sj + dj >= 0) & (sj + dj < half)
        S.tap_small[t] = jnp.where(ok, 1.0, 0.0).astype(F32)
    mask, tap, tap_small = S.mask, S.tap, S.tap_small
    srow = lax.broadcasted_iota(jnp.int32, (images * half * half, rows), 0)
    brow = lax.broadcasted_iota(jnp.int32, (images * half * half, rows), 1)
    parent = (brow // cells) * half * half + (lax.rem(brow, cells) // grid) // 2 * half + lax.rem(brow, grid) // 2
    S.pool[...] = jnp.where(srow == parent, 0.25, 0.0).astype(BF16)
    brow = lax.broadcasted_iota(jnp.int32, (rows, images * half * half), 0)
    srow = lax.broadcasted_iota(jnp.int32, (rows, images * half * half), 1)
    parent = (brow // cells) * half * half + (lax.rem(brow, cells) // grid) // 2 * half + lax.rem(brow, grid) // 2
    S.up[...] = jnp.where(srow == parent, 1.0, 0.0).astype(BF16)
    for ref in (S.tmp, S.z, S.tmp_small):
        ref[:PAD] = jnp.zeros((PAD, ref.shape[1]), F32)
        ref[ref.shape[0] - PAD :] = jnp.zeros((PAD, ref.shape[1]), F32)
    grads = S.grads

    near = [S.near0, S.near1, S.near2, S.near3, S.near4, S.near5]
    far = [S.far0, S.far1, S.far2, S.far3, S.far4, S.far5]
    stats = [S.res0, S.res1, S.res2, S.res3, S.res4, S.res5]

    def sums(k):
        return Sums(place, near[k], far[k], stats[k], sends, recvs)

    all_sums = [sums(k) for k in range(6)]

    def local_moments(src, width, ar, masked):
        def body(at, j):
            s = q = jnp.zeros((8, LANES), F32)
            for r in blocks:
                v = src[r : r + BLOCK, lanes(at)]
                w = v * mask[r : r + BLOCK] if masked else v
                s, q = s + fold(w), q + fold(w * v)
            ar.put(0, at, total_of(s))
            ar.put(1, at, total_of(q))

        columns(width, body)

    gains = [R.gain_one, R.gain_two, R.gain_three]
    biases = [R.bias_one, R.bias_two, R.bias_three]

    def affine(k, at):
        stat = stats[k]
        mean = stat[0:1, lanes(at)] * inv
        spread = stat[1:2, lanes(at)] * inv - mean * mean
        root = lax.rsqrt(spread + 1e-05)
        scale = root * gains[k][0:1, lanes(at)]
        return scale, biases[k][0:1, lanes(at)] - mean * scale, mean, root

    def spread_taps(tmp, masks, per, count, stride, store):
        for t, (di, dj) in enumerate(TAPS):
            off = PAD + di * stride + dj
            for r in range(0, count, BLOCK):
                v = tmp[r + off : r + off + BLOCK, :] * masks[t, r % per : r % per + BLOCK]
                store(t, r, v)

    def gather_taps(z, width, masks, per, r, stride, at):
        acc = None
        for t, (di, dj) in enumerate(TAPS):
            off = PAD + r + di * stride + dj
            v = z[off : off + BLOCK, lanes((ntap - 1 - t) * width + at)] * masks[t, r % per : r % per + BLOCK]
            acc = v if acc is None else acc + v
        return acc

    stem = Stem(R, S, images, S.frames.shape[1], float(S.stem_cot.shape[0] * clips * segs))
    loads.x.wait()
    x = S.x

    def cut(at, j):
        for r in blocks:
            x[r : r + BLOCK, lanes(at)] = (x[r : r + BLOCK, lanes(at)].astype(F32) * mask[r : r + BLOCK]).astype(BF16)

    columns(wide, cut)
    loads.wr.wait()
    S.f1[...] = dot(x[...], S.wr[...])
    local_moments(S.f1, mid, all_sums[0], False)
    all_sums[0].start()
    stem.tables()
    all_sums[0].middle()
    loads.frames.wait()
    stem.patches()
    all_sums[0].finish()

    def hidden_one(at, j):
        scale, shift, _, _ = affine(0, at)
        for r in blocks:
            y = S.f1[r : r + BLOCK, lanes(at)] * scale + shift
            S.tmp[PAD + r : PAD + r + BLOCK, :] = y * jax.nn.sigmoid(y) * mask[r : r + BLOCK]

        def store(t, r, v):
            S.col[r : r + BLOCK, lanes(pl.multiple_of(t * mid + at, LANES))] = v.astype(BF16)

        spread_taps(S.tmp, tap, cells, rows, grid, store)

    columns(mid, hidden_one)
    loads.ws.wait()
    S.f2[...] = dot(S.col[...], S.ws[...])
    local_moments(S.f2, mid, all_sums[1], True)
    all_sums[1].start()
    stem.forward(all_sums[2], wide)
    all_sums[1].middle()
    all_sums[1].finish()

    def hidden_two(at, j):
        scale, shift, _, _ = affine(1, at)
        for r in blocks:
            y = S.f2[r : r + BLOCK, lanes(at)] * scale + shift
            S.h2[r : r + BLOCK, lanes(at)] = (y * jax.nn.sigmoid(y) * mask[r : r + BLOCK]).astype(BF16)

    columns(mid, hidden_two)
    loads.we.wait()
    S.f3[...] = dot(S.h2[...], S.we[...])
    local_moments(S.f3, wide, all_sums[2], False)
    all_sums[2].start()
    all_sums[2].middle()
    all_sums[2].finish()

    def branch_low(at, j):
        scale, shift, _, _ = affine(2, at)
        for r in blocks:
            y = (S.f3[r : r + BLOCK, lanes(at)] * scale + shift) * mask[r : r + BLOCK]
            S.branch[r : r + BLOCK, lanes(at)] = y.astype(BF16)

    columns(wide, branch_low)
    loads.wq.wait()
    S.sq[...] = dot(S.branch[...], S.wq[...]).astype(BF16)

    def swap(mine, slots):
        after, before = lax.rem(place.seg + 1, segs), lax.rem(place.seg + segs - 1, segs)
        copies = [
            remote(mine, slots.at[0], sends, recvs, (place.clip, after)),
            remote(mine, slots.at[1], sends, recvs, (place.clip, before)),
        ]
        return copies

    has_before = jnp.where(jnp.full((1, LANES), place.seg, jnp.int32) > 0, 1.0, 0.0).astype(F32)
    has_after = jnp.where(jnp.full((1, LANES), place.seg, jnp.int32) < segs - 1, 1.0, 0.0).astype(F32)
    copies = swap(S.sq, S.halo)
    for copy in copies:
        copy.wait()

    diffs = S.diffs
    for r in blocks:
        own = S.sq[r : r + BLOCK].astype(F32)
        later = S.halo[1, r : r + BLOCK].astype(F32) * has_after - own
        earlier = S.halo[0, r : r + BLOCK].astype(F32) * has_before - own
        diffs[r : r + BLOCK, lanes(0, red)] = later.astype(BF16)
        diffs[r : r + BLOCK, lanes(red, red)] = earlier.astype(BF16)
        S.tmp[PAD + r : PAD + r + BLOCK, :] = later.astype(BF16).astype(F32) + earlier.astype(BF16).astype(F32)

    def store_fine(t, r, v):
        S.cc[r : r + BLOCK, lanes(t * red, red)] = v.astype(BF16)

    spread_taps(S.tmp, tap, cells, rows, grid, store_fine)
    pooled = dot(S.pool[...], diffs[...]).astype(BF16).astype(F32)
    small_rows = pooled.shape[0]
    S.tmp_small[PAD : PAD + small_rows, :] = pooled[:, :red] + pooled[:, red:]

    def store_small(t, r, v):
        S.small_col[r : r + BLOCK, lanes(t * red, red)] = v.astype(BF16)

    spread_taps(S.tmp_small, tap_small, cells, small_rows, half, store_small)
    S.cc[:, lanes(ntap * red, ntap * red)] = dot(S.up[...], S.small_col[...]).astype(BF16)
    loads.wf.wait()
    loads.wc.wait()
    S.mo[...] = dot(S.cc[...], S.wfc[...]).astype(BF16)
    loads.wx.wait()
    S.gb[...] = dot(S.mo[...], S.wx[...])
    loads.cot.wait()

    def ends(at, j):
        scale, shift, _, _ = affine(2, at)
        for r in blocks:
            here = (slice(r, r + BLOCK), lanes(at))
            m = mask[r : r + BLOCK]
            branch = (S.f3[here] * scale + shift) * m
            gate = jax.nn.sigmoid(S.gb[here])
            z = x[here].astype(F32) + branch * (1.0 + gate)
            s = jax.nn.sigmoid(z)
            out = z * s
            gz = S.cot[here].astype(F32) * m * (s + out * (1.0 - s))
            S.cot[here] = (out * m).astype(BF16)
            S.gi[here] = gz
            S.gb[here] = gz * (1.0 + gate)
            S.g3[here] = (gz * branch * gate * (1.0 - gate)).astype(BF16)

    columns(wide, ends)
    out_copy = pltpu.make_async_copy(S.cot, R.block_out, local.take())
    out_copy.start()

    S.gm[...] = dot_bt(S.g3[...], S.wx[...]).astype(BF16)
    zf = dot_bt(S.gm[...], S.wfc[0 : ntap * red, :])
    S.z[PAD : PAD + rows, lanes(0, ntap * red)] = zf
    gmc = lax.dot_general(S.up[...], S.gm[...], (((0,), (0,)), ((), ())), preferred_element_type=F32).astype(BF16)
    S.z[PAD : PAD + small_rows, lanes(ntap * red, ntap * red)] = dot_bt(gmc, S.wfc[ntap * red :, :])
    S.z[PAD + small_rows : PAD + small_rows + PAD, lanes(ntap * red, ntap * red)] = jnp.zeros((PAD, ntap * red), F32)
    coarse = gather_taps(S.z, red, tap_small, cells, 0, half, ntap * red)
    coarse = dot_at(S.pool[...], coarse.astype(BF16))
    for r in blocks:
        gd = gather_taps(S.z, red, tap, cells, r, grid, 0) + coarse[r : r + BLOCK]
        S.gd[r : r + BLOCK] = gd
        S.gd_low[r : r + BLOCK] = gd.astype(BF16)
    copies = swap(S.gd_low, S.halo2)
    last = lay.squeeze - red
    grads[last : lay.squeeze] = jnp.zeros((red, mid), BF16)
    for b in range(wide // mid):
        grads[lay.excite + b * red : lay.excite + (b + 1) * red] = dot_at(
            S.mo[...], S.g3[:, lanes(b * mid, mid)]
        ).astype(BF16)
    for t in range(2 * ntap):
        top = lay.scales + t // lay.scale_taps * red
        grads[top : top + red, lanes(t % lay.scale_taps * red, red)] = dot_at(
            S.cc[:, lanes(t * red, red)], S.gm[...]
        ).astype(BF16)
    for copy in copies:
        copy.wait()
    for r in blocks:
        g = S.halo2[0, r : r + BLOCK].astype(F32) * has_before + S.halo2[1, r : r + BLOCK].astype(F32) * has_after
        S.gsq[r : r + BLOCK] = (g - 2.0 * S.gd[r : r + BLOCK]).astype(BF16)
    S.z[PAD : PAD + rows, lanes(0, wide)] = dot_bt(S.gsq[...], S.wq[...])

    def branch_grad(at, j):
        _, _, mean, root = affine(2, at)
        s = q = jnp.zeros((8, LANES), F32)
        for r in blocks:
            here = (slice(r, r + BLOCK), lanes(at))
            g = (S.gb[here] + S.z[PAD + r : PAD + r + BLOCK, lanes(at)]) * mask[r : r + BLOCK]
            S.gb[here] = g
            s, q = s + fold(g), q + fold(g * ((S.f3[here] - mean) * root))
        all_sums[3].put(0, at, total_of(s))
        all_sums[3].put(1, at, total_of(q))

    columns(wide, branch_grad)
    all_sums[3].start()
    loads.stem_cot.wait()
    stem.rear(stats[2][:, lanes(wide)], all_sums[4], mid)
    stem_copy = pltpu.make_async_copy(S.stem_cot, R.stem_out, local.take())
    stem_copy.start()
    for b in range(mid // red):
        grads[lay.squeeze : lay.squeeze + mid, lanes(b * red, red)] = dot_at(
            S.branch[:, lanes(b * mid, mid)], S.gsq[...]
        ).astype(BF16)
    all_sums[3].middle()
    all_sums[3].finish()

    def through(k, back, src, given, dst, width):
        stat = stats[back]

        def body(at, j):
            scale, _, mean, root = affine(k, at)
            gb, gg = stat[0:1, lanes(at)] * inv, stat[1:2, lanes(at)] * inv
            for r in blocks:
                here = (slice(r, r + BLOCK), lanes(at))
                hat = (src[here] - mean) * root
                dst[here] = (scale * (given[here] - (gb + hat * gg) * mask[r : r + BLOCK])).astype(BF16)

        columns(width, body)

    def act_back(k, ar, src, value, at):
        scale, shift, mean, root = affine(k, at)
        s = q = jnp.zeros((8, LANES), F32)
        for r in blocks:
            here = (slice(r, r + BLOCK), lanes(at))
            a = src[here]
            y = a * scale + shift
            sg = jax.nn.sigmoid(y)
            g = value(r) * mask[r : r + BLOCK] * (sg * (1.0 + y * (1.0 - sg)))
            S.gy[here] = g
            s, q = s + fold(g), q + fold(g * ((a - mean) * root))
        ar.put(0, at, total_of(s))
        ar.put(1, at, total_of(q))

    through(2, 3, S.f3, S.gb, S.g3, wide)
    S.gh[...] = dot_bt(S.g3[...], S.we[...])

    def back_two(at, j):
        act_back(1, all_sums[4], S.f2, lambda r: S.gh[r : r + BLOCK, lanes(at)], at)

    columns(mid, back_two)
    all_sums[4].start()
    for b in range(wide // mid):
        grads[lay.expand + b * mid : lay.expand + (b + 1) * mid] = dot_at(
            S.h2[...], S.g3[:, lanes(b * mid, mid)]
        ).astype(BF16)
    all_sums[4].middle()
    all_sums[4].finish()
    through(1, 4, S.f2, S.gy, S.g2, mid)
    S.z[PAD : PAD + rows, :] = dot_bt(S.g2[...], S.ws[...])

    def back_one(at, j):
        act_back(
            0,
            all_sums[5],
            S.f1,
            lambda r: gather_taps_at(S.z, mid, tap, cells, r, grid, at),
            at,
        )

    def gather_taps_at(z, width, masks, per, r, stride, at):
        acc = None
        for t, (di, dj) in enumerate(TAPS):
            off = PAD + r + di * stride + dj
            start = pl.multiple_of((ntap - 1 - t) * width + at, LANES)
            v = z[off : off + BLOCK, lanes(start)] * masks[t, r % per : r % per + BLOCK]
            acc = v if acc is None else acc + v
        return acc

    columns(mid, back_one)
    all_sums[5].start()

    def spatial_grad(t, carry):
        start = pl.multiple_of(t * mid, mid)
        grads[pl.ds(pl.multiple_of(lay.spatial + start, LANES), mid)] = dot_at(
            S.col[:, lanes(start, mid)], S.g2[...]
        ).astype(BF16)
        return carry

    lax.fori_loop(0, ntap, spatial_grad, 0)
    all_sums[5].middle()
    stem.back(stats[4][:, lanes(mid)], lay.stem)
    all_sums[5].finish()
    through(0, 5, S.f1, S.gy, S.g1, mid)
    for b in range(wide // mid):
        grads[lay.reduce + b * mid : lay.reduce + (b + 1) * mid] = dot_at(
            x[:, lanes(b * mid, mid)], S.g1[...]
        ).astype(BF16)
    S.z[PAD : PAD + rows, lanes(0, wide)] = dot_bt(S.g1[...], S.wr[...])

    def features_grad(at, j):
        for r in blocks:
            here = (slice(r, r + BLOCK), lanes(at))
            g = (S.gi[here] + S.z[PAD + r : PAD + r + BLOCK, lanes(at)]) * mask[r : r + BLOCK]
            S.g3[here] = g.astype(BF16)

    columns(wide, features_grad)
    feat_copy = pltpu.make_async_copy(S.g3, R.grad_features, local.take())
    feat_copy.start()

    jobs, land = [], 0
    for group in job_list(lay, mid):
        for base, size, kind in group:
            job = Job(
                place, grads, S.landing, R.packed, base, size, bit_order(clips, segs, kind), land, local, sends, recvs
            )
            land = job.land_end
            jobs.append(job)
    for job in jobs:
        job.scatter_start()
    count_steps = len(jobs[0].steps)
    for k in range(count_steps):
        for job in jobs:
            job.scatter_finish()
            if k + 1 < count_steps:
                job.scatter_start()
            else:
                job.own_start()
    for job in jobs:
        job.own_finish()
        job.gather_start()
    for k in range(count_steps):
        for job in jobs:
            job.gather_finish()
            if k + 1 < count_steps:
                job.gather_start()
    small = R.sums
    at = 0
    for k, width in ((5, mid), (4, mid + LANES), (3, wide)):
        small[:, lanes(at, width)] = stats[k][...]
        at += width
    stem_copy.wait()
    out_copy.wait()
    feat_copy.wait()


def block(clips, segs, feats, cot, res_group, deep, stem):
    (w_reduce, gain_one, bias_one, w_spatial, gain_two, bias_two, w_expand, gain_three, bias_three) = deep[:9]
    w_squeeze, w_fine, w_coarse, w_excite = deep[9:]
    images, _, grid, _, wide = feats.shape
    rows = images * grid * grid
    mid, red = w_reduce.shape[1], w_squeeze.shape[1]
    taps = len(TAPS)
    lay = Layout(wide, mid, red)
    small_rows = rows // 4
    frames, stem_cot, stem_weight, diff_weight, stem_gain, stem_bias = stem
    count, side, colours = frames.shape[2], frames.shape[3], frames.shape[5]
    kernel, channels = stem_weight.shape[0], stem_weight.shape[3]
    stem_cells = images * (side // 2) ** 2
    stem_rows = images * side // 2
    stem_lanes = side // 2 * channels
    depth = colours * side * 8 + 3 * 256
    inputs = dict(
        x=feats.reshape(rows, wide),
        cot=cot.reshape(rows, wide),
        groups=res_group,
        wr=w_reduce,
        ws=w_spatial.reshape(taps * mid, mid),
        we=w_expand,
        wq=w_squeeze,
        wf=w_fine.reshape(taps * red, red),
        wc=w_coarse.reshape(taps * red, red),
        wx=w_excite,
        gain_one=gain_one.reshape(1, mid),
        bias_one=bias_one.reshape(1, mid),
        gain_two=gain_two.reshape(1, mid),
        bias_two=bias_two.reshape(1, mid),
        gain_three=gain_three.reshape(1, wide),
        bias_three=bias_three.reshape(1, wide),
        frames=jnp.transpose(frames, (0, 1, 2, 5, 3, 4)).reshape(images * count * colours, side, side),
        stem_cot=stem_cot.reshape(stem_cells, channels),
        stem_w=jnp.transpose(stem_weight, (0, 2, 1, 3)).reshape(kernel * colours, kernel, channels),
        diff_w=diff_weight.reshape(len(TAPS), diff_weight.shape[2], channels),
        stem_gain=stem_gain.reshape(1, channels),
        stem_bias=stem_bias.reshape(1, channels),
    )
    outputs = dict(
        block_out=jax.ShapeDtypeStruct((rows, wide), BF16),
        grad_features=jax.ShapeDtypeStruct((rows, wide), BF16),
        packed=jax.ShapeDtypeStruct((lay.rows, mid), BF16),
        sums=jax.ShapeDtypeStruct((2, 2 * mid + wide + LANES), F32),
        stem_out=jax.ShapeDtypeStruct((stem_cells, channels), BF16),
    )

    def spec(name):
        if name == "groups":
            return pl.BlockSpec(memory_space=pltpu.SMEM)
        if inputs.get(name, frames).size < 1 << 15 or name == "sums":
            return pl.BlockSpec(memory_space=pltpu.VMEM)
        return pl.BlockSpec(memory_space=pl.ANY)

    jobs = [job for group in job_list(lay, mid) for job in group]
    land = sum(landing_rows(size, bit_order(clips, segs, kind)) for _, size, kind in jobs)
    bits = len(bit_order(clips, segs, 0))
    near, far = 2 * segs, clips // 2
    remote_count = len(jobs) * bits * 2 + 6 * (near + far) + 8
    v = pltpu.VMEM
    scratch = dict(
        x=v((rows, wide), BF16),
        cot=v((rows, wide), BF16),
        wr=v((wide, mid), BF16),
        ws=v((taps * mid, mid), BF16),
        we=v((mid, wide), BF16),
        wq=v((wide, red), BF16),
        wfc=v((2 * taps * red, red), BF16),
        wx=v((red, wide), BF16),
        mask=v((rows, LANES), F32),
        tap=v((taps, grid * grid, LANES), F32),
        tap_small=v((taps, grid * grid, LANES), F32),
        pool=v((small_rows, rows), BF16),
        up=v((rows, small_rows), BF16),
        tmp=v((rows + 2 * PAD, LANES), F32),
        tmp_small=v((small_rows + 2 * PAD, LANES), F32),
        small_col=v((small_rows, taps * red), BF16),
        f1=v((rows, mid), F32),
        f2=v((rows, mid), F32),
        f3=v((rows, wide), F32),
        col=v((rows, taps * mid), BF16),
        h2=v((rows, mid), BF16),
        branch=v((rows, wide), BF16),
        sq=v((rows, red), BF16),
        halo=v((2, rows, red), BF16),
        halo2=v((2, rows, red), BF16),
        diffs=v((rows, 2 * red), BF16),
        cc=v((rows, 2 * taps * red), BF16),
        mo=v((rows, red), BF16),
        gm=v((rows, red), BF16),
        gd=v((rows, red), F32),
        gd_low=v((rows, red), BF16),
        gsq=v((rows, red), BF16),
        gb=v((rows, wide), F32),
        gi=v((rows, wide), F32),
        g3=v((rows, wide), BF16),
        gh=v((rows, mid), F32),
        gy=v((rows, mid), F32),
        g2=v((rows, mid), BF16),
        g1=v((rows, mid), BF16),
        z=v((rows + 2 * PAD, taps * mid), F32),
        grads=v((lay.rows, mid), BF16),
        landing=v((land, mid), BF16),
        frames=v((images * count * colours, side, side), BF16),
        stem_cot=v((stem_cells, channels), BF16),
        stem_wide=v((stem_cells, LANES), F32),
        stem_stat=v((2, LANES), F32),
        padded=v((images * (side + 8), LANES), F32),
        stem_taps=v((stem_rows, 512), F32),
        columns=v((2, images * side, LANES), F32),
        xx=v((stem_rows, depth), BF16),
        pre=v((stem_rows, stem_lanes), F32),
        gpre=v((stem_rows, stem_lanes), F32),
        prod=v((depth, LANES), F32),
        bands=v((240, LANES), F32),
        spots=v((144, LANES), F32),
        wt=v((192, LANES), F32),
        wd=v((144, LANES), F32),
    )
    for k, width in enumerate((mid, mid, wide + LANES, wide, mid + LANES, mid)):
        scratch[f"near{k}"] = v((near, 2, width), F32)
        scratch[f"far{k}"] = v((far, 2, width), F32)
        scratch[f"res{k}"] = v((2, width), F32)
    scratch.update(
        local=pltpu.SemaphoreType.DMA((32,)),
        send=pltpu.SemaphoreType.DMA((remote_count,)),
        recv=pltpu.SemaphoreType.DMA((remote_count,)),
    )
    names = list(inputs) + list(outputs)
    result = pl.pallas_call(
        partial(block_kernel, clips, segs, grid, names, list(scratch)),
        out_shape=list(outputs.values()),
        in_specs=[spec(name) for name in inputs],
        out_specs=[spec(name) for name in outputs],
        scratch_shapes=list(scratch.values()),
        compiler_params=pltpu.CompilerParams(
            collective_id=0, has_side_effects=True, vmem_limit_bytes=VMEM_LIMIT
        ),
        name="block",
    )(*inputs.values())
    return result


VMEM_LIMIT = 62 << 20


def spread_kernel(lay, mid, red, wide, packed, reduce, spatial, expand, squeeze, fine, coarse, excite, stem, held, wide_held, reads, writes):
    taps = len(TAPS)
    parts = []
    at = 0
    while at < lay.rows:
        size = min(512, lay.rows - at)
        if at < lay.expand:
            size = {lay.excite: lay.scales - lay.excite, lay.scales: lay.squeeze - lay.scales, lay.squeeze: lay.expand - lay.squeeze}[at]
        parts.append((at, size))
        at += size
    copies = []
    for k, (at, size) in enumerate(parts):
        copy = pltpu.make_async_copy(packed.at[pl.ds(at, size)], held.at[pl.ds(at, size)], reads.at[k])
        copy.start()
        copies.append(copy)
    out, used = [], 0

    def write(src, dst):
        copy = pltpu.make_async_copy(src, dst, writes.at[len(out)])
        copy.start()
        out.append(copy)

    for k, (at, size) in enumerate(parts):
        copies[k].wait()

        def convert(i, carry):
            here = pl.ds(pl.multiple_of(at + i * 32, 32), 32)
            wide_held[here] = held[here].astype(F32)
            return carry

        lax.fori_loop(0, size // 32, convert, 0)
        block = wide_held.at[pl.ds(at, size)]
        if at == lay.excite:
            for b in range(wide // mid):
                write(wide_held.at[pl.ds(at + b * red, red)], excite.at[:, pl.ds(b * mid, mid)])
        elif at == lay.scales:
            for t in range(2 * taps):
                src = wide_held.at[
                    pl.ds(at + t // lay.scale_taps * red, red), pl.ds(t % lay.scale_taps * red, red)
                ]
                dst = fine if t < taps else coarse
                write(src, dst.at[pl.ds(t % taps * red, red)])
        elif at == lay.squeeze:
            for b in range(mid // red):
                write(wide_held.at[pl.ds(at, mid), pl.ds(b * red, red)], squeeze.at[pl.ds(b * mid, mid)])
        elif at == lay.stem:
            write(block, stem)
        elif at < lay.spatial:
            write(block, expand.at[:, pl.ds(at - lay.expand, size)])
        elif at < lay.reduce:
            write(block, spatial.at[pl.ds(at - lay.spatial, size)])
        else:
            write(block, reduce.at[pl.ds(at - lay.reduce, size)])
    for copy in out:
        copy.wait()


def spread(packed, mid, red, wide):
    lay = Layout(wide, mid, red)
    taps = len(TAPS)
    shapes = [(wide, mid), (taps * mid, mid), (mid, wide), (wide, red), (taps * red, red), (taps * red, red), (red, wide), (LANES, mid)]
    return pl.pallas_call(
        partial(spread_kernel, lay, mid, red, wide),
        out_shape=[jax.ShapeDtypeStruct(shape, F32) for shape in shapes],
        in_specs=[pl.BlockSpec(memory_space=pl.ANY)],
        out_specs=[pl.BlockSpec(memory_space=pl.ANY)] * len(shapes),
        scratch_shapes=[
            pltpu.VMEM((lay.rows, mid), BF16),
            pltpu.VMEM((lay.rows, mid), F32),
            pltpu.SemaphoreType.DMA((64,)),
            pltpu.SemaphoreType.DMA((64,)),
        ],
        compiler_params=pltpu.CompilerParams(vmem_limit_bytes=VMEM_LIMIT),
        name="spread",
    )(packed)


def shards(
    frames,
    features,
    res_group,
    stem_weight,
    diff_weight,
    stem_gain,
    stem_bias,
    w_reduce,
    gain_one,
    bias_one,
    w_spatial,
    gain_two,
    bias_two,
    w_expand,
    gain_three,
    bias_three,
    w_squeeze,
    w_fine,
    w_coarse,
    w_excite,
    stem_cotangent,
    block_cotangent,
):
    clips, segs = lax.axis_size("clip"), lax.axis_size("seg")
    wide, mid, red = w_reduce.shape[0], w_reduce.shape[1], w_squeeze.shape[1]
    deep = (
        w_reduce, gain_one, bias_one, w_spatial, gain_two, bias_two, w_expand, gain_three, bias_three,
        w_squeeze, w_fine, w_coarse, w_excite,
    )
    stem = (frames, stem_cotangent, stem_weight, diff_weight, stem_gain, stem_bias)
    block_out, grad_feats, packed, sums, stem_out = block(
        clips, segs, features, block_cotangent, res_group, deep, stem
    )
    g_reduce, g_spatial, g_expand, g_squeeze, g_fine, g_coarse, g_excite, g_stem = spread(packed, mid, red, wide)
    kernel, colours, channels = stem_weight.shape[0], stem_weight.shape[2], stem_weight.shape[3]
    parts = [g_stem[:, k * LANES : k * LANES + channels] for k in range(4)]
    g_stem_w = jnp.concatenate(parts[:2])[: colours * kernel * 8].reshape(colours, kernel, 8, channels)
    g_stem_w = jnp.transpose(g_stem_w[:, :, :kernel], (2, 1, 0, 3))
    g_diff_w = jnp.concatenate([parts[2], parts[3][:16]]).reshape(3, 3, 16, channels)[:, :, : diff_weight.shape[2]]

    def pick(row, at, width):
        return sums[row, at : at + width]

    return (
        stem_out.reshape(stem_cotangent.shape),
        block_out.reshape(features.shape),
        grad_feats.reshape(features.shape),
        g_stem_w,
        g_diff_w,
        pick(1, 2 * mid, channels),
        pick(0, 2 * mid, channels),
        g_reduce,
        pick(1, 0, mid),
        pick(0, 0, mid),
        g_spatial.reshape(w_spatial.shape),
        pick(1, mid, mid),
        pick(0, mid, mid),
        g_expand,
        pick(1, 2 * mid + LANES, wide),
        pick(0, 2 * mid + LANES, wide),
        g_squeeze,
        g_fine.reshape(w_fine.shape),
        g_coarse.reshape(w_coarse.shape),
        g_excite,
    )


def solution(mesh):
    split = P("clip", "seg")
    whole = P()
    ins = (split, split) + (whole,) * 18 + (split, split)
    outs = (split,) * 3 + (whole,) * 17
    return jax.shard_map(shards, mesh=mesh, in_specs=ins, out_specs=outs, check_vma=False)
```

```python
from functools import partial
from types import SimpleNamespace

import jax
import jax.numpy as jnp
from jax import lax
from jax.experimental import pallas as pl
from jax.experimental.pallas import tpu as pltpu
from jax.sharding import PartitionSpec as P

MESH = pl.DeviceIdType.MESH
F32, BF16 = jnp.float32, jnp.bfloat16
LANES = 128
BLOCK = 64
PAD = 16
TAPS = [(di, dj) for di in (-1, 0, 1) for dj in (-1, 0, 1)]


def dot(a, b):
    return lax.dot_general(a, b, (((1,), (0,)), ((), ())), preferred_element_type=F32)


def dot_bt(a, b):
    return lax.dot_general(a, b, (((1,), (1,)), ((), ())), preferred_element_type=F32)


def dot_at(a, b):
    return lax.dot_general(a, b, (((0,), (0,)), ((), ())), preferred_element_type=F32)


def columns(total, body, step=LANES):
    def go(j, carry):
        body(pl.multiple_of(j * step, step), j)
        return carry

    lax.fori_loop(0, total // step, go, 0)


def lanes(start, size=LANES):
    return pl.ds(start, size)


def fold(block):
    return block.reshape(block.shape[0] // 8, 8, LANES).sum(axis=0)


def total_of(part):
    return jnp.sum(part, axis=0, keepdims=True)


class Sems:
    def __init__(self, ref):
        self.ref, self.used = ref, 0

    def take(self):
        self.used += 1
        return self.ref.at[self.used - 1]


class Place:
    def __init__(self, clips, segs):
        self.clips, self.segs = clips, segs
        self.clip, self.seg = lax.axis_index("clip"), lax.axis_index("seg")
        self.near = 2 * segs
        self.far = clips // 2
        self.near_me = lax.rem(self.clip, 2) * segs + self.seg
        self.far_me = self.clip // 2

        self.plane = 8
        self.plane_me = lax.rem(self.clip, 2) * 4 + lax.rem(self.seg, 4)

    def plane_device(self, t):
        return ((self.clip // 2) * 2 + t // 4, (self.seg // 4) * 4 + lax.rem(t, 4))

    def near_device(self, t):
        return ((self.clip // 2) * 2 + t // self.segs, lax.rem(t, self.segs))

    def far_device(self, t):
        return (t * 2 + lax.rem(self.clip, 2), self.seg)

    def bit(self, axis, stride):
        mine = self.seg if axis == "seg" else self.clip
        bit = lax.rem(mine // stride, 2)
        other = mine + stride * (1 - 2 * bit)
        return bit, (self.clip, other) if axis == "seg" else (other, self.seg)

    def greet(self):
        sem = pltpu.get_barrier_semaphore()

        def near(k, carry):
            pl.semaphore_signal(
                sem, inc=1, device_id=self.near_device(lax.rem(self.near_me + k, self.near)), device_id_type=MESH
            )
            return carry

        def far(k, carry):
            pl.semaphore_signal(
                sem, inc=1, device_id=self.far_device(lax.rem(self.far_me + k, self.far)), device_id_type=MESH
            )
            return carry

        lax.fori_loop(1, self.near, near, 0)
        lax.fori_loop(1, self.far, far, 0)

    def greeted(self):
        pl.semaphore_wait(pltpu.get_barrier_semaphore(), self.near + self.far - 2)


def remote(src, dst, sends, recvs, device):
    copy = pltpu.make_async_remote_copy(
        src_ref=src,
        dst_ref=dst,
        send_sem=sends.take(),
        recv_sem=recvs.take(),
        device_id=device,
        device_id_type=MESH,
    )
    copy.start()
    return copy


class Sums:
    def __init__(self, place, near_buf, far_buf, result, sends, recvs):
        self.place, self.near_buf, self.far_buf, self.result = place, near_buf, far_buf, result
        self.sends, self.recvs = sends, recvs

    def put(self, row, at, value):
        self.near_buf[self.place.near_me, row : row + 1, lanes(at, value.shape[1])] = value

    def _send(self, buf, me, count, device):
        mine = buf.at[me]
        return [remote(mine, mine, self.sends, self.recvs, device(lax.rem(me + k, count))) for k in range(1, count)]

    def _add(self, buf, count):
        value = buf[0]
        for k in range(1, count):
            value = value + buf[k]
        return value

    def start(self):
        p = self.place
        self.copies = self._send(self.near_buf, p.near_me, p.near, p.near_device)

    def middle(self):
        p = self.place
        for copy in self.copies:
            copy.wait()
        self.far_buf[p.far_me] = self._add(self.near_buf, p.near)
        self.copies = self._send(self.far_buf, p.far_me, p.far, p.far_device)

    def finish(self):
        for copy in self.copies:
            copy.wait()
        self.result[...] = self._add(self.far_buf, self.place.far)


def bit_order(clips, segs, letters):
    seg = [("seg", 1 << k) for k in range(segs.bit_length() - 1)]
    clip = [("clip", 1 << k) for k in range(clips.bit_length() - 1)]
    others = seg[2:] + clip[1:]
    named = dict(c=seg[:1], x=clip[:1], y=seg[1:2], p=others[:-1], q=others[-1:])
    return [bit for letter in letters for bit in named[letter]]


class Plan:
    def __init__(self, clips, segs, first, rows, letters, nest, skip=""):
        self.first, self.rows = first, rows
        skip = bit_order(clips, segs, skip)
        held = rows >> len(skip)
        self.block, self.sums, split = held, [], list(skip)
        for bit in bit_order(clips, segs, letters):
            if bit in skip:
                continue
            half = held // 2
            halved = held % 2 == 0 and half % 16 == 0
            held = half if halved else held
            self.sums.append((bit, held, halved))
            if halved:
                split.append(bit)
        self.piece = held
        self.places, size = [], rows
        for bit in bit_order(clips, segs, nest):
            if bit in split:
                size //= 2
                self.places.append((bit, size))
        self.landing_rows = sum(size for _, size, _ in self.sums)
        self.transfers = len(self.sums) + len(self.places)

    def pieces(self):
        bits = [bit for bit, _ in self.places]

        def bits_of(number):
            return {bit: lax.rem(lax.shift_right_logical(number, k), 2) for k, bit in enumerate(bits)}

        return 1 << len(bits), bits_of

    def packed_at(self, values):
        return sum((values[bit] * size for bit, size in self.places), self.first)

    def summed_at(self, values):
        return sum((values[bit] * size for bit, size, halved in self.sums if halved), 0)


class Job:
    def __init__(self, place, plan, buffers, held, land, sems):
        self.grads, self.landing, self.packed = buffers
        self.local, self.sends, self.recvs = sems
        self.sums, self.places = [], []
        for (axis, stride), size, halved in plan.sums:
            bit, device = place.bit(axis, stride)
            away = held
            if halved:
                away = held + (1 - bit) * size
                held = held + bit * size
            self.sums.append((held, away, size, device, land))
            land += size
        self.held, self.piece, self.land_end = held, plan.piece, land
        first = plan.first
        for (axis, stride), size in plan.places:
            bit, device = place.bit(axis, stride)
            first = first + bit * size
            self.places.append((first, size, device))
        self.first = first
        self.at = self.phase = 0

    def _rows(self, ref, start, size):
        if not isinstance(start, int):
            start = pl.multiple_of(start, 16)
        return ref.at[pl.ds(start, size)]

    def scatter_start(self):
        held, away, size, device, land = self.sums[self.at]
        self.copy = remote(
            self._rows(self.grads, away, size), self._rows(self.landing, land, size), self.sends, self.recvs, device
        )

    def scatter_finish(self):
        held, away, size, device, land = self.sums[self.at]
        self.copy.wait()
        block = 32 if size % 32 == 0 else 16

        def add(k, carry):
            mine = pl.ds(pl.multiple_of(held + k * block, 16), block)
            theirs = pl.ds(pl.multiple_of(land + k * block, 16), block)
            self.grads[mine] = self.grads[mine] + self.landing[theirs]
            return carry

        lax.fori_loop(0, size // block, add, 0)
        self.at += 1

    def own_start(self):
        self.copy = pltpu.make_async_copy(
            self._rows(self.grads, self.held, self.piece),
            self._rows(self.packed, self.first, self.piece),
            self.local.take(),
        )
        self.copy.start()
        self.at = len(self.places)

    def gather_start(self):
        first, size, device = self.places[self.at - 1]
        mine = self._rows(self.packed, first, size)
        self.copy = remote(mine, mine, self.sends, self.recvs, device)

    def gather_finish(self):
        self.at -= 1
        self.copy.wait()

    def step(self):
        if self.phase == 0:
            self.scatter_start()
            self.phase = 1
        elif self.phase == 1:
            self.scatter_finish()
            if self.at < len(self.sums):
                self.scatter_start()
            else:
                self.own_start()
                self.phase = 2
        elif self.phase == 2:
            self.copy.wait()
            self.gather_start()
            self.phase = 3
        elif self.phase == 3:
            self.gather_finish()
            if self.at > 0:
                self.gather_start()
            else:
                self.phase = 4
        return self.phase


class Stem:
    KERNEL = 7
    COLOURS = 3

    def __init__(self, R, S, images, side, count):
        self.R, self.S, self.images, self.side, self.count = R, S, images, side, count
        self.cells = side // 2
        self.pairs = self.cells // 2
        self.band = side * 8
        self.fine = self.COLOURS * self.band
        self.half_rows = images * self.pairs
        self.depth = S.xx.shape[1]
        self.spread = (self.depth - self.fine) // 3

    def _table(self, q):
        per = self.S.grads.shape[1] // LANES
        table, top = self._part(q // per)
        return table, top, lanes(q % per * LANES)

    def _part(self, n):
        return (self.S.grads, n * self.depth) if n < 2 else (self.S.landing, 0)

    def tables(self):
        R, S = self.R, self.S
        wt, wd = S.wt, S.wd
        tall = 32

        def clear(k, carry):
            for n in range(3):
                table, top = self._part(n)
                table[pl.ds(pl.multiple_of(top + k * tall, tall), tall)] = jnp.zeros((tall, table.shape[1]), BF16)
            return carry

        lax.fori_loop(0, self.depth // tall, clear, 0)
        wt[...] = jnp.zeros(wt.shape, F32)
        wd[...] = jnp.zeros(wd.shape, F32)
        weights = R.stem_w[...].astype(F32)
        for ki in range(self.KERNEL):
            for c in range(self.COLOURS):
                for kj in range(self.KERNEL):
                    at = c * 64 + kj * 8 + ki
                    wt[at : at + 1, 0:64] = weights[ki * self.COLOURS + c, kj : kj + 1]
        for c in range(self.COLOURS):
            for p in range(5):
                block = jnp.zeros((16, LANES), F32)
                if p < 4:
                    block = block + wt[c * 64 + 16 * p : c * 64 + 16 * p + 16, :]
                if p > 0:
                    high = wt[c * 64 + 16 * p - 16 : c * 64 + 16 * p, :]
                    block = block + pltpu.roll(high, 64, 1)
                block = block.astype(BF16)
                for q in range(self.pairs):
                    j = 4 * q - 2 + 2 * p
                    if 0 <= j < self.side:
                        table, top, at = self._table(q)
                        top = top + c * self.band + j * 8
                        table[top : top + 16, at] = block
        weights = R.diff_w[...].astype(F32)
        for t in range(9):
            wd[t * 16 : t * 16 + weights.shape[1], 0:64] = weights[t]
        for ki in range(3):
            for kj in range(3):
                block = wd[(ki * 3 + kj) * 16 : (ki * 3 + kj) * 16 + 16, :]
                block = (block + pltpu.roll(block, 64, 1)).astype(BF16)
                for q in range(self.pairs):
                    j = q + kj - 1
                    if 0 <= j < self.pairs:
                        table, top, at = self._table(q)
                        top = top + self.fine + ki * self.spread + j * 16
                        table[top : top + 16, at] = block

    def patches(self):
        S, side, images = self.S, self.side, self.images
        frames, padded, taps, xx = S.frames, S.padded, S.stem_taps, S.xx
        tall = padded.shape[0] // images
        padded[...] = jnp.zeros(padded.shape, F32)
        taps[...] = jnp.zeros(taps.shape, F32)
        row = lax.broadcasted_iota(jnp.int32, (taps.shape[1], self.band), 0)
        lane = lax.broadcasted_iota(jnp.int32, (taps.shape[1], self.band), 1)
        place = jnp.where(row == lax.rem(lane, 8) * 64 + lane // 8, 1.0, 0.0).astype(BF16)
        for c in range(self.COLOURS):
            for img in range(images):
                plane = frames[(img * 5 + 2) * self.COLOURS + c].astype(F32)
                padded[img * tall + 2 : img * tall + 2 + side, 0:side] = plane
            for ki in range(self.KERNEL):
                for parity in range(2):
                    for img in range(images):
                        start = img * tall + 2 * parity + ki
                        piece = padded[pl.ds(start, self.pairs, stride=4), 0:64]
                        top = parity * self.half_rows + img * self.pairs
                        taps[top : top + self.pairs, ki * 64 : ki * 64 + 64] = piece
            xx[:, lanes(c * self.band, self.band)] = dot(taps[...].astype(BF16), place).astype(BF16)
        row = lax.broadcasted_iota(jnp.int32, (side, self.spread), 0)
        lane = lax.broadcasted_iota(jnp.int32, (side, self.spread), 1)
        inside = row // 4 == lane // 16
        channel = lax.rem(lane, 16)
        total = None
        for f in range(5):
            for c in range(self.COLOURS):
                sign = jnp.zeros((side, self.spread), F32)
                if f > 0:
                    sign = sign + jnp.where(channel == (f - 1) * self.COLOURS + c, 1.0, 0.0)
                if f < 4:
                    sign = sign - jnp.where(channel == f * self.COLOURS + c, 1.0, 0.0)
                sign = jnp.where(inside, sign, 0.0).astype(BF16)
                planes = jnp.concatenate(
                    [frames[(img * 5 + f) * self.COLOURS + c] for img in range(images)], axis=0
                )
                part = dot(planes, sign)
                total = part if total is None else total + part
        for h in range(self.spread // LANES):
            S.columns[h] = total[:, h * LANES : (h + 1) * LANES]
        pooled = None
        for k in range(4):
            parts = [
                S.columns[h, pl.ds(k, self.half_rows, stride=4), :] for h in range(self.spread // LANES)
            ]
            part = jnp.concatenate(parts, axis=1)
            pooled = part if pooled is None else pooled + part
        pooled = (pooled * 0.0625).astype(BF16).astype(F32)
        row = lax.rem(lax.broadcasted_iota(jnp.int32, pooled.shape, 0), self.pairs)
        for ki in range(3):
            rolled = pltpu.roll(pooled, (1 - ki) % self.half_rows, 0)
            ok = (row + ki - 1 >= 0) & (row + ki - 1 < self.pairs)
            rolled = jnp.where(ok, rolled, 0.0).astype(BF16)
            at = lanes(self.fine + ki * self.spread, self.spread)
            xx[0 : self.half_rows, at] = rolled
            xx[self.half_rows :, at] = rolled

    def forward(self, sums, at):
        S, per = self.S, self.S.grads.shape[1]
        for n in range(self.pairs * LANES // per):
            table, top = self._part(n)
            S.pre[:, lanes(n * per, per)] = dot(S.xx[...], table[top : top + self.depth, :])
        s = q = jnp.zeros((8, LANES), F32)
        for k in range(self.pairs):
            v = S.pre[:, lanes(k * LANES)]
            s, q = s + fold(v), q + fold(v * v)
        self._put(sums, at, s, q)

    def _put(self, sums, at, s, q):
        for row, part in enumerate((s, q)):
            part = total_of(part)
            sums.put(row, at, part + pltpu.roll(part, 64, 1))

    def _norm(self):
        S, inv = self.S, 1.0 / self.count
        mean = S.stem_stat[0:1, :] * inv
        root = lax.rsqrt(S.stem_stat[1:2, :] * inv - mean * mean + 1e-05)
        gain, bias = self.R.stem_gain[...], self.R.stem_bias[...]
        scale = root * jnp.concatenate([gain, gain], axis=1)
        return scale, jnp.concatenate([bias, bias], axis=1) - mean * scale, mean, root

    def rear(self, stat, sums, at):
        S = self.S
        S.stem_stat[...] = stat
        scale, shift, mean, root = self._norm()
        step = 2 * self.cells
        S.stem_wide[:, 0:64] = S.stem_cot[...].astype(F32)
        s = q = jnp.zeros((8, LANES), F32)
        for k in range(self.pairs):
            pre = S.pre[:, lanes(k * LANES)]
            cot = []
            for parity in range(2):
                pieces = [
                    S.stem_wide[pl.ds(parity * self.cells + 2 * k + i, self.half_rows, stride=step), 0:64]
                    for i in range(2)
                ]
                cot.append(jnp.concatenate(pieces, axis=1))
            y = pre * scale + shift
            sg = jax.nn.sigmoid(y)
            out = y * sg
            g = jnp.concatenate(cot, axis=0) * (sg + out * (1.0 - sg))
            S.gpre[:, lanes(k * LANES)] = g
            s, q = s + fold(g), q + fold(g * ((pre - mean) * root))
            swapped = pltpu.roll(out, 64, 1)
            for parity in range(2):
                rows = slice(parity * self.half_rows, (parity + 1) * self.half_rows)
                for i, half in enumerate((out, swapped)):
                    where = pl.ds(parity * self.cells + 2 * k + i, self.half_rows, stride=step)
                    S.stem_wide[where, :] = half[rows]
        S.stem_cot[...] = S.stem_wide[:, 0:64].astype(BF16)
        self._put(sums, at, s, q)

    def back(self, stat, top):
        S, inv = self.S, 1.0 / self.count
        scale, _, mean, root = self._norm()
        gb, gg = stat[0:1, :] * inv, stat[1:2, :] * inv
        bands, spots = S.bands, S.spots
        bands[...] = jnp.zeros(bands.shape, F32)
        spots[...] = jnp.zeros(spots.shape, F32)
        for k in range(self.pairs):
            hat = (S.pre[:, lanes(k * LANES)] - mean) * root
            g = (scale * (S.gpre[:, lanes(k * LANES)] - gb - hat * gg)).astype(BF16)
            S.prod[...] = dot_at(S.xx[...], g)
            for c in range(self.COLOURS):
                for p in range(5):
                    j = 4 * k - 2 + 2 * p
                    if 0 <= j < self.side:
                        here = slice((c * 5 + p) * 16, (c * 5 + p) * 16 + 16)
                        start = c * self.band + j * 8
                        bands[here] = bands[here] + S.prod[start : start + 16]
            for ki in range(3):
                for kj in range(3):
                    j = k + kj - 1
                    if 0 <= j < self.pairs:
                        here = slice((ki * 3 + kj) * 16, (ki * 3 + kj) * 16 + 16)
                        start = self.fine + ki * self.spread + j * 16
                        spots[here] = spots[here] + S.prod[start : start + 16]
        low = lax.broadcasted_iota(jnp.int32, (8, LANES), 1) < 64
        for c in range(self.COLOURS):
            for kj in range(self.KERNEL):
                first = bands[c * 80 + kj * 8 : c * 80 + kj * 8 + 8]
                other = bands[c * 80 + kj * 8 + 16 : c * 80 + kj * 8 + 24]
                at = (c * self.KERNEL + kj) * 8
                S.wt[at : at + 8] = jnp.where(low, first + pltpu.roll(other, 64, 1), 0.0)
        grads = S.grads
        grads[top : top + LANES, :] = jnp.zeros((LANES, grads.shape[1]), BF16)
        rest = S.wt.shape[0] - LANES
        used = self.COLOURS * self.KERNEL * 8
        S.wt[used:] = jnp.zeros((S.wt.shape[0] - used, LANES), F32)
        grads[top : top + LANES, lanes(0)] = S.wt[0:LANES].astype(BF16)
        grads[top : top + rest, lanes(LANES)] = S.wt[LANES:].astype(BF16)
        both = spots[...] + pltpu.roll(spots[...], 64, 1)
        grads[top : top + LANES, lanes(2 * LANES)] = both[0:LANES].astype(BF16)
        grads[top : top + 16, lanes(3 * LANES)] = both[LANES:].astype(BF16)


class Layout:
    def __init__(self, wide, mid, red):
        taps = len(TAPS)
        self.excite = 0
        self.scales = self.excite + red * wide // mid
        self.scale_taps = mid // red
        groups = -(-2 * taps // self.scale_taps)
        self.squeeze = self.scales + groups * red
        self.stem = self.squeeze + wide * red // mid
        self.expand = self.stem + LANES
        self.reduce = self.expand + wide
        self.rows = self.reduce + wide
        self.spatial_in = mid // 2
        self.spatial_block = taps * self.spatial_in
        self.share_rows = 8 * self.spatial_block

    def plans(self, clips, segs):
        quarter = (self.reduce - self.expand) // 4
        half = (self.rows - self.reduce) // 2

        def plan(first, end, letters, nest):
            return Plan(clips, segs, first, end - first, letters, nest)

        cut = self.expand // 512 * 512
        bounds = [0, cut - 512, cut, self.expand]
        early = [plan(bounds[k], bounds[k + 1], *orders) for k, orders in enumerate(EARLY)]
        middle = [
            plan(self.expand + k * quarter, self.expand + (k + 1) * quarter, *orders)
            for k, orders in enumerate(MIDDLE)
        ]
        late = [plan(self.reduce, self.reduce + half, *LATE[0]), plan(self.reduce + half, self.rows, *LATE[1])]
        return early, middle, late

    def shared_plans(self, clips, segs):
        parts, first = [], 0
        for k, nest in enumerate(SPATIAL):
            count = min(2, len(TAPS) - 2 * k)
            rows = 8 * count * self.spatial_in
            parts.append((2 * k, count, Plan(clips, segs, first, rows, "cxypq", nest, "cxy")))
            first += rows
        return parts


EARLY = (("cxypq", "cxypq"), ("cpyxq", "cyxpq"), ("cyxpq", "cpxqy"))
MIDDLE = (("cpxqy", "cpyxq"), ("cpxyq", "cpxqy"), ("cpqyx", "cxypq"), ("cxypq", "cxpyq"))
SPATIAL = ("cxypq", "cypqx", "cyxpq", "cpxqy", "cpqyx")
LATE = (("cyxpq", "cyxpq"), ("cyxpq", "cxpqy"))
SLOTS = (
    (0, 1),
    (0, 1),
    (),
    (),
    (3, 4, 5, 6, 1),
    (3, 4, 5, 6, 0, 1, 2),
    (),
    (),
    (3, 2),
    (4, 6, 0, 1),
    (5,),
    (12, 13, 0),
    (7, 3, 1, 2),
    (12, 13, 8, 4, 5, 6, 0, 1, 2),
    (7, 9, 3, 0),
    (8, 10, 6, 1, 2),
    (7, 9, 11),
    (12, 7, 0),
    (8, 10, 6, 1),
    (8, 2, 6, 13, 11, 4, 12, 9, 2, 3, 7, 0, 1, 9, 3, 5, 8, 10, 2, 6, 10, 12, 11, 13, 4, 5, 7, 2, 0, 4, 5, 11, 9, 3, 1, 6, 13, 10, 8, 1, 2, 12, 5, 7, 9, 12, 4, 0, 2, 11, 6, 3, 13, 0, 11, 13, 3, 10, 8, 5, 13, 7, 12, 4, 9, 7, 3, 11, 6, 8, 3, 12, 5, 13, 10, 6, 8, 4, 11, 12, 11, 13, 9, 5, 9, 5, 10, 12, 13, 4, 10, 12, 13, 4),
)


def block_kernel(clips, segs, grid, names, sc_names, *refs):
    R = SimpleNamespace(**dict(zip(names, refs[: len(names)])))
    S = SimpleNamespace(**dict(zip(sc_names, refs[len(names) :])))
    rows, wide = S.x.shape
    mid, red = S.f1.shape[1], S.sq.shape[1]
    cells = grid * grid
    images = rows // cells
    lay = Layout(wide, mid, red)
    blocks = range(0, rows, BLOCK)
    ntap = len(TAPS)
    place = Place(clips, segs)
    local, sends, recvs = Sems(S.local), Sems(S.send), Sems(S.recv)

    wfine = S.wfc.at[pl.ds(0, ntap * red)]
    wcoarse = S.wfc.at[pl.ds(ntap * red, ntap * red)]

    def load(src, dst):
        copy = pltpu.make_async_copy(src, dst, local.take())
        copy.start()
        return copy

    loads = SimpleNamespace(
        x=load(R.x, S.x),
        frames=load(R.frames, S.frames),
        wr=load(R.wr, S.wr),
        ws=load(R.ws, S.ws),
        we=load(R.we, S.we),
        wq=load(R.wq, S.wq),
        wf=load(R.wf, wfine),
        wc=load(R.wc, wcoarse),
        wx=load(R.wx, S.wx),
        cot=load(R.cot, S.cot),
        stem_cot=load(R.stem_cot, S.stem_cot),
    )

    place.greet()

    groups = R.groups
    total_groups = groups.shape[0]

    def side_of(group):
        return 5 + 2 * group - group // 2

    def area(k, acc):
        side = side_of(groups[k])
        return acc + side * side

    count = lax.fori_loop(0, total_groups, area, jnp.int32(0)) * segs
    inv = 1.0 / jnp.full((1, LANES), count.astype(F32), F32)
    cell = lax.broadcasted_iota(jnp.int32, (cells, LANES), 0)
    ci, cj = cell // grid, lax.rem(cell, grid)
    for img in range(images):
        side = side_of(groups[place.clip * images + img])
        S.mask[img * cells : (img + 1) * cells] = jnp.where((ci < side) & (cj < side), 1.0, 0.0).astype(F32)
    half = grid // 2
    small = lax.rem(cell, half * half)
    si, sj = small // half, lax.rem(small, half)
    for t, (di, dj) in enumerate(TAPS):
        ok = (ci + di >= 0) & (ci + di < grid) & (cj + dj >= 0) & (cj + dj < grid)
        S.tap[t] = jnp.where(ok, 1.0, 0.0).astype(F32)
        ok = (si + di >= 0) & (si + di < half) & (sj + dj >= 0) & (sj + dj < half)
        S.tap_small[t] = jnp.where(ok, 1.0, 0.0).astype(F32)
    mask, tap, tap_small = S.mask, S.tap, S.tap_small
    srow = lax.broadcasted_iota(jnp.int32, (images * half * half, rows), 0)
    brow = lax.broadcasted_iota(jnp.int32, (images * half * half, rows), 1)
    parent = (brow // cells) * half * half + (lax.rem(brow, cells) // grid) // 2 * half + lax.rem(brow, grid) // 2
    S.pool[...] = jnp.where(srow == parent, 0.25, 0.0).astype(BF16)
    brow = lax.broadcasted_iota(jnp.int32, (rows, images * half * half), 0)
    srow = lax.broadcasted_iota(jnp.int32, (rows, images * half * half), 1)
    parent = (brow // cells) * half * half + (lax.rem(brow, cells) // grid) // 2 * half + lax.rem(brow, grid) // 2
    S.up[...] = jnp.where(srow == parent, 1.0, 0.0).astype(BF16)
    for ref in (S.tmp, S.z, S.tmp_small, S.h1_all):
        ref[:PAD] = jnp.zeros((PAD, ref.shape[1]), F32)
        ref[ref.shape[0] - PAD :] = jnp.zeros((PAD, ref.shape[1]), F32)
    grads = S.grads

    near = [S.near0, S.near1, S.near2, S.near3, S.near4, S.near5]
    far = [S.far0, S.far1, S.far2, S.far3, S.far4, S.far5]
    stats = [S.res0, S.res1, S.res2, S.res3, S.res4, S.res5]

    def sums(k):
        return Sums(place, near[k], far[k], stats[k], sends, recvs)

    all_sums = [sums(k) for k in range(6)]

    def local_moments(src, width, ar, masked):
        def body(at, j):
            s = q = jnp.zeros((8, LANES), F32)
            for r in blocks:
                v = src[r : r + BLOCK, lanes(at)]
                w = v * mask[r : r + BLOCK] if masked else v
                s, q = s + fold(w), q + fold(w * v)
            ar.put(0, at, total_of(s))
            ar.put(1, at, total_of(q))

        columns(width, body)

    gains = [R.gain_one, R.gain_two, R.gain_three]
    biases = [R.bias_one, R.bias_two, R.bias_three]

    def affine(k, at):
        stat = stats[k]
        mean = stat[0:1, lanes(at)] * inv
        spread = stat[1:2, lanes(at)] * inv - mean * mean
        root = lax.rsqrt(spread + 1e-05)
        scale = root * gains[k][0:1, lanes(at)]
        return scale, biases[k][0:1, lanes(at)] - mean * scale, mean, root

    def spread_taps(tmp, masks, per, count, stride, store):
        for t, (di, dj) in enumerate(TAPS):
            off = PAD + di * stride + dj
            for r in range(0, count, BLOCK):
                v = tmp[r + off : r + off + BLOCK, :] * masks[t, r % per : r % per + BLOCK]
                store(t, r, v)

    def gather_taps(z, width, masks, per, r, stride, at):
        acc = None
        for t, (di, dj) in enumerate(TAPS):
            off = PAD + r + di * stride + dj
            v = z[off : off + BLOCK, lanes((ntap - 1 - t) * width + at)] * masks[t, r % per : r % per + BLOCK]
            acc = v if acc is None else acc + v
        return acc

    stem = Stem(R, S, images, S.frames.shape[1], float(S.stem_cot.shape[0] * clips * segs))
    sems = (local, sends, recvs)
    jobs, land = [], 0
    for plan in [plan for group in lay.plans(clips, segs) for plan in group]:
        job = Job(place, plan, (grads, S.landing, R.packed), plan.first, land, sems)
        land = job.land_end
        jobs.append(job)
    shared, land, held = [], 0, 0
    for _, _, plan in lay.shared_plans(clips, segs):
        job = Job(place, plan, (S.shares, S.share_landing, R.shared), held, land, sems)
        land, held = job.land_end, held + plan.block
        shared.append(job)
    jobs = jobs[:7] + shared + jobs[7:]
    slots = iter(SLOTS)

    def advance():
        for k in next(slots):
            jobs[k].step()

    def plane_send(view, slots):
        me, copies = place.plane_me, []
        for k in range(1, place.plane):
            t = lax.rem(me + k, place.plane)
            copies.append(remote(view(t), slots.at[me], sends, recvs, place.plane_device(t)))
        own = pltpu.make_async_copy(view(me), slots.at[me], local.take())
        own.start()
        return copies + [own]

    loads.x.wait()
    x = S.x

    def cut(at, j):
        for r in blocks:
            x[r : r + BLOCK, lanes(at)] = (x[r : r + BLOCK, lanes(at)].astype(F32) * mask[r : r + BLOCK]).astype(BF16)

    columns(wide, cut)

    loads.wr.wait()
    S.f1[...] = dot(x[...], S.wr[...])
    local_moments(S.f1, mid, all_sums[0], False)
    place.greeted()
    all_sums[0].start()
    stem.tables()
    all_sums[0].middle()
    loads.frames.wait()
    stem.patches()
    all_sums[0].finish()

    def hidden_one(at, j):
        scale, shift, _, _ = affine(0, at)
        for r in blocks:
            y = S.f1[r : r + BLOCK, lanes(at)] * scale + shift
            S.tmp[PAD + r : PAD + r + BLOCK, :] = y * jax.nn.sigmoid(y) * mask[r : r + BLOCK]

        def store(t, r, v):
            S.col[r : r + BLOCK, lanes(pl.multiple_of(t * mid + at, LANES))] = v.astype(BF16)

        spread_taps(S.tmp, tap, cells, rows, grid, store)

    columns(mid, hidden_one)
    me, centre = place.plane_me, ntap // 2 * mid
    sibling = me + 1 - 2 * lax.rem(me, 2)

    def half_inputs(t):
        start = pl.multiple_of(centre + t // 4 * lay.spatial_in, lay.spatial_in)
        return S.col.at[:, pl.ds(start, lay.spatial_in)]

    def same_core(k):
        return lax.rem(me // 2 + k, 4) * 2 + lax.rem(me, 2)

    def h1_send():
        copies = [
            remote(half_inputs(same_core(k)), S.h1_in.at[me], sends, recvs, place.plane_device(same_core(k)))
            for k in range(1, 4)
        ]
        own = pltpu.make_async_copy(half_inputs(me), S.h1_in.at[me], local.take())
        own.start()
        return copies, [remote(half_inputs(me), S.h1_in.at[me], sends, recvs, place.plane_device(sibling)), own]

    def h1_relay(copies):
        more = []
        for copy in copies:
            copy.wait()
        for k in range(1, 4):
            block = S.h1_in.at[same_core(k)]
            more.append(remote(block, block, sends, recvs, place.plane_device(sibling)))
        return more
    loads.ws.wait()
    S.f2[...] = dot(S.col[...], S.ws[...])
    local_moments(S.f2, mid, all_sums[1], True)
    all_sums[1].start()
    stem.forward(all_sums[2], wide)
    all_sums[1].middle()
    h1_far, h1_copies = h1_send()
    all_sums[1].finish()

    def hidden_two(at, j):
        scale, shift, _, _ = affine(1, at)
        for r in blocks:
            y = S.f2[r : r + BLOCK, lanes(at)] * scale + shift
            S.h2[r : r + BLOCK, lanes(at)] = (y * jax.nn.sigmoid(y) * mask[r : r + BLOCK]).astype(BF16)

    columns(mid, hidden_two)
    loads.we.wait()
    S.f3[...] = dot(S.h2[...], S.we[...])
    local_moments(S.f3, wide, all_sums[2], False)
    all_sums[2].start()
    all_sums[2].middle()
    h1_copies = h1_copies + h1_relay(h1_far)
    all_sums[2].finish()

    def branch_low(at, j):
        scale, shift, _, _ = affine(2, at)
        for r in blocks:
            y = (S.f3[r : r + BLOCK, lanes(at)] * scale + shift) * mask[r : r + BLOCK]
            S.branch[r : r + BLOCK, lanes(at)] = y.astype(BF16)

    columns(wide, branch_low)
    loads.wq.wait()
    S.sq[...] = dot(S.branch[...], S.wq[...]).astype(BF16)

    def swap(mine, slots):
        after, before = lax.rem(place.seg + 1, segs), lax.rem(place.seg + segs - 1, segs)
        copies = [
            remote(mine, slots.at[0], sends, recvs, (place.clip, after)),
            remote(mine, slots.at[1], sends, recvs, (place.clip, before)),
        ]
        return copies

    has_before = jnp.where(jnp.full((1, LANES), place.seg, jnp.int32) > 0, 1.0, 0.0).astype(F32)
    has_after = jnp.where(jnp.full((1, LANES), place.seg, jnp.int32) < segs - 1, 1.0, 0.0).astype(F32)
    copies = swap(S.sq, S.halo)
    loads.stem_cot.wait()
    stem.rear(stats[2][:, lanes(wide)], all_sums[3], wide)
    stem_copy = pltpu.make_async_copy(S.stem_cot, R.stem_out, local.take())
    stem_copy.start()
    for copy in copies:
        copy.wait()

    diffs = S.diffs
    for r in blocks:
        own = S.sq[r : r + BLOCK].astype(F32)
        later = S.halo[1, r : r + BLOCK].astype(F32) * has_after - own
        earlier = S.halo[0, r : r + BLOCK].astype(F32) * has_before - own
        diffs[r : r + BLOCK, lanes(0, red)] = later.astype(BF16)
        diffs[r : r + BLOCK, lanes(red, red)] = earlier.astype(BF16)
        S.tmp[PAD + r : PAD + r + BLOCK, :] = later.astype(BF16).astype(F32) + earlier.astype(BF16).astype(F32)

    def store_fine(t, r, v):
        S.cc[r : r + BLOCK, lanes(t * red, red)] = v.astype(BF16)

    spread_taps(S.tmp, tap, cells, rows, grid, store_fine)
    pooled = dot(S.pool[...], diffs[...]).astype(BF16).astype(F32)
    small_rows = pooled.shape[0]
    S.tmp_small[PAD : PAD + small_rows, :] = pooled[:, :red] + pooled[:, red:]

    def store_small(t, r, v):
        S.small_col[r : r + BLOCK, lanes(t * red, red)] = v.astype(BF16)

    spread_taps(S.tmp_small, tap_small, cells, small_rows, half, store_small)
    S.cc[:, lanes(ntap * red, ntap * red)] = dot(S.up[...], S.small_col[...]).astype(BF16)
    loads.wf.wait()
    loads.wc.wait()
    S.mo[...] = dot(S.cc[...], S.wfc[...]).astype(BF16)
    loads.wx.wait()
    S.gb[...] = dot(S.mo[...], S.wx[...])
    loads.cot.wait()

    def ends(at, j):
        scale, shift, _, _ = affine(2, at)
        for r in blocks:
            here = (slice(r, r + BLOCK), lanes(at))
            m = mask[r : r + BLOCK]
            branch = (S.f3[here] * scale + shift) * m
            gate = jax.nn.sigmoid(S.gb[here])
            z = x[here].astype(F32) + branch * (1.0 + gate)
            s = jax.nn.sigmoid(z)
            out = z * s
            gz = S.cot[here].astype(F32) * m * (s + out * (1.0 - s))
            S.cot[here] = (out * m).astype(BF16)
            S.gi[here] = gz
            S.gb[here] = gz * (1.0 + gate)
            S.g3[here] = (gz * branch * gate * (1.0 - gate)).astype(BF16)

    columns(wide, ends)
    out_copy = pltpu.make_async_copy(S.cot, R.block_out, local.take())
    out_copy.start()

    S.gm[...] = dot_bt(S.g3[...], S.wx[...]).astype(BF16)
    zf = dot_bt(S.gm[...], S.wfc[0 : ntap * red, :])
    S.z[PAD : PAD + rows, lanes(0, ntap * red)] = zf
    gmc = lax.dot_general(S.up[...], S.gm[...], (((0,), (0,)), ((), ())), preferred_element_type=F32).astype(BF16)
    S.z[PAD : PAD + small_rows, lanes(ntap * red, ntap * red)] = dot_bt(gmc, S.wfc[ntap * red :, :])
    S.z[PAD + small_rows : PAD + small_rows + PAD, lanes(ntap * red, ntap * red)] = jnp.zeros((PAD, ntap * red), F32)
    coarse = gather_taps(S.z, red, tap_small, cells, 0, half, ntap * red)
    coarse = dot_at(S.pool[...], coarse.astype(BF16))
    for r in blocks:
        gd = gather_taps(S.z, red, tap, cells, r, grid, 0) + coarse[r : r + BLOCK]
        S.gd[r : r + BLOCK] = gd
        S.gd_low[r : r + BLOCK] = gd.astype(BF16)
    copies = swap(S.gd_low, S.halo2)
    last = lay.squeeze - red
    grads[last : lay.squeeze] = jnp.zeros((red, mid), BF16)
    for b in range(wide // mid):
        grads[lay.excite + b * red : lay.excite + (b + 1) * red] = dot_at(
            S.mo[...], S.g3[:, lanes(b * mid, mid)]
        ).astype(BF16)
    for t in range(2 * ntap):
        top = lay.scales + t // lay.scale_taps * red
        grads[top : top + red, lanes(t % lay.scale_taps * red, red)] = dot_at(
            S.cc[:, lanes(t * red, red)], S.gm[...]
        ).astype(BF16)
    for copy in copies:
        copy.wait()
    for r in blocks:
        g = S.halo2[0, r : r + BLOCK].astype(F32) * has_before + S.halo2[1, r : r + BLOCK].astype(F32) * has_after
        S.gsq[r : r + BLOCK] = (g - 2.0 * S.gd[r : r + BLOCK]).astype(BF16)
    S.z[PAD : PAD + rows, lanes(0, wide)] = dot_bt(S.gsq[...], S.wq[...])

    def branch_grad(at, j):
        _, _, mean, root = affine(2, at)
        s = q = jnp.zeros((8, LANES), F32)
        for r in blocks:
            here = (slice(r, r + BLOCK), lanes(at))
            g = (S.gb[here] + S.z[PAD + r : PAD + r + BLOCK, lanes(at)]) * mask[r : r + BLOCK]
            S.gb[here] = g
            s, q = s + fold(g), q + fold(g * ((S.f3[here] - mean) * root))
        all_sums[3].put(0, at, total_of(s))
        all_sums[3].put(1, at, total_of(q))

    columns(wide, branch_grad)
    all_sums[3].start()
    for b in range(mid // red):
        grads[lay.squeeze : lay.squeeze + mid, lanes(b * red, red)] = dot_at(
            S.branch[:, lanes(b * mid, mid)], S.gsq[...]
        ).astype(BF16)
    advance()
    all_sums[3].middle()
    advance()
    for copy in h1_copies:
        copy.wait()

    def widen(k, carry):
        for r in blocks:
            start = pl.multiple_of(k * rows + r, BLOCK)
            S.h1_all[pl.ds(PAD + start, BLOCK)] = S.h1_in[k, r : r + BLOCK].astype(F32)
        return carry

    lax.fori_loop(0, place.plane, widen, 0)
    all_sums[3].finish()
    advance()

    def through(k, back, src, given, dst, width):
        stat = stats[back]

        def body(at, j):
            scale, _, mean, root = affine(k, at)
            gb, gg = stat[0:1, lanes(at)] * inv, stat[1:2, lanes(at)] * inv
            for r in blocks:
                here = (slice(r, r + BLOCK), lanes(at))
                hat = (src[here] - mean) * root
                dst[here] = (scale * (given[here] - (gb + hat * gg) * mask[r : r + BLOCK])).astype(BF16)

        columns(width, body)

    def act_back(k, ar, src, value, at):
        scale, shift, mean, root = affine(k, at)
        s = q = jnp.zeros((8, LANES), F32)
        for r in blocks:
            here = (slice(r, r + BLOCK), lanes(at))
            a = src[here]
            y = a * scale + shift
            sg = jax.nn.sigmoid(y)
            g = value(r) * mask[r : r + BLOCK] * (sg * (1.0 + y * (1.0 - sg)))
            S.gy[here] = g
            s, q = s + fold(g), q + fold(g * ((a - mean) * root))
        ar.put(0, at, total_of(s))
        ar.put(1, at, total_of(q))

    through(2, 3, S.f3, S.gb, S.g3, wide)
    S.gh[...] = dot_bt(S.g3[...], S.we[...])

    def back_two(at, j):
        act_back(1, all_sums[4], S.f2, lambda r: S.gh[r : r + BLOCK, lanes(at)], at)

    columns(mid, back_two)
    advance()
    all_sums[4].start()
    for b in range(wide // mid):
        grads[lay.expand + b * mid : lay.expand + (b + 1) * mid] = dot_at(
            S.h2[...], S.g3[:, lanes(b * mid, mid)]
        ).astype(BF16)
    advance()
    stem.back(stats[3][:, lanes(wide)], lay.stem)
    all_sums[4].middle()
    advance()
    all_sums[4].finish()
    advance()
    through(1, 4, S.f2, S.gy, S.g2, mid)

    def output_quarter(ref):
        return lambda t: ref.at[:, pl.ds(pl.multiple_of(lax.rem(t, 4) * LANES, LANES), LANES)]
    S.z[PAD : PAD + rows, :] = dot_bt(S.g2[...], S.ws[...])
    advance()

    def back_one(at, j):
        act_back(
            0,
            all_sums[5],
            S.f1,
            lambda r: gather_taps_at(S.z, mid, tap, cells, r, grid, at),
            at,
        )

    def gather_taps_at(z, width, masks, per, r, stride, at):
        acc = None
        for t, (di, dj) in enumerate(TAPS):
            off = PAD + r + di * stride + dj
            start = pl.multiple_of((ntap - 1 - t) * width + at, LANES)
            v = z[off : off + BLOCK, lanes(start)] * masks[t, r % per : r % per + BLOCK]
            acc = v if acc is None else acc + v
        return acc

    columns(mid, back_one)
    all_sums[5].start()

    g_copies = plane_send(output_quarter(S.g2), S.g2_in)
    advance()
    all_sums[5].middle()
    advance()
    all_sums[5].finish()
    advance()
    through(0, 5, S.f1, S.gy, S.g1, mid)
    for b in range(wide // mid):
        grads[lay.reduce + b * mid : lay.reduce + (b + 1) * mid] = dot_at(
            x[:, lanes(b * mid, mid)], S.g1[...]
        ).astype(BF16)
    advance()
    for copy in g_copies:
        copy.wait()
    all_rows = place.plane * rows
    g_all = S.g2_in[...].reshape(all_rows, LANES)
    for t, (di, dj) in enumerate(TAPS):
        off = PAD + di * grid + dj

        def shifted(k, carry):
            for r in range(0, rows, BLOCK):
                start = pl.multiple_of(k * rows + r, BLOCK)
                for at in range(0, lay.spatial_in, LANES):
                    v = S.h1_all[pl.ds(start, BLOCK + 2 * PAD), at : at + LANES][off : off + BLOCK]
                    v = v * tap[t, r % cells : r % cells + BLOCK]
                    S.h1_tap[pl.ds(start, BLOCK), at : at + LANES] = v.astype(BF16)
            return carry

        lax.fori_loop(0, place.plane, shifted, 0)
        block = dot_at(g_all, S.h1_tap[...])
        S.shares[t * lay.spatial_in : (t + 1) * lay.spatial_in] = block.T.astype(BF16)
        if t % 2 == 1 or t == ntap - 1:
            advance()
    S.z[PAD : PAD + rows, lanes(0, wide)] = dot_bt(S.g1[...], S.wr[...])
    advance()

    def features_grad(at, j):
        for r in blocks:
            here = (slice(r, r + BLOCK), lanes(at))
            g = (S.gi[here] + S.z[PAD + r : PAD + r + BLOCK, lanes(at)]) * mask[r : r + BLOCK]
            S.g3[here] = g.astype(BF16)

    columns(wide, features_grad)
    feat_copy = pltpu.make_async_copy(S.g3, R.grad_features, local.take())
    feat_copy.start()

    advance()
    advance()
    while jobs:
        jobs = [job for job in jobs if job.step() < 4]
    small = R.sums
    at = 0
    for k, width in ((5, mid), (4, mid), (3, wide + LANES)):
        small[:, lanes(at, width)] = stats[k][...]
        at += width
    stem_copy.wait()
    out_copy.wait()
    feat_copy.wait()


def block(clips, segs, feats, cot, res_group, deep, stem):
    (w_reduce, gain_one, bias_one, w_spatial, gain_two, bias_two, w_expand, gain_three, bias_three) = deep[:9]
    w_squeeze, w_fine, w_coarse, w_excite = deep[9:]
    images, _, grid, _, wide = feats.shape
    rows = images * grid * grid
    mid, red = w_reduce.shape[1], w_squeeze.shape[1]
    taps = len(TAPS)
    lay = Layout(wide, mid, red)
    small_rows = rows // 4
    frames, stem_cot, stem_weight, diff_weight, stem_gain, stem_bias = stem
    count, side, colours = frames.shape[2], frames.shape[3], frames.shape[5]
    kernel, channels = stem_weight.shape[0], stem_weight.shape[3]
    stem_cells = images * (side // 2) ** 2
    stem_rows = images * side // 2
    stem_lanes = side // 2 * channels
    depth = colours * side * 8 + 3 * 256
    inputs = dict(
        x=feats.reshape(rows, wide),
        cot=cot.reshape(rows, wide),
        groups=res_group,
        wr=w_reduce,
        ws=w_spatial.reshape(taps * mid, mid),
        we=w_expand,
        wq=w_squeeze,
        wf=w_fine.reshape(taps * red, red),
        wc=w_coarse.reshape(taps * red, red),
        wx=w_excite,
        gain_one=gain_one.reshape(1, mid),
        bias_one=bias_one.reshape(1, mid),
        gain_two=gain_two.reshape(1, mid),
        bias_two=bias_two.reshape(1, mid),
        gain_three=gain_three.reshape(1, wide),
        bias_three=bias_three.reshape(1, wide),
        frames=jnp.transpose(frames, (0, 1, 2, 5, 3, 4)).reshape(images * count * colours, side, side),
        stem_cot=stem_cot.reshape(stem_cells, channels),
        stem_w=jnp.transpose(stem_weight, (0, 2, 1, 3)).reshape(kernel * colours, kernel, channels),
        diff_w=diff_weight.reshape(len(TAPS), diff_weight.shape[2], channels),
        stem_gain=stem_gain.reshape(1, channels),
        stem_bias=stem_bias.reshape(1, channels),
    )
    outputs = dict(
        block_out=jax.ShapeDtypeStruct((rows, wide), BF16),
        grad_features=jax.ShapeDtypeStruct((rows, wide), BF16),
        packed=jax.ShapeDtypeStruct((lay.rows, mid), BF16),
        shared=jax.ShapeDtypeStruct((lay.share_rows, LANES), BF16),
        sums=jax.ShapeDtypeStruct((2, 2 * mid + wide + LANES), F32),
        stem_out=jax.ShapeDtypeStruct((stem_cells, channels), BF16),
    )

    def spec(name):
        if name == "groups":
            return pl.BlockSpec(memory_space=pltpu.SMEM)
        if inputs.get(name, frames).size < 1 << 15 or name == "sums":
            return pl.BlockSpec(memory_space=pltpu.VMEM)
        return pl.BlockSpec(memory_space=pl.ANY)

    plans = [plan for group in lay.plans(clips, segs) for plan in group]
    shared = [plan for _, _, plan in lay.shared_plans(clips, segs)]
    land = sum(plan.landing_rows for plan in plans)
    share_land = sum(plan.landing_rows for plan in shared)
    near, far = 2 * segs, clips // 2
    remote_count = sum(plan.transfers for plan in plans + shared) + 6 * (near + far) + 48
    v = pltpu.VMEM
    scratch = dict(
        x=v((rows, wide), BF16),
        cot=v((rows, wide), BF16),
        wr=v((wide, mid), BF16),
        ws=v((taps * mid, mid), BF16),
        we=v((mid, wide), BF16),
        wq=v((wide, red), BF16),
        wfc=v((2 * taps * red, red), BF16),
        wx=v((red, wide), BF16),
        mask=v((rows, LANES), F32),
        tap=v((taps, grid * grid, LANES), F32),
        tap_small=v((taps, grid * grid, LANES), F32),
        pool=v((small_rows, rows), BF16),
        up=v((rows, small_rows), BF16),
        tmp=v((rows + 2 * PAD, LANES), F32),
        tmp_small=v((small_rows + 2 * PAD, LANES), F32),
        small_col=v((small_rows, taps * red), BF16),
        f1=v((rows, mid), F32),
        f2=v((rows, mid), F32),
        f3=v((rows, wide), F32),
        col=v((rows, taps * mid), BF16),
        h2=v((rows, mid), BF16),
        branch=v((rows, wide), BF16),
        sq=v((rows, red), BF16),
        halo=v((2, rows, red), BF16),
        halo2=v((2, rows, red), BF16),
        diffs=v((rows, 2 * red), BF16),
        cc=v((rows, 2 * taps * red), BF16),
        mo=v((rows, red), BF16),
        gm=v((rows, red), BF16),
        gd=v((rows, red), F32),
        gd_low=v((rows, red), BF16),
        gsq=v((rows, red), BF16),
        gb=v((rows, wide), F32),
        gi=v((rows, wide), F32),
        g3=v((rows, wide), BF16),
        gh=v((rows, mid), F32),
        gy=v((rows, mid), F32),
        g2=v((rows, mid), BF16),
        g1=v((rows, mid), BF16),
        z=v((rows + 2 * PAD, taps * mid), F32),
        grads=v((lay.rows, mid), BF16),
        landing=v((land, mid), BF16),
        shares=v((lay.spatial_block, LANES), BF16),
        share_landing=v((share_land, LANES), BF16),
        h1_in=v((8, rows, lay.spatial_in), BF16),
        h1_all=v((8 * rows + 2 * PAD, lay.spatial_in), F32),
        h1_tap=v((8 * rows, lay.spatial_in), BF16),
        g2_in=v((8, rows, LANES), BF16),
        frames=v((images * count * colours, side, side), BF16),
        stem_cot=v((stem_cells, channels), BF16),
        stem_wide=v((stem_cells, LANES), F32),
        stem_stat=v((2, LANES), F32),
        padded=v((images * (side + 8), LANES), F32),
        stem_taps=v((stem_rows, 512), F32),
        columns=v((2, images * side, LANES), F32),
        xx=v((stem_rows, depth), BF16),
        pre=v((stem_rows, stem_lanes), F32),
        gpre=v((stem_rows, stem_lanes), F32),
        prod=v((depth, LANES), F32),
        bands=v((240, LANES), F32),
        spots=v((144, LANES), F32),
        wt=v((192, LANES), F32),
        wd=v((144, LANES), F32),
    )
    for k, width in enumerate((mid, mid, wide + LANES, wide + LANES, mid, mid)):
        scratch[f"near{k}"] = v((near, 2, width), F32)
        scratch[f"far{k}"] = v((far, 2, width), F32)
        scratch[f"res{k}"] = v((2, width), F32)
    scratch.update(
        local=pltpu.SemaphoreType.DMA((32,)),
        send=pltpu.SemaphoreType.DMA((remote_count,)),
        recv=pltpu.SemaphoreType.DMA((remote_count,)),
    )
    names = list(inputs) + list(outputs)
    result = pl.pallas_call(
        partial(block_kernel, clips, segs, grid, names, list(scratch)),
        out_shape=list(outputs.values()),
        in_specs=[spec(name) for name in inputs],
        out_specs=[spec(name) for name in outputs],
        scratch_shapes=list(scratch.values()),
        compiler_params=pltpu.CompilerParams(
            collective_id=0, has_side_effects=True, vmem_limit_bytes=VMEM_LIMIT
        ),
        name="block",
    )(*inputs.values())
    return result


VMEM_LIMIT = 62 << 20


def spread_kernel(lay, plans, shared_plans, mid, red, wide, ins, outs, names, *refs):
    R = SimpleNamespace(**dict(zip(ins + outs + names, refs)))
    taps = len(TAPS)
    copies, out = [], []

    def read(src, dst):
        copy = pltpu.make_async_copy(src, dst, R.reads.at[len(copies)])
        copy.start()
        copies.append(copy)

    def write(src, dst):
        copy = pltpu.make_async_copy(src, dst, R.writes.at[len(out)])
        copy.start()
        out.append(copy)

    for plan in plans:
        here = pl.ds(plan.first, plan.rows)
        read(R.packed.at[here], R.held.at[here])
    for _, _, plan in shared_plans:
        here = pl.ds(plan.first, plan.rows)
        read(R.shared.at[here], R.shares.at[here])
    passed = [
        (R.block_out, R.block_held, R.out_block),
        (R.grad_features, R.features_held, R.out_features),
        (R.stem_out, R.stem_held, R.out_stem),
    ]
    for src, here, _ in passed:
        read(src, here)
    at = 0
    for bias, gain in (
        (R.bias_one, R.gain_one),
        (R.bias_two, R.gain_two),
        (R.bias_three, R.gain_three),
        (R.stem_bias, R.stem_gain),
    ):
        width = bias.shape[1]
        bias[...] = R.sums[0:1, at : at + width]
        gain[...] = R.sums[1:2, at : at + width]
        at += width
    full = R.full

    def wait_and_convert(k, plan):
        copies[k].wait()
        count, bits_of = plan.pieces()

        def convert(number, carry):
            values = bits_of(number)
            src = pl.multiple_of(plan.packed_at(values), 16)
            dst = pl.multiple_of(plan.first + plan.summed_at(values), 16)
            for r in range(0, plan.piece, 16):
                full[pl.ds(dst + r, 16)] = R.held[pl.ds(src + r, 16)].astype(F32)
            return carry

        lax.fori_loop(0, count, convert, 0)

    for k, plan in enumerate(plans[:3]):
        wait_and_convert(k, plan)
    for k, (_, here, dst) in enumerate(passed):
        copies[len(plans) + len(shared_plans) + k].wait()
        write(here, dst)
    for b in range(wide // mid):
        write(full.at[pl.ds(lay.excite + b * red, red)], R.excite.at[:, pl.ds(b * mid, mid)])
    for t in range(2 * taps):
        top, at = lay.scales + t // lay.scale_taps * red, t % lay.scale_taps * red
        write(full.at[pl.ds(top, red), pl.ds(at, red)], (R.fine if t < taps else R.coarse).at[pl.ds(t % taps * red, red)])
    for b in range(mid // red):
        write(full.at[pl.ds(lay.squeeze, mid), pl.ds(b * red, red)], R.squeeze.at[pl.ds(b * mid, mid)])
    for k, plan in enumerate(plans[3:7]):
        wait_and_convert(3 + k, plan)
        write(full.at[pl.ds(plan.first, mid)], R.expand.at[:, pl.ds(k * mid, mid)])

    for k, (tap, count, plan) in enumerate(shared_plans):
        copies[len(plans) + k].wait()
        number, bits_of = plan.pieces()

        def convert(i, carry):
            values = bits_of(i)
            src = pl.multiple_of(plan.packed_at(values), 16)
            row = plan.summed_at(values)
            x, y, core = values[("clip", 1)], values[("seg", 2)], values[("seg", 1)]
            dst = (tap + row // lay.spatial_in) * mid + x * lay.spatial_in + lax.rem(row, lay.spatial_in)
            at = lanes(pl.multiple_of((y * 2 + core) * LANES, LANES))
            for r in range(0, plan.piece, 16):
                here = pl.ds(pl.multiple_of(dst + r, 16), 16)
                R.full_spatial[here, at] = R.shares[pl.ds(src + r, 16)].astype(F32)
            return carry

        lax.fori_loop(0, number, convert, 0)
        here = pl.ds(tap * mid, count * mid)
        write(R.full_spatial.at[here], R.spatial.at[here])
    for k, plan in enumerate(plans[7:]):
        wait_and_convert(7 + k, plan)
        write(full.at[pl.ds(plan.first, plan.rows)], R.reduce.at[pl.ds(plan.first - lay.reduce, plan.rows)])
    kernel, channels = R.stem_w.shape[1], R.stem_w.shape[2]
    colours = R.stem_w.shape[0] // kernel
    rest = R.rows.shape[0] - LANES
    R.rows[0:LANES] = full[lay.stem : lay.stem + LANES, lanes(0)]
    R.rows[LANES:] = full[lay.stem : lay.stem + rest, lanes(LANES)]
    for ki in range(kernel):
        for c in range(colours):
            part = R.rows[pl.ds(c * kernel * 8 + ki, kernel, stride=8), :]
            R.stem_w[ki * colours + c] = part[:, 0:channels]
    for t in range(taps):
        top, at = (lay.stem + t * 16, 2 * LANES) if t < 8 else (lay.stem, 3 * LANES)
        R.diff_w[t] = full[top : top + R.diff_w.shape[1], at : at + channels]
    for copy in out:
        copy.wait()


def spread(clips, segs, given, sizes):
    mid, red, wide, kernel, colours, channels, differences = sizes
    lay = Layout(wide, mid, red)
    taps = len(TAPS)
    plans = [plan for group in lay.plans(clips, segs) for plan in group]
    shared_plans = lay.shared_plans(clips, segs)

    def f32(*shape):
        return jax.ShapeDtypeStruct(shape, F32)

    outs = dict(
        out_block=given["block_out"],
        out_features=given["grad_features"],
        out_stem=given["stem_out"],
        reduce=f32(wide, mid),
        spatial=f32(taps * mid, mid),
        expand=f32(mid, wide),
        squeeze=f32(wide, red),
        fine=f32(taps * red, red),
        coarse=f32(taps * red, red),
        excite=f32(red, wide),
    )
    outs = {name: jax.ShapeDtypeStruct(out.shape, out.dtype) for name, out in outs.items()}
    small = dict(
        stem_w=f32(kernel * colours, kernel, channels),
        diff_w=f32(taps, differences, channels),
        bias_one=f32(1, mid),
        gain_one=f32(1, mid),
        bias_two=f32(1, mid),
        gain_two=f32(1, mid),
        bias_three=f32(1, wide),
        gain_three=f32(1, wide),
        stem_bias=f32(1, channels),
        stem_gain=f32(1, channels),
    )
    scratch = dict(
        held=pltpu.VMEM((lay.rows, mid), BF16),
        shares=pltpu.VMEM((lay.share_rows, LANES), BF16),
        full=pltpu.VMEM((lay.rows, mid), F32),
        full_spatial=pltpu.VMEM((taps * mid, mid), F32),
        rows=pltpu.VMEM((176, LANES), F32),
        block_held=pltpu.VMEM(given["block_out"].shape, BF16),
        features_held=pltpu.VMEM(given["grad_features"].shape, BF16),
        stem_held=pltpu.VMEM(given["stem_out"].shape, BF16),
        reads=pltpu.SemaphoreType.DMA((32,)),
        writes=pltpu.SemaphoreType.DMA((64,)),
    )
    here, anywhere = pl.BlockSpec(memory_space=pltpu.VMEM), pl.BlockSpec(memory_space=pl.ANY)
    names = list(outs) + list(small)
    results = pl.pallas_call(
        partial(
            spread_kernel, lay, plans, shared_plans, mid, red, wide, list(given), names, list(scratch)
        ),
        out_shape=list(outs.values()) + list(small.values()),
        in_specs=[here if array.size < 1 << 15 else anywhere for array in given.values()],
        out_specs=[anywhere] * len(outs) + [here] * len(small),
        scratch_shapes=list(scratch.values()),
        compiler_params=pltpu.CompilerParams(vmem_limit_bytes=VMEM_LIMIT),
        name="spread",
    )(*given.values())
    return SimpleNamespace(**dict(zip(names, results)))


def shards(
    frames,
    features,
    res_group,
    stem_weight,
    diff_weight,
    stem_gain,
    stem_bias,
    w_reduce,
    gain_one,
    bias_one,
    w_spatial,
    gain_two,
    bias_two,
    w_expand,
    gain_three,
    bias_three,
    w_squeeze,
    w_fine,
    w_coarse,
    w_excite,
    stem_cotangent,
    block_cotangent,
):
    clips, segs = lax.axis_size("clip"), lax.axis_size("seg")
    wide, mid, red = w_reduce.shape[0], w_reduce.shape[1], w_squeeze.shape[1]
    deep = (
        w_reduce, gain_one, bias_one, w_spatial, gain_two, bias_two, w_expand, gain_three, bias_three,
        w_squeeze, w_fine, w_coarse, w_excite,
    )
    stem = (frames, stem_cotangent, stem_weight, diff_weight, stem_gain, stem_bias)
    block_out, grad_feats, packed, shared, sums, stem_out = block(
        clips, segs, features, block_cotangent, res_group, deep, stem
    )
    kernel, colours, channels = stem_weight.shape[0], stem_weight.shape[2], stem_weight.shape[3]
    given = dict(
        packed=packed, shared=shared, sums=sums, block_out=block_out, grad_features=grad_feats, stem_out=stem_out
    )
    sizes = (mid, red, wide, kernel, colours, channels, diff_weight.shape[2])
    g = spread(clips, segs, given, sizes)
    g_stem_w = jnp.transpose(g.stem_w.reshape(kernel, colours, kernel, channels), (0, 2, 1, 3))
    return (
        g.out_stem.reshape(stem_cotangent.shape),
        g.out_block.reshape(features.shape),
        g.out_features.reshape(features.shape),
        g_stem_w,
        g.diff_w.reshape(diff_weight.shape),
        g.stem_gain.reshape(channels),
        g.stem_bias.reshape(channels),
        g.reduce,
        g.gain_one.reshape(mid),
        g.bias_one.reshape(mid),
        g.spatial.reshape(w_spatial.shape),
        g.gain_two.reshape(mid),
        g.bias_two.reshape(mid),
        g.expand,
        g.gain_three.reshape(wide),
        g.bias_three.reshape(wide),
        g.squeeze,
        g.fine.reshape(w_fine.shape),
        g.coarse.reshape(w_coarse.shape),
        g.excite,
    )


def solution(mesh):
    split = P("clip", "seg")
    whole = P()
    ins = (split, split) + (whole,) * 18 + (split, split)
    outs = (split,) * 3 + (whole,) * 17
    return jax.shard_map(shards, mesh=mesh, in_specs=ins, out_specs=outs, check_vma=False)
```

```python
from functools import partial
from types import SimpleNamespace

import jax
import jax.numpy as jnp
from jax import lax
from jax.experimental import pallas as pl
from jax.experimental.pallas import tpu as pltpu
from jax.sharding import PartitionSpec as P

MESH = pl.DeviceIdType.MESH
F32, BF16 = jnp.float32, jnp.bfloat16
LANES = 128
BLOCK = 64
PAD = 16
TAPS = [(di, dj) for di in (-1, 0, 1) for dj in (-1, 0, 1)]


def dot(a, b):
    return lax.dot_general(a, b, (((1,), (0,)), ((), ())), preferred_element_type=F32)


def dot_bt(a, b):
    return lax.dot_general(a, b, (((1,), (1,)), ((), ())), preferred_element_type=F32)


def dot_at(a, b):
    return lax.dot_general(a, b, (((0,), (0,)), ((), ())), preferred_element_type=F32)


def columns(total, body, step=LANES):
    def go(j, carry):
        body(pl.multiple_of(j * step, step), j)
        return carry

    lax.fori_loop(0, total // step, go, 0)


def log2(power):
    return power.bit_length() - 1


def lanes(start, size=LANES):
    return pl.ds(start, size)


def fold(block):
    return block.reshape(block.shape[0] // 8, 8, LANES).sum(axis=0)


def total_of(part):
    return jnp.sum(part, axis=0, keepdims=True)


class Sems:
    def __init__(self, ref):
        self.ref, self.used = ref, 0

    def take(self):
        self.used += 1
        return self.ref.at[self.used - 1]


class Place:
    def __init__(self, clips, segs):
        self.clips, self.segs = clips, segs
        self.clip, self.seg = lax.axis_index("clip"), lax.axis_index("seg")
        self.near = 2 * segs
        self.far = clips // 2
        self.near_me = lax.rem(self.clip, 2) * segs + self.seg
        self.far_me = self.clip // 2

        self.plane = 8
        self.plane_me = lax.rem(self.clip, 2) * 4 + lax.rem(self.seg, 4)

    def plane_device(self, t):
        return ((self.clip // 2) * 2 + t // 4, (self.seg // 4) * 4 + lax.rem(t, 4))

    def near_device(self, t):
        return ((self.clip // 2) * 2 + t // self.segs, lax.rem(t, self.segs))

    def far_device(self, t):
        return (t * 2 + lax.rem(self.clip, 2), self.seg)

    def bit(self, axis, stride):
        mine = self.seg if axis == "seg" else self.clip
        bit = lax.rem(mine // stride, 2)
        other = mine + stride * (1 - 2 * bit)
        return bit, (self.clip, other) if axis == "seg" else (other, self.seg)

    def greet(self):
        sem = pltpu.get_barrier_semaphore()

        def near(k, carry):
            pl.semaphore_signal(
                sem, inc=1, device_id=self.near_device(lax.rem(self.near_me + k, self.near)), device_id_type=MESH
            )
            return carry

        def far(k, carry):
            pl.semaphore_signal(
                sem, inc=1, device_id=self.far_device(lax.rem(self.far_me + k, self.far)), device_id_type=MESH
            )
            return carry

        lax.fori_loop(1, self.near, near, 0)
        lax.fori_loop(1, self.far, far, 0)

    def greeted(self):
        pl.semaphore_wait(pltpu.get_barrier_semaphore(), self.near + self.far - 2)


def remote(src, dst, sends, recvs, device):
    copy = pltpu.make_async_remote_copy(
        src_ref=src,
        dst_ref=dst,
        send_sem=sends.take(),
        recv_sem=recvs.take(),
        device_id=device,
        device_id_type=MESH,
    )
    copy.start()
    return copy


class Sums:
    def __init__(self, place, near_buf, far_buf, result, sends, recvs):
        self.place, self.near_buf, self.far_buf, self.result = place, near_buf, far_buf, result
        self.sends, self.recvs = sends, recvs

    def put(self, row, at, value):
        self.near_buf[self.place.near_me, row : row + 1, lanes(at, value.shape[1])] = value

    def _send(self, buf, me, count, device):
        mine = buf.at[me]
        return [remote(mine, mine, self.sends, self.recvs, device(lax.rem(me + k, count))) for k in range(1, count)]

    def _add(self, buf, count):
        value = buf[0]
        for k in range(1, count):
            value = value + buf[k]
        return value

    def start(self):
        p = self.place
        self.copies = self._send(self.near_buf, p.near_me, p.near, p.near_device)

    def middle(self):
        p = self.place
        for copy in self.copies:
            copy.wait()
        self.far_buf[p.far_me] = self._add(self.near_buf, p.near)
        self.copies = self._send(self.far_buf, p.far_me, p.far, p.far_device)

    def finish(self):
        for copy in self.copies:
            copy.wait()
        self.result[...] = self._add(self.far_buf, self.place.far)


def bit_order(clips, segs, letters):
    seg = [("seg", 1 << k) for k in range(segs.bit_length() - 1)]
    clip = [("clip", 1 << k) for k in range(clips.bit_length() - 1)]
    others = seg[2:] + clip[1:]
    named = dict(c=seg[:1], x=clip[:1], y=seg[1:2], p=others[:-1], q=others[-1:])
    return [bit for letter in letters for bit in named[letter]]


class Plan:
    def __init__(self, clips, segs, first, rows, letters, nest, skip=""):
        self.first, self.rows = first, rows
        skip = bit_order(clips, segs, skip)
        held = rows >> len(skip)
        self.block, self.sums, split = held, [], list(skip)
        for bit in bit_order(clips, segs, letters):
            if bit in skip:
                continue
            half = held // 2
            halved = held % 2 == 0 and half % 16 == 0
            held = half if halved else held
            self.sums.append((bit, held, halved))
            if halved:
                split.append(bit)
        self.piece = held
        self.places, size = [], rows
        for bit in bit_order(clips, segs, nest):
            if bit in split:
                size //= 2
                self.places.append((bit, size))
        self.landing_rows = sum(size for _, size, _ in self.sums)
        self.transfers = len(self.sums) + len(self.places)

    def each_piece(self, body):
        bits = [bit for bit, _ in self.places]
        outer, inner = bits[:-3], bits[-3:]

        def some(number, carry):
            values = {bit: lax.rem(number // (1 << k), 2) for k, bit in enumerate(outer)}
            for n in range(1 << len(inner)):
                values.update({bit: (n >> k) % 2 for k, bit in enumerate(inner)})
                body(values)
            return carry

        lax.fori_loop(0, 1 << len(outer), some, 0)

    def packed_at(self, values):
        return sum((values[bit] * size for bit, size in self.places), self.first)

    def summed_at(self, values):
        return sum((values[bit] * size for bit, size, halved in self.sums if halved), 0)


class Job:
    def __init__(self, place, plan, buffers, held, land, sems):
        self.grads, self.landing, self.packed = buffers
        self.local, self.sends, self.recvs = sems
        self.sums, self.places = [], []
        for (axis, stride), size, halved in plan.sums:
            bit, device = place.bit(axis, stride)
            away = held
            if halved:
                away = held + (1 - bit) * size
                held = held + bit * size
            self.sums.append((held, away, size, device, land))
            land += size
        self.held, self.piece, self.land_end = held, plan.piece, land
        first = plan.first
        for (axis, stride), size in plan.places:
            bit, device = place.bit(axis, stride)
            first = first + bit * size
            self.places.append((first, size, device))
        self.first = first
        self.at = self.phase = 0

    def _rows(self, ref, start, size):
        if not isinstance(start, int):
            start = pl.multiple_of(start, 16)
        return ref.at[pl.ds(start, size)]

    def scatter_start(self):
        held, away, size, device, land = self.sums[self.at]
        self.copy = remote(
            self._rows(self.grads, away, size), self._rows(self.landing, land, size), self.sends, self.recvs, device
        )

    def scatter_finish(self):
        held, away, size, device, land = self.sums[self.at]
        self.copy.wait()
        block = 32 if size % 32 == 0 else 16

        def add(k, carry):
            mine = pl.ds(pl.multiple_of(held + k * block, 16), block)
            theirs = pl.ds(pl.multiple_of(land + k * block, 16), block)
            self.grads[mine] = self.grads[mine] + self.landing[theirs]
            return carry

        lax.fori_loop(0, size // block, add, 0)
        self.at += 1

    def own_start(self):
        self.copy = pltpu.make_async_copy(
            self._rows(self.grads, self.held, self.piece),
            self._rows(self.packed, self.first, self.piece),
            self.local.take(),
        )
        self.copy.start()
        self.at = len(self.places)

    def gather_start(self):
        first, size, device = self.places[self.at - 1]
        mine = self._rows(self.packed, first, size)
        self.copy = remote(mine, mine, self.sends, self.recvs, device)

    def gather_finish(self):
        self.at -= 1
        self.copy.wait()

    def step(self):
        if self.phase == 0:
            self.scatter_start()
            self.phase = 1
        elif self.phase == 1:
            self.scatter_finish()
            if self.at < len(self.sums):
                self.scatter_start()
            else:
                self.own_start()
                self.phase = 2
        elif self.phase == 2:
            self.copy.wait()
            self.gather_start()
            self.phase = 3
        elif self.phase == 3:
            self.gather_finish()
            if self.at > 0:
                self.gather_start()
            else:
                self.phase = 4
        return self.phase


class Stem:
    KERNEL = 7
    COLOURS = 3

    def __init__(self, R, S, images, side, count):
        self.R, self.S, self.images, self.side, self.count = R, S, images, side, count
        self.cells = side // 2
        self.pairs = self.cells // 2
        self.band = side * 8
        self.fine = self.COLOURS * self.band
        self.half_rows = images * self.pairs
        self.depth = S.xx.shape[1]
        self.spread = (self.depth - self.fine) // 3

    def _table(self, q):
        per = self.S.grads.shape[1] // LANES
        table, top = self._part(q // per)
        return table, top, lanes(q % per * LANES)

    def _part(self, n):
        return (self.S.grads, n * self.depth) if n < 2 else (self.S.landing, 0)

    def tables(self):
        R, S = self.R, self.S
        wt, wd = S.wt, S.wd
        tall = 32

        def clear(k, carry):
            for n in range(3):
                table, top = self._part(n)
                table[pl.ds(pl.multiple_of(top + k * tall, tall), tall)] = jnp.zeros((tall, table.shape[1]), BF16)
            return carry

        lax.fori_loop(0, self.depth // tall, clear, 0)
        wt[...] = jnp.zeros(wt.shape, F32)
        wd[...] = jnp.zeros(wd.shape, F32)
        weights = R.stem_w[...].astype(F32)
        for ki in range(self.KERNEL):
            for c in range(self.COLOURS):
                for kj in range(self.KERNEL):
                    at = c * 64 + kj * 8 + ki
                    wt[at : at + 1, 0:64] = weights[ki * self.COLOURS + c, kj : kj + 1]
        for c in range(self.COLOURS):
            for p in range(5):
                block = jnp.zeros((16, LANES), F32)
                if p < 4:
                    block = block + wt[c * 64 + 16 * p : c * 64 + 16 * p + 16, :]
                if p > 0:
                    high = wt[c * 64 + 16 * p - 16 : c * 64 + 16 * p, :]
                    block = block + pltpu.roll(high, 64, 1)
                block = block.astype(BF16)
                for q in range(self.pairs):
                    j = 4 * q - 2 + 2 * p
                    if 0 <= j < self.side:
                        table, top, at = self._table(q)
                        top = top + c * self.band + j * 8
                        table[top : top + 16, at] = block
        weights = R.diff_w[...].astype(F32)
        for t in range(9):
            wd[t * 16 : t * 16 + weights.shape[1], 0:64] = weights[t]
        for ki in range(3):
            for kj in range(3):
                block = wd[(ki * 3 + kj) * 16 : (ki * 3 + kj) * 16 + 16, :]
                block = (block + pltpu.roll(block, 64, 1)).astype(BF16)
                for q in range(self.pairs):
                    j = q + kj - 1
                    if 0 <= j < self.pairs:
                        table, top, at = self._table(q)
                        top = top + self.fine + ki * self.spread + j * 16
                        table[top : top + 16, at] = block

    def patches(self):
        S, side, images = self.S, self.side, self.images
        frames, padded, taps, xx = S.frames, S.padded, S.stem_taps, S.xx
        tall = padded.shape[0] // images
        padded[...] = jnp.zeros(padded.shape, F32)
        taps[...] = jnp.zeros(taps.shape, F32)
        row = lax.broadcasted_iota(jnp.int32, (taps.shape[1], self.band), 0)
        lane = lax.broadcasted_iota(jnp.int32, (taps.shape[1], self.band), 1)
        place = jnp.where(row == (lane & 7) * 64 + (lane >> 3), 1.0, 0.0).astype(BF16)
        for c in range(self.COLOURS):
            for img in range(images):
                plane = frames[(img * 5 + 2) * self.COLOURS + c].astype(F32)
                padded[img * tall + 2 : img * tall + 2 + side, 0:side] = plane
            for ki in range(self.KERNEL):
                for parity in range(2):
                    for img in range(images):
                        start = img * tall + 2 * parity + ki
                        piece = padded[pl.ds(start, self.pairs, stride=4), 0:64]
                        top = parity * self.half_rows + img * self.pairs
                        taps[top : top + self.pairs, ki * 64 : ki * 64 + 64] = piece
            xx[:, lanes(c * self.band, self.band)] = dot(taps[...].astype(BF16), place).astype(BF16)
        row = lax.broadcasted_iota(jnp.int32, (side, self.spread), 0)
        lane = lax.broadcasted_iota(jnp.int32, (side, self.spread), 1)
        inside = (row >> 2) == (lane >> 4)
        channel = lane & 15
        total = None
        for f in range(5):
            for c in range(self.COLOURS):
                sign = jnp.zeros((side, self.spread), F32)
                if f > 0:
                    sign = sign + jnp.where(channel == (f - 1) * self.COLOURS + c, 1.0, 0.0)
                if f < 4:
                    sign = sign - jnp.where(channel == f * self.COLOURS + c, 1.0, 0.0)
                sign = jnp.where(inside, sign, 0.0).astype(BF16)
                planes = jnp.concatenate(
                    [frames[(img * 5 + f) * self.COLOURS + c] for img in range(images)], axis=0
                )
                part = dot(planes, sign)
                total = part if total is None else total + part
        for h in range(self.spread // LANES):
            S.columns[h] = total[:, h * LANES : (h + 1) * LANES]
        pooled = None
        for k in range(4):
            parts = [
                S.columns[h, pl.ds(k, self.half_rows, stride=4), :] for h in range(self.spread // LANES)
            ]
            part = jnp.concatenate(parts, axis=1)
            pooled = part if pooled is None else pooled + part
        pooled = (pooled * 0.0625).astype(BF16).astype(F32)
        row = lax.rem(lax.broadcasted_iota(jnp.int32, pooled.shape, 0), self.pairs)
        for ki in range(3):
            rolled = pltpu.roll(pooled, (1 - ki) % self.half_rows, 0)
            ok = (row + ki - 1 >= 0) & (row + ki - 1 < self.pairs)
            rolled = jnp.where(ok, rolled, 0.0).astype(BF16)
            at = lanes(self.fine + ki * self.spread, self.spread)
            xx[0 : self.half_rows, at] = rolled
            xx[self.half_rows :, at] = rolled

    def forward(self, sums, at):
        S, per = self.S, self.S.grads.shape[1]
        for n in range(self.pairs * LANES // per):
            table, top = self._part(n)
            S.pre[:, lanes(n * per, per)] = dot(S.xx[...], table[top : top + self.depth, :])
        s = q = jnp.zeros((8, LANES), F32)
        for k in range(self.pairs):
            v = S.pre[:, lanes(k * LANES)]
            s, q = s + fold(v), q + fold(v * v)
        self._put(sums, at, s, q)

    def _put(self, sums, at, s, q):
        for row, part in enumerate((s, q)):
            part = total_of(part)
            sums.put(row, at, part + pltpu.roll(part, 64, 1))

    def _norm(self):
        S, inv = self.S, 1.0 / self.count
        mean = S.stem_stat[0:1, :] * inv
        root = lax.rsqrt(S.stem_stat[1:2, :] * inv - mean * mean + 1e-05)
        gain, bias = self.R.stem_gain[...], self.R.stem_bias[...]
        scale = root * jnp.concatenate([gain, gain], axis=1)
        return scale, jnp.concatenate([bias, bias], axis=1) - mean * scale, mean, root

    def rear(self, stat, sums, at):
        S = self.S
        S.stem_stat[...] = stat
        scale, shift, mean, root = self._norm()
        step = 2 * self.cells
        S.stem_wide[:, 0:64] = S.stem_cot[...].astype(F32)
        s = q = jnp.zeros((8, LANES), F32)
        for k in range(self.pairs):
            pre = S.pre[:, lanes(k * LANES)]
            cot = []
            for parity in range(2):
                pieces = [
                    S.stem_wide[pl.ds(parity * self.cells + 2 * k + i, self.half_rows, stride=step), 0:64]
                    for i in range(2)
                ]
                cot.append(jnp.concatenate(pieces, axis=1))
            y = pre * scale + shift
            sg = jax.nn.sigmoid(y)
            out = y * sg
            g = jnp.concatenate(cot, axis=0) * (sg + out * (1.0 - sg))
            S.gpre[:, lanes(k * LANES)] = g
            s, q = s + fold(g), q + fold(g * ((pre - mean) * root))
            swapped = pltpu.roll(out, 64, 1)
            for parity in range(2):
                rows = slice(parity * self.half_rows, (parity + 1) * self.half_rows)
                for i, half in enumerate((out, swapped)):
                    where = pl.ds(parity * self.cells + 2 * k + i, self.half_rows, stride=step)
                    S.stem_wide[where, :] = half[rows]
        S.stem_cot[...] = S.stem_wide[:, 0:64].astype(BF16)
        self._put(sums, at, s, q)

    def back(self, stat, top):
        S, inv = self.S, 1.0 / self.count
        scale, _, mean, root = self._norm()
        gb, gg = stat[0:1, :] * inv, stat[1:2, :] * inv
        bands, spots = S.bands, S.spots
        bands[...] = jnp.zeros(bands.shape, F32)
        spots[...] = jnp.zeros(spots.shape, F32)
        for k in range(self.pairs):
            hat = (S.pre[:, lanes(k * LANES)] - mean) * root
            g = (scale * (S.gpre[:, lanes(k * LANES)] - gb - hat * gg)).astype(BF16)
            S.prod[...] = dot_at(S.xx[...], g)
            for c in range(self.COLOURS):
                for p in range(5):
                    j = 4 * k - 2 + 2 * p
                    if 0 <= j < self.side:
                        here = slice((c * 5 + p) * 16, (c * 5 + p) * 16 + 16)
                        start = c * self.band + j * 8
                        bands[here] = bands[here] + S.prod[start : start + 16]
            for ki in range(3):
                for kj in range(3):
                    j = k + kj - 1
                    if 0 <= j < self.pairs:
                        here = slice((ki * 3 + kj) * 16, (ki * 3 + kj) * 16 + 16)
                        start = self.fine + ki * self.spread + j * 16
                        spots[here] = spots[here] + S.prod[start : start + 16]
        low = lax.broadcasted_iota(jnp.int32, (8, LANES), 1) < 64
        for c in range(self.COLOURS):
            for kj in range(self.KERNEL):
                first = bands[c * 80 + kj * 8 : c * 80 + kj * 8 + 8]
                other = bands[c * 80 + kj * 8 + 16 : c * 80 + kj * 8 + 24]
                at = (c * self.KERNEL + kj) * 8
                S.wt[at : at + 8] = jnp.where(low, first + pltpu.roll(other, 64, 1), 0.0)
        grads = S.grads
        grads[top : top + LANES, :] = jnp.zeros((LANES, grads.shape[1]), BF16)
        rest = S.wt.shape[0] - LANES
        used = self.COLOURS * self.KERNEL * 8
        S.wt[used:] = jnp.zeros((S.wt.shape[0] - used, LANES), F32)
        grads[top : top + LANES, lanes(0)] = S.wt[0:LANES].astype(BF16)
        grads[top : top + rest, lanes(LANES)] = S.wt[LANES:].astype(BF16)
        both = spots[...] + pltpu.roll(spots[...], 64, 1)
        grads[top : top + LANES, lanes(2 * LANES)] = both[0:LANES].astype(BF16)
        grads[top : top + 16, lanes(3 * LANES)] = both[LANES:].astype(BF16)


class Layout:
    def __init__(self, wide, mid, red):
        taps = len(TAPS)
        self.excite = 0
        self.scales = self.excite + red * wide // mid
        self.scale_taps = mid // red
        groups = -(-2 * taps // self.scale_taps)
        self.squeeze = self.scales + groups * red
        self.stem = self.squeeze + wide * red // mid
        self.expand = self.stem + LANES
        self.reduce = self.expand + wide
        self.rows = self.reduce + wide
        self.spatial_in = mid // 2
        self.spatial_block = taps * self.spatial_in
        self.share_rows = 8 * self.spatial_block

    def plans(self, clips, segs):
        quarter = (self.reduce - self.expand) // 4
        half = (self.rows - self.reduce) // 2

        def plan(first, end, letters, nest):
            return Plan(clips, segs, first, end - first, letters, nest)

        bounds = list(range(0, self.expand, 512)) + [self.expand]
        early = [plan(bounds[k], bounds[k + 1], *orders) for k, orders in enumerate(EARLY)]
        middle = [
            plan(self.expand + k * quarter, self.expand + (k + 1) * quarter, *orders)
            for k, orders in enumerate(MIDDLE)
        ]
        late = [plan(self.reduce, self.reduce + half, *LATE[0]), plan(self.reduce + half, self.rows, *LATE[1])]
        return early, middle, late

    def shared_plans(self, clips, segs):
        parts, first = [], 0
        for k, nest in enumerate(SPATIAL):
            count = min(2, len(TAPS) - 2 * k)
            rows = 8 * count * self.spatial_in
            parts.append((2 * k, count, Plan(clips, segs, first, rows, "cxypq", nest, "cxy")))
            first += rows
        return parts


EARLY = (("cpqyx", "cyxpq"), ("cypqx", "cyxpq"), ("cyxpq", "cxpqy"), ("cyxpq", "cxypq"))
MIDDLE = (("cypxq", "cyxpq"), ("cxpqy", "cypxq"), ("cpyxq", "cpyxq"), ("cpyxq", "cxpqy"))
SPATIAL = ("cxypq", "cyxpq", "cypxq", "cpxyq", "cpqxy")
LATE = (("cxypq", "cxpqy"), ("cyxpq", "cyxpq"))
SLOTS = (
    (0, 1),
    (0, 1, 2),
    (2, 0, 1),
    (),
    (),
    (),
    (4, 5, 6, 7, 1, 2),
    (3, 0),
    (4, 5, 6, 7, 3, 1, 2),
    (0,),
    (),
    (),
    (3, 4, 0, 5, 6, 7, 1, 2, 0),
    (),
    (4, 13, 1, 14),
    (3, 8, 5, 6, 2),
    (4, 13, 9, 0, 7, 1, 2, 14),
    (3, 8, 10, 5, 6, 2),
    (4, 9, 0, 11, 1),
    (3, 4, 8, 10, 12),
    (3, 13, 8, 0, 5, 6, 7, 11, 1, 2, 14),
    (),
    (3, 4, 9, 10, 5, 13, 8, 9, 10, 6, 7, 12, 4, 2, 11, 7, 0, 5, 14, 13, 11, 8, 0, 4, 1, 3, 7, 9, 10, 2, 1, 6, 5, 14, 12, 8, 3, 2, 13, 12, 10, 9, 11, 13, 3, 4, 6, 5, 7, 12, 14, 4, 11, 14, 13, 10, 6, 8, 7, 14, 5, 9, 8, 12, 13, 5, 6, 11, 14, 6, 10, 7, 12, 13, 10, 7, 14, 9, 11, 9, 13, 12, 11, 14, 13, 12, 14),
)


def block_kernel(clips, segs, grid, names, sc_names, *refs):
    R = SimpleNamespace(**dict(zip(names, refs[: len(names)])))
    S = SimpleNamespace(**dict(zip(sc_names, refs[len(names) :])))
    rows, wide = S.x.shape
    mid, red = S.f1.shape[1], S.sq.shape[1]
    cells = grid * grid
    images = rows // cells
    lay = Layout(wide, mid, red)
    blocks = range(0, rows, BLOCK)
    ntap = len(TAPS)
    place = Place(clips, segs)
    local, sends, recvs = Sems(S.local), Sems(S.send), Sems(S.recv)

    wfine = S.wfc.at[pl.ds(0, ntap * red)]
    wcoarse = S.wfc.at[pl.ds(ntap * red, ntap * red)]

    def load(src, dst):
        copy = pltpu.make_async_copy(src, dst, local.take())
        copy.start()
        return copy

    x_load, wr_load = load(R.x, S.x), load(R.wr, S.wr)

    def other_loads():
        return SimpleNamespace(
            frames=load(R.frames, S.frames),
            ws=load(R.ws, S.ws),
            we=load(R.we, S.we),
            wq=load(R.wq, S.wq),
            wf=load(R.wf, wfine),
            wc=load(R.wc, wcoarse),
            wx=load(R.wx, S.wx),
            cot=load(R.cot, S.cot),
            stem_cot=load(R.stem_cot, S.stem_cot),
        )

    place.greet()

    groups = R.groups
    total_groups = groups.shape[0]

    def side_of(group):
        return 5 + 2 * group - group // 2

    def area(k, acc):
        side = side_of(groups[k])
        return acc + side * side

    cell = lax.broadcasted_iota(jnp.int32, (cells, LANES), 0)
    ci, cj = cell >> log2(grid), cell & (grid - 1)
    for img in range(images):
        side = side_of(groups[place.clip * images + img])
        S.mask[img * cells : (img + 1) * cells] = jnp.where((ci < side) & (cj < side), 1.0, 0.0).astype(F32)
    half = grid // 2
    mask, tap, tap_small = S.mask, S.tap, S.tap_small

    def parent_of(row):
        i, j = (row & (cells - 1)) >> log2(grid), row & (grid - 1)
        return (row >> log2(cells)) * half * half + (i >> 1) * half + (j >> 1)

    def prepare():
        small = cell & (half * half - 1)
        si, sj = small >> log2(half), small & (half - 1)
        for t, (di, dj) in enumerate(TAPS):
            ok = (ci + di >= 0) & (ci + di < grid) & (cj + dj >= 0) & (cj + dj < grid)
            tap[t] = jnp.where(ok, 1.0, 0.0).astype(F32)
            ok = (si + di >= 0) & (si + di < half) & (sj + dj >= 0) & (sj + dj < half)
            tap_small[t] = jnp.where(ok, 1.0, 0.0).astype(F32)
        shape = (images * half * half, rows)
        here = lax.broadcasted_iota(jnp.int32, shape, 0) == parent_of(lax.broadcasted_iota(jnp.int32, shape, 1))
        S.pool[...] = jnp.where(here, 0.25, 0.0).astype(BF16)
        here = lax.broadcasted_iota(jnp.int32, shape[::-1], 1) == parent_of(
            lax.broadcasted_iota(jnp.int32, shape[::-1], 0)
        )
        S.up[...] = jnp.where(here, 1.0, 0.0).astype(BF16)
        for ref in (S.tmp, S.z, S.tmp_small, S.h1_all):
            ref[:PAD] = jnp.zeros((PAD, ref.shape[1]), F32)
            ref[ref.shape[0] - PAD :] = jnp.zeros((PAD, ref.shape[1]), F32)
        count = lax.fori_loop(0, total_groups, area, jnp.int32(0)) * segs
        return 1.0 / jnp.full((1, LANES), count.astype(F32), F32)

    grads = S.grads

    near = [S.near0, S.near1, S.near2, S.near3, S.near4, S.near5]
    far = [S.far0, S.far1, S.far2, S.far3, S.far4, S.far5]
    stats = [S.res0, S.res1, S.res2, S.res3, S.res4, S.res5]

    def sums(k):
        return Sums(place, near[k], far[k], stats[k], sends, recvs)

    all_sums = [sums(k) for k in range(6)]

    def local_moments(src, width, ar, masked):
        def body(at, j):
            s = q = jnp.zeros((8, LANES), F32)
            for r in blocks:
                v = src[r : r + BLOCK, lanes(at)]
                w = v * mask[r : r + BLOCK] if masked else v
                s, q = s + fold(w), q + fold(w * v)
            ar.put(0, at, total_of(s))
            ar.put(1, at, total_of(q))

        columns(width, body)

    gains = [R.gain_one, R.gain_two, R.gain_three]
    biases = [R.bias_one, R.bias_two, R.bias_three]

    def affine(k, at):
        stat = stats[k]
        mean = stat[0:1, lanes(at)] * inv
        spread = stat[1:2, lanes(at)] * inv - mean * mean
        root = lax.rsqrt(spread + 1e-05)
        scale = root * gains[k][0:1, lanes(at)]
        return scale, biases[k][0:1, lanes(at)] - mean * scale, mean, root

    def spread_taps(tmp, masks, per, count, stride, store):
        for t, (di, dj) in enumerate(TAPS):
            off = PAD + di * stride + dj
            for r in range(0, count, BLOCK):
                v = tmp[r + off : r + off + BLOCK, :] * masks[t, r % per : r % per + BLOCK]
                store(t, r, v)

    def gather_taps(z, width, masks, per, r, stride, at):
        acc = None
        for t, (di, dj) in enumerate(TAPS):
            off = PAD + r + di * stride + dj
            v = z[off : off + BLOCK, lanes((ntap - 1 - t) * width + at)] * masks[t, r % per : r % per + BLOCK]
            acc = v if acc is None else acc + v
        return acc

    stem = Stem(R, S, images, S.frames.shape[1], float(S.stem_cot.shape[0] * clips * segs))
    sems = (local, sends, recvs)
    jobs, land = [], 0
    for plan in [plan for group in lay.plans(clips, segs) for plan in group]:
        job = Job(place, plan, (grads, S.landing, R.packed), plan.first, land, sems)
        land = job.land_end
        jobs.append(job)
    shared, land, held = [], 0, 0
    for _, _, plan in lay.shared_plans(clips, segs):
        job = Job(place, plan, (S.shares, S.share_landing, R.shared), held, land, sems)
        land, held = job.land_end, held + plan.block
        shared.append(job)
    jobs = jobs[:8] + shared + jobs[8:]
    slots = iter(SLOTS)

    def advance():
        for k in next(slots):
            jobs[k].step()

    def plane_send(view, slots):
        me, copies = place.plane_me, []
        for k in range(1, place.plane):
            t = lax.rem(me + k, place.plane)
            copies.append(remote(view(t), slots.at[me], sends, recvs, place.plane_device(t)))
        own = pltpu.make_async_copy(view(me), slots.at[me], local.take())
        own.start()
        return copies + [own]

    x_load.wait()
    x = S.x

    def cut(at, j):
        for r in blocks:
            x[r : r + BLOCK, lanes(at)] = (x[r : r + BLOCK, lanes(at)].astype(F32) * mask[r : r + BLOCK]).astype(BF16)

    columns(wide, cut)

    wr_load.wait()
    S.f1[...] = dot(x[...], S.wr[...])
    local_moments(S.f1, mid, all_sums[0], False)
    place.greeted()
    all_sums[0].start()
    loads = other_loads()
    inv = prepare()
    stem.tables()
    all_sums[0].middle()
    loads.frames.wait()
    stem.patches()
    all_sums[0].finish()

    def hidden_one(at, j):
        scale, shift, _, _ = affine(0, at)
        for r in blocks:
            y = S.f1[r : r + BLOCK, lanes(at)] * scale + shift
            S.tmp[PAD + r : PAD + r + BLOCK, :] = y * jax.nn.sigmoid(y) * mask[r : r + BLOCK]

        def store(t, r, v):
            S.col[r : r + BLOCK, lanes(pl.multiple_of(t * mid + at, LANES))] = v.astype(BF16)

        spread_taps(S.tmp, tap, cells, rows, grid, store)

    columns(mid, hidden_one)
    me, centre = place.plane_me, ntap // 2 * mid
    sibling = me + 1 - 2 * lax.rem(me, 2)

    def half_inputs(t):
        start = pl.multiple_of(centre + t // 4 * lay.spatial_in, lay.spatial_in)
        return S.col.at[:, pl.ds(start, lay.spatial_in)]

    def same_core(k):
        return lax.rem(me // 2 + k, 4) * 2 + lax.rem(me, 2)

    def h1_send():
        copies = [
            remote(half_inputs(same_core(k)), S.h1_in.at[me], sends, recvs, place.plane_device(same_core(k)))
            for k in range(1, 4)
        ]
        own = pltpu.make_async_copy(half_inputs(me), S.h1_in.at[me], local.take())
        own.start()
        return copies, [remote(half_inputs(me), S.h1_in.at[me], sends, recvs, place.plane_device(sibling)), own]

    def h1_relay(copies):
        more = []
        for copy in copies:
            copy.wait()
        for k in range(1, 4):
            block = S.h1_in.at[same_core(k)]
            more.append(remote(block, block, sends, recvs, place.plane_device(sibling)))
        return more
    loads.ws.wait()
    S.f2[...] = dot(S.col[...], S.ws[...])
    local_moments(S.f2, mid, all_sums[1], True)
    all_sums[1].start()
    stem.forward(all_sums[2], wide)
    all_sums[1].middle()
    h1_far, h1_copies = h1_send()
    all_sums[1].finish()

    def hidden_two(at, j):
        scale, shift, _, _ = affine(1, at)
        for r in blocks:
            y = S.f2[r : r + BLOCK, lanes(at)] * scale + shift
            S.h2[r : r + BLOCK, lanes(at)] = (y * jax.nn.sigmoid(y) * mask[r : r + BLOCK]).astype(BF16)

    columns(mid, hidden_two)
    loads.we.wait()
    S.f3[...] = dot(S.h2[...], S.we[...])
    local_moments(S.f3, wide, all_sums[2], False)
    all_sums[2].start()
    all_sums[2].middle()
    h1_copies = h1_copies + h1_relay(h1_far)
    all_sums[2].finish()

    def branch_low(at, j):
        scale, shift, _, _ = affine(2, at)
        for r in blocks:
            y = (S.f3[r : r + BLOCK, lanes(at)] * scale + shift) * mask[r : r + BLOCK]
            S.branch[r : r + BLOCK, lanes(at)] = y.astype(BF16)

    columns(wide, branch_low)
    loads.wq.wait()
    S.sq[...] = dot(S.branch[...], S.wq[...]).astype(BF16)

    def swap(mine, slots):
        after, before = lax.rem(place.seg + 1, segs), lax.rem(place.seg + segs - 1, segs)
        copies = [
            remote(mine, slots.at[0], sends, recvs, (place.clip, after)),
            remote(mine, slots.at[1], sends, recvs, (place.clip, before)),
        ]
        return copies

    has_before = jnp.where(jnp.full((1, LANES), place.seg, jnp.int32) > 0, 1.0, 0.0).astype(F32)
    has_after = jnp.where(jnp.full((1, LANES), place.seg, jnp.int32) < segs - 1, 1.0, 0.0).astype(F32)
    copies = swap(S.sq, S.halo)
    loads.stem_cot.wait()
    stem.rear(stats[2][:, lanes(wide)], all_sums[3], wide)
    stem_copy = pltpu.make_async_copy(S.stem_cot, R.stem_out, local.take())
    stem_copy.start()
    for copy in copies:
        copy.wait()

    diffs = S.diffs
    for r in blocks:
        own = S.sq[r : r + BLOCK].astype(F32)
        later = S.halo[1, r : r + BLOCK].astype(F32) * has_after - own
        earlier = S.halo[0, r : r + BLOCK].astype(F32) * has_before - own
        diffs[r : r + BLOCK, lanes(0, red)] = later.astype(BF16)
        diffs[r : r + BLOCK, lanes(red, red)] = earlier.astype(BF16)
        S.tmp[PAD + r : PAD + r + BLOCK, :] = later.astype(BF16).astype(F32) + earlier.astype(BF16).astype(F32)

    def store_fine(t, r, v):
        S.cc[r : r + BLOCK, lanes(t * red, red)] = v.astype(BF16)

    spread_taps(S.tmp, tap, cells, rows, grid, store_fine)
    pooled = dot(S.pool[...], diffs[...]).astype(BF16).astype(F32)
    small_rows = pooled.shape[0]
    S.tmp_small[PAD : PAD + small_rows, :] = pooled[:, :red] + pooled[:, red:]

    def store_small(t, r, v):
        S.small_col[r : r + BLOCK, lanes(t * red, red)] = v.astype(BF16)

    spread_taps(S.tmp_small, tap_small, cells, small_rows, half, store_small)
    S.cc[:, lanes(ntap * red, ntap * red)] = dot(S.up[...], S.small_col[...]).astype(BF16)
    loads.wf.wait()
    loads.wc.wait()
    S.mo[...] = dot(S.cc[...], S.wfc[...]).astype(BF16)
    loads.wx.wait()
    S.gb[...] = dot(S.mo[...], S.wx[...])
    loads.cot.wait()

    def ends(at, j):
        scale, shift, _, _ = affine(2, at)
        for r in blocks:
            here = (slice(r, r + BLOCK), lanes(at))
            m = mask[r : r + BLOCK]
            branch = (S.f3[here] * scale + shift) * m
            gate = jax.nn.sigmoid(S.gb[here])
            z = x[here].astype(F32) + branch * (1.0 + gate)
            s = jax.nn.sigmoid(z)
            out = z * s
            gz = S.cot[here].astype(F32) * m * (s + out * (1.0 - s))
            S.cot[here] = (out * m).astype(BF16)
            S.gi[here] = gz
            S.gb[here] = gz * (1.0 + gate)
            S.g3[here] = (gz * branch * gate * (1.0 - gate)).astype(BF16)

    columns(wide, ends)
    out_copy = pltpu.make_async_copy(S.cot, R.block_out, local.take())
    out_copy.start()

    S.gm[...] = dot_bt(S.g3[...], S.wx[...]).astype(BF16)
    zf = dot_bt(S.gm[...], S.wfc[0 : ntap * red, :])
    S.z[PAD : PAD + rows, lanes(0, ntap * red)] = zf
    gmc = lax.dot_general(S.up[...], S.gm[...], (((0,), (0,)), ((), ())), preferred_element_type=F32).astype(BF16)
    S.z[PAD : PAD + small_rows, lanes(ntap * red, ntap * red)] = dot_bt(gmc, S.wfc[ntap * red :, :])
    S.z[PAD + small_rows : PAD + small_rows + PAD, lanes(ntap * red, ntap * red)] = jnp.zeros((PAD, ntap * red), F32)
    coarse = gather_taps(S.z, red, tap_small, cells, 0, half, ntap * red)
    coarse = dot_at(S.pool[...], coarse.astype(BF16))
    for r in blocks:
        gd = gather_taps(S.z, red, tap, cells, r, grid, 0) + coarse[r : r + BLOCK]
        S.gd[r : r + BLOCK] = gd
        S.gd_low[r : r + BLOCK] = gd.astype(BF16)
    copies = swap(S.gd_low, S.halo2)
    last = lay.squeeze - red
    grads[last : lay.squeeze] = jnp.zeros((red, mid), BF16)
    for b in range(wide // mid):
        grads[lay.excite + b * red : lay.excite + (b + 1) * red] = dot_at(
            S.mo[...], S.g3[:, lanes(b * mid, mid)]
        ).astype(BF16)
    for t in range(2 * ntap):
        top = lay.scales + t // lay.scale_taps * red
        grads[top : top + red, lanes(t % lay.scale_taps * red, red)] = dot_at(
            S.cc[:, lanes(t * red, red)], S.gm[...]
        ).astype(BF16)
    advance()
    for copy in copies:
        copy.wait()
    for r in blocks:
        g = S.halo2[0, r : r + BLOCK].astype(F32) * has_before + S.halo2[1, r : r + BLOCK].astype(F32) * has_after
        S.gsq[r : r + BLOCK] = (g - 2.0 * S.gd[r : r + BLOCK]).astype(BF16)
    S.z[PAD : PAD + rows, lanes(0, wide)] = dot_bt(S.gsq[...], S.wq[...])

    def branch_grad(at, j):
        _, _, mean, root = affine(2, at)
        s = q = jnp.zeros((8, LANES), F32)
        for r in blocks:
            here = (slice(r, r + BLOCK), lanes(at))
            g = (S.gb[here] + S.z[PAD + r : PAD + r + BLOCK, lanes(at)]) * mask[r : r + BLOCK]
            S.gb[here] = g
            s, q = s + fold(g), q + fold(g * ((S.f3[here] - mean) * root))
        all_sums[3].put(0, at, total_of(s))
        all_sums[3].put(1, at, total_of(q))

    columns(wide, branch_grad)
    all_sums[3].start()
    for b in range(mid // red):
        grads[lay.squeeze : lay.squeeze + mid, lanes(b * red, red)] = dot_at(
            S.branch[:, lanes(b * mid, mid)], S.gsq[...]
        ).astype(BF16)
    advance()
    all_sums[3].middle()
    advance()
    for copy in h1_copies:
        copy.wait()

    def widen(k, carry):
        for r in blocks:
            start = pl.multiple_of(k * rows + r, BLOCK)
            S.h1_all[pl.ds(PAD + start, BLOCK)] = S.h1_in[k, r : r + BLOCK].astype(F32)
        return carry

    lax.fori_loop(0, place.plane, widen, 0)
    all_sums[3].finish()
    advance()

    def through(k, back, src, given, dst, width):
        stat = stats[back]

        def body(at, j):
            scale, _, mean, root = affine(k, at)
            gb, gg = stat[0:1, lanes(at)] * inv, stat[1:2, lanes(at)] * inv
            for r in blocks:
                here = (slice(r, r + BLOCK), lanes(at))
                hat = (src[here] - mean) * root
                dst[here] = (scale * (given[here] - (gb + hat * gg) * mask[r : r + BLOCK])).astype(BF16)

        columns(width, body)

    def act_back(k, ar, src, value, at):
        scale, shift, mean, root = affine(k, at)
        s = q = jnp.zeros((8, LANES), F32)
        for r in blocks:
            here = (slice(r, r + BLOCK), lanes(at))
            a = src[here]
            y = a * scale + shift
            sg = jax.nn.sigmoid(y)
            g = value(r) * mask[r : r + BLOCK] * (sg * (1.0 + y * (1.0 - sg)))
            S.gy[here] = g
            s, q = s + fold(g), q + fold(g * ((a - mean) * root))
        ar.put(0, at, total_of(s))
        ar.put(1, at, total_of(q))

    through(2, 3, S.f3, S.gb, S.g3, wide)
    advance()
    S.gh[...] = dot_bt(S.g3[...], S.we[...])

    def back_two(at, j):
        act_back(1, all_sums[4], S.f2, lambda r: S.gh[r : r + BLOCK, lanes(at)], at)

    columns(mid, back_two)
    advance()
    all_sums[4].start()
    for b in range(wide // mid):
        grads[lay.expand + b * mid : lay.expand + (b + 1) * mid] = dot_at(
            S.h2[...], S.g3[:, lanes(b * mid, mid)]
        ).astype(BF16)
    advance()
    stem.back(stats[3][:, lanes(wide)], lay.stem)
    advance()
    all_sums[4].middle()
    advance()
    all_sums[4].finish()
    advance()
    through(1, 4, S.f2, S.gy, S.g2, mid)

    def output_quarter(ref):
        return lambda t: ref.at[:, pl.ds(pl.multiple_of(lax.rem(t, 4) * LANES, LANES), LANES)]
    S.z[PAD : PAD + rows, :] = dot_bt(S.g2[...], S.ws[...])
    advance()

    def back_one(at, j):
        act_back(
            0,
            all_sums[5],
            S.f1,
            lambda r: gather_taps_at(S.z, mid, tap, cells, r, grid, at),
            at,
        )

    def gather_taps_at(z, width, masks, per, r, stride, at):
        acc = None
        for t, (di, dj) in enumerate(TAPS):
            off = PAD + r + di * stride + dj
            start = pl.multiple_of((ntap - 1 - t) * width + at, LANES)
            v = z[off : off + BLOCK, lanes(start)] * masks[t, r % per : r % per + BLOCK]
            acc = v if acc is None else acc + v
        return acc

    columns(mid, back_one)
    all_sums[5].start()

    g_copies = plane_send(output_quarter(S.g2), S.g2_in)
    advance()
    all_sums[5].middle()
    advance()
    all_sums[5].finish()
    advance()
    through(0, 5, S.f1, S.gy, S.g1, mid)
    for b in range(wide // mid):
        grads[lay.reduce + b * mid : lay.reduce + (b + 1) * mid] = dot_at(
            x[:, lanes(b * mid, mid)], S.g1[...]
        ).astype(BF16)
    advance()
    for copy in g_copies:
        copy.wait()
    all_rows = place.plane * rows
    g_all = S.g2_in[...].reshape(all_rows, LANES)
    for t, (di, dj) in enumerate(TAPS):
        off = PAD + di * grid + dj

        def shifted(k, carry):
            for r in range(0, rows, BLOCK):
                start = pl.multiple_of(k * rows + r, BLOCK)
                for at in range(0, lay.spatial_in, LANES):
                    v = S.h1_all[pl.ds(start, BLOCK + 2 * PAD), at : at + LANES][off : off + BLOCK]
                    v = v * tap[t, r % cells : r % cells + BLOCK]
                    S.h1_tap[pl.ds(start, BLOCK), at : at + LANES] = v.astype(BF16)
            return carry

        lax.fori_loop(0, place.plane, shifted, 0)
        block = dot_at(g_all, S.h1_tap[...])
        S.shares[t * lay.spatial_in : (t + 1) * lay.spatial_in] = block.T.astype(BF16)
        if t % 2 == 1 or t == ntap - 1:
            advance()
    S.z[PAD : PAD + rows, lanes(0, wide)] = dot_bt(S.g1[...], S.wr[...])
    advance()

    def features_grad(at, j):
        for r in blocks:
            here = (slice(r, r + BLOCK), lanes(at))
            g = (S.gi[here] + S.z[PAD + r : PAD + r + BLOCK, lanes(at)]) * mask[r : r + BLOCK]
            S.g3[here] = g.astype(BF16)

    columns(wide, features_grad)
    feat_copy = pltpu.make_async_copy(S.g3, R.grad_features, local.take())
    feat_copy.start()

    advance()
    advance()
    while jobs:
        jobs = [job for job in jobs if job.step() < 4]
    small = R.sums
    at = 0
    for k, width in ((5, mid), (4, mid), (3, wide + LANES)):
        small[:, lanes(at, width)] = stats[k][...]
        at += width
    stem_copy.wait()
    out_copy.wait()
    feat_copy.wait()


def block(clips, segs, feats, cot, res_group, deep, stem):
    (w_reduce, gain_one, bias_one, w_spatial, gain_two, bias_two, w_expand, gain_three, bias_three) = deep[:9]
    w_squeeze, w_fine, w_coarse, w_excite = deep[9:]
    images, _, grid, _, wide = feats.shape
    rows = images * grid * grid
    mid, red = w_reduce.shape[1], w_squeeze.shape[1]
    taps = len(TAPS)
    lay = Layout(wide, mid, red)
    small_rows = rows // 4
    frames, stem_cot, stem_weight, diff_weight, stem_gain, stem_bias = stem
    count, side, colours = frames.shape[2], frames.shape[3], frames.shape[5]
    kernel, channels = stem_weight.shape[0], stem_weight.shape[3]
    stem_cells = images * (side // 2) ** 2
    stem_rows = images * side // 2
    stem_lanes = side // 2 * channels
    depth = colours * side * 8 + 3 * 256
    inputs = dict(
        x=feats.reshape(rows, wide),
        cot=cot.reshape(rows, wide),
        groups=res_group,
        wr=w_reduce,
        ws=w_spatial.reshape(taps * mid, mid),
        we=w_expand,
        wq=w_squeeze,
        wf=w_fine.reshape(taps * red, red),
        wc=w_coarse.reshape(taps * red, red),
        wx=w_excite,
        gain_one=gain_one.reshape(1, mid),
        bias_one=bias_one.reshape(1, mid),
        gain_two=gain_two.reshape(1, mid),
        bias_two=bias_two.reshape(1, mid),
        gain_three=gain_three.reshape(1, wide),
        bias_three=bias_three.reshape(1, wide),
        frames=jnp.transpose(frames, (0, 1, 2, 5, 3, 4)).reshape(images * count * colours, side, side),
        stem_cot=stem_cot.reshape(stem_cells, channels),
        stem_w=jnp.transpose(stem_weight, (0, 2, 1, 3)).reshape(kernel * colours, kernel, channels),
        diff_w=diff_weight.reshape(len(TAPS), diff_weight.shape[2], channels),
        stem_gain=stem_gain.reshape(1, channels),
        stem_bias=stem_bias.reshape(1, channels),
    )
    outputs = dict(
        block_out=jax.ShapeDtypeStruct((rows, wide), BF16),
        grad_features=jax.ShapeDtypeStruct((rows, wide), BF16),
        packed=jax.ShapeDtypeStruct((lay.rows, mid), BF16),
        shared=jax.ShapeDtypeStruct((lay.share_rows, LANES), BF16),
        sums=jax.ShapeDtypeStruct((2, 2 * mid + wide + LANES), F32),
        stem_out=jax.ShapeDtypeStruct((stem_cells, channels), BF16),
    )

    def spec(name):
        if name == "groups":
            return pl.BlockSpec(memory_space=pltpu.SMEM)
        if inputs.get(name, frames).size < 1 << 15 or name == "sums":
            return pl.BlockSpec(memory_space=pltpu.VMEM)
        return pl.BlockSpec(memory_space=pl.ANY)

    plans = [plan for group in lay.plans(clips, segs) for plan in group]
    shared = [plan for _, _, plan in lay.shared_plans(clips, segs)]
    land = sum(plan.landing_rows for plan in plans)
    share_land = sum(plan.landing_rows for plan in shared)
    near, far = 2 * segs, clips // 2
    remote_count = sum(plan.transfers for plan in plans + shared) + 6 * (near + far) + 48
    v = pltpu.VMEM
    scratch = dict(
        x=v((rows, wide), BF16),
        cot=v((rows, wide), BF16),
        wr=v((wide, mid), BF16),
        ws=v((taps * mid, mid), BF16),
        we=v((mid, wide), BF16),
        wq=v((wide, red), BF16),
        wfc=v((2 * taps * red, red), BF16),
        wx=v((red, wide), BF16),
        mask=v((rows, LANES), F32),
        tap=v((taps, grid * grid, LANES), F32),
        tap_small=v((taps, grid * grid, LANES), F32),
        pool=v((small_rows, rows), BF16),
        up=v((rows, small_rows), BF16),
        tmp=v((rows + 2 * PAD, LANES), F32),
        tmp_small=v((small_rows + 2 * PAD, LANES), F32),
        small_col=v((small_rows, taps * red), BF16),
        f1=v((rows, mid), F32),
        f2=v((rows, mid), F32),
        f3=v((rows, wide), F32),
        col=v((rows, taps * mid), BF16),
        h2=v((rows, mid), BF16),
        branch=v((rows, wide), BF16),
        sq=v((rows, red), BF16),
        halo=v((2, rows, red), BF16),
        halo2=v((2, rows, red), BF16),
        diffs=v((rows, 2 * red), BF16),
        cc=v((rows, 2 * taps * red), BF16),
        mo=v((rows, red), BF16),
        gm=v((rows, red), BF16),
        gd=v((rows, red), F32),
        gd_low=v((rows, red), BF16),
        gsq=v((rows, red), BF16),
        gb=v((rows, wide), F32),
        gi=v((rows, wide), F32),
        g3=v((rows, wide), BF16),
        gh=v((rows, mid), F32),
        gy=v((rows, mid), F32),
        g2=v((rows, mid), BF16),
        g1=v((rows, mid), BF16),
        z=v((rows + 2 * PAD, taps * mid), F32),
        grads=v((lay.rows, mid), BF16),
        landing=v((land, mid), BF16),
        shares=v((lay.spatial_block, LANES), BF16),
        share_landing=v((share_land, LANES), BF16),
        h1_in=v((8, rows, lay.spatial_in), BF16),
        h1_all=v((8 * rows + 2 * PAD, lay.spatial_in), F32),
        h1_tap=v((8 * rows, lay.spatial_in), BF16),
        g2_in=v((8, rows, LANES), BF16),
        frames=v((images * count * colours, side, side), BF16),
        stem_cot=v((stem_cells, channels), BF16),
        stem_wide=v((stem_cells, LANES), F32),
        stem_stat=v((2, LANES), F32),
        padded=v((images * (side + 8), LANES), F32),
        stem_taps=v((stem_rows, 512), F32),
        columns=v((2, images * side, LANES), F32),
        xx=v((stem_rows, depth), BF16),
        pre=v((stem_rows, stem_lanes), F32),
        gpre=v((stem_rows, stem_lanes), F32),
        prod=v((depth, LANES), F32),
        bands=v((240, LANES), F32),
        spots=v((144, LANES), F32),
        wt=v((192, LANES), F32),
        wd=v((144, LANES), F32),
    )
    for k, width in enumerate((mid, mid, wide + LANES, wide + LANES, mid, mid)):
        scratch[f"near{k}"] = v((near, 2, width), F32)
        scratch[f"far{k}"] = v((far, 2, width), F32)
        scratch[f"res{k}"] = v((2, width), F32)
    scratch.update(
        local=pltpu.SemaphoreType.DMA((32,)),
        send=pltpu.SemaphoreType.DMA((remote_count,)),
        recv=pltpu.SemaphoreType.DMA((remote_count,)),
    )
    names = list(inputs) + list(outputs)
    result = pl.pallas_call(
        partial(block_kernel, clips, segs, grid, names, list(scratch)),
        out_shape=list(outputs.values()),
        in_specs=[spec(name) for name in inputs],
        out_specs=[spec(name) for name in outputs],
        scratch_shapes=list(scratch.values()),
        compiler_params=pltpu.CompilerParams(
            collective_id=0, has_side_effects=True, vmem_limit_bytes=VMEM_LIMIT
        ),
        name="block",
    )(*inputs.values())
    return result


VMEM_LIMIT = 62 << 20


AHEAD = 16


def spread_kernel(lay, plans, shared_plans, mid, red, wide, ins, outs, names, *refs):
    R = SimpleNamespace(**dict(zip(ins + outs + names, refs)))
    taps = len(TAPS)
    copies, out = [], []

    def read(src, dst):
        copies.append(pltpu.make_async_copy(src, dst, R.reads.at[len(copies)]))

    arrived = iter(range(len(plans) + len(shared_plans) + 3))

    def arrive():
        k = next(arrived)
        if k == 0:
            for copy in copies[:AHEAD]:
                copy.start()
        copies[k].wait()
        if k + AHEAD < len(copies):
            copies[k + AHEAD].start()

    def write(src, dst):
        copy = pltpu.make_async_copy(src, dst, R.writes.at[len(out)])
        copy.start()
        out.append(copy)

    for plan in plans[:8] + [plan for _, _, plan in shared_plans] + plans[8:]:
        here = pl.ds(plan.first, plan.rows)
        if plan in plans:
            read(R.packed.at[here], R.held.at[here])
        else:
            read(R.shared.at[here], R.shares.at[here])
    passed = [
        (R.block_out, R.block_held, R.out_block),
        (R.grad_features, R.features_held, R.out_features),
        (R.stem_out, R.stem_held, R.out_stem),
    ]
    for src, here, _ in passed:
        read(src, here)
    at = 0
    for bias, gain in (
        (R.bias_one, R.gain_one),
        (R.bias_two, R.gain_two),
        (R.bias_three, R.gain_three),
        (R.stem_bias, R.stem_gain),
    ):
        width = bias.shape[1]
        bias[...] = R.sums[0:1, at : at + width]
        gain[...] = R.sums[1:2, at : at + width]
        at += width
    full = R.full

    def wait_and_convert(plan):
        arrive()

        def convert(values):
            src = plan.packed_at(values)
            dst = plan.first + plan.summed_at(values)
            for r in range(0, plan.piece, 16):
                here = pl.ds(pl.multiple_of(dst + r, 16), 16)
                full[here] = R.held[pl.ds(pl.multiple_of(src + r, 16), 16)].astype(F32)

        plan.each_piece(convert)

    for plan in plans[:4]:
        wait_and_convert(plan)
    for b in range(wide // mid):
        write(full.at[pl.ds(lay.excite + b * red, red)], R.excite.at[:, pl.ds(b * mid, mid)])
    for t in range(2 * taps):
        top, at = lay.scales + t // lay.scale_taps * red, t % lay.scale_taps * red
        write(full.at[pl.ds(top, red), pl.ds(at, red)], (R.fine if t < taps else R.coarse).at[pl.ds(t % taps * red, red)])
    for b in range(mid // red):
        write(full.at[pl.ds(lay.squeeze, mid), pl.ds(b * red, red)], R.squeeze.at[pl.ds(b * mid, mid)])
    for k, plan in enumerate(plans[4:8]):
        wait_and_convert(plan)
        write(full.at[pl.ds(plan.first, mid)], R.expand.at[:, pl.ds(k * mid, mid)])

    for tap, count, plan in shared_plans:
        arrive()

        def convert(values):
            src, row = plan.packed_at(values), plan.summed_at(values)
            x, y, core = values[("clip", 1)], values[("seg", 2)], values[("seg", 1)]
            dst = (tap + row // lay.spatial_in) * mid + x * lay.spatial_in + row % lay.spatial_in
            at = lanes(pl.multiple_of((y * 2 + core) * LANES, LANES))
            for r in range(0, plan.piece, 16):
                here = pl.ds(pl.multiple_of(dst + r, 16), 16)
                R.full_spatial[here, at] = R.shares[pl.ds(pl.multiple_of(src + r, 16), 16)].astype(F32)

        plan.each_piece(convert)
        here = pl.ds(tap * mid, count * mid)
        write(R.full_spatial.at[here], R.spatial.at[here])
    for plan in plans[8:]:
        wait_and_convert(plan)
        write(full.at[pl.ds(plan.first, plan.rows)], R.reduce.at[pl.ds(plan.first - lay.reduce, plan.rows)])
    for _, here, dst in passed:
        arrive()
        write(here, dst)
    kernel, channels = R.stem_w.shape[1], R.stem_w.shape[2]
    colours = R.stem_w.shape[0] // kernel
    rest = R.rows.shape[0] - LANES
    R.rows[0:LANES] = full[lay.stem : lay.stem + LANES, lanes(0)]
    R.rows[LANES:] = full[lay.stem : lay.stem + rest, lanes(LANES)]
    for ki in range(kernel):
        for c in range(colours):
            part = R.rows[pl.ds(c * kernel * 8 + ki, kernel, stride=8), :]
            R.stem_w[ki * colours + c] = part[:, 0:channels]
    for t in range(taps):
        top, at = (lay.stem + t * 16, 2 * LANES) if t < 8 else (lay.stem, 3 * LANES)
        R.diff_w[t] = full[top : top + R.diff_w.shape[1], at : at + channels]
    for copy in out:
        copy.wait()


def spread(clips, segs, given, sizes):
    mid, red, wide, kernel, colours, channels, differences = sizes
    lay = Layout(wide, mid, red)
    taps = len(TAPS)
    plans = [plan for group in lay.plans(clips, segs) for plan in group]
    shared_plans = lay.shared_plans(clips, segs)

    def f32(*shape):
        return jax.ShapeDtypeStruct(shape, F32)

    outs = dict(
        out_block=given["block_out"],
        out_features=given["grad_features"],
        out_stem=given["stem_out"],
        reduce=f32(wide, mid),
        spatial=f32(taps * mid, mid),
        expand=f32(mid, wide),
        squeeze=f32(wide, red),
        fine=f32(taps * red, red),
        coarse=f32(taps * red, red),
        excite=f32(red, wide),
    )
    outs = {name: jax.ShapeDtypeStruct(out.shape, out.dtype) for name, out in outs.items()}
    small = dict(
        stem_w=f32(kernel * colours, kernel, channels),
        diff_w=f32(taps, differences, channels),
        bias_one=f32(1, mid),
        gain_one=f32(1, mid),
        bias_two=f32(1, mid),
        gain_two=f32(1, mid),
        bias_three=f32(1, wide),
        gain_three=f32(1, wide),
        stem_bias=f32(1, channels),
        stem_gain=f32(1, channels),
    )
    scratch = dict(
        held=pltpu.VMEM((lay.rows, mid), BF16),
        shares=pltpu.VMEM((lay.share_rows, LANES), BF16),
        full=pltpu.VMEM((lay.rows, mid), F32),
        full_spatial=pltpu.VMEM((taps * mid, mid), F32),
        rows=pltpu.VMEM((176, LANES), F32),
        block_held=pltpu.VMEM(given["block_out"].shape, BF16),
        features_held=pltpu.VMEM(given["grad_features"].shape, BF16),
        stem_held=pltpu.VMEM(given["stem_out"].shape, BF16),
        reads=pltpu.SemaphoreType.DMA((32,)),
        writes=pltpu.SemaphoreType.DMA((64,)),
    )
    here, anywhere = pl.BlockSpec(memory_space=pltpu.VMEM), pl.BlockSpec(memory_space=pl.ANY)
    names = list(outs) + list(small)
    results = pl.pallas_call(
        partial(
            spread_kernel, lay, plans, shared_plans, mid, red, wide, list(given), names, list(scratch)
        ),
        out_shape=list(outs.values()) + list(small.values()),
        in_specs=[here if array.size < 1 << 15 else anywhere for array in given.values()],
        out_specs=[anywhere] * len(outs) + [here] * len(small),
        scratch_shapes=list(scratch.values()),
        compiler_params=pltpu.CompilerParams(vmem_limit_bytes=VMEM_LIMIT),
        name="spread",
    )(*given.values())
    return SimpleNamespace(**dict(zip(names, results)))


def shards(
    frames,
    features,
    res_group,
    stem_weight,
    diff_weight,
    stem_gain,
    stem_bias,
    w_reduce,
    gain_one,
    bias_one,
    w_spatial,
    gain_two,
    bias_two,
    w_expand,
    gain_three,
    bias_three,
    w_squeeze,
    w_fine,
    w_coarse,
    w_excite,
    stem_cotangent,
    block_cotangent,
):
    clips, segs = lax.axis_size("clip"), lax.axis_size("seg")
    wide, mid, red = w_reduce.shape[0], w_reduce.shape[1], w_squeeze.shape[1]
    deep = (
        w_reduce, gain_one, bias_one, w_spatial, gain_two, bias_two, w_expand, gain_three, bias_three,
        w_squeeze, w_fine, w_coarse, w_excite,
    )
    stem = (frames, stem_cotangent, stem_weight, diff_weight, stem_gain, stem_bias)
    block_out, grad_feats, packed, shared, sums, stem_out = block(
        clips, segs, features, block_cotangent, res_group, deep, stem
    )
    kernel, colours, channels = stem_weight.shape[0], stem_weight.shape[2], stem_weight.shape[3]
    given = dict(
        packed=packed, shared=shared, sums=sums, block_out=block_out, grad_features=grad_feats, stem_out=stem_out
    )
    sizes = (mid, red, wide, kernel, colours, channels, diff_weight.shape[2])
    g = spread(clips, segs, given, sizes)
    g_stem_w = jnp.transpose(g.stem_w.reshape(kernel, colours, kernel, channels), (0, 2, 1, 3))
    return (
        g.out_stem.reshape(stem_cotangent.shape),
        g.out_block.reshape(features.shape),
        g.out_features.reshape(features.shape),
        g_stem_w,
        g.diff_w.reshape(diff_weight.shape),
        g.stem_gain.reshape(channels),
        g.stem_bias.reshape(channels),
        g.reduce,
        g.gain_one.reshape(mid),
        g.bias_one.reshape(mid),
        g.spatial.reshape(w_spatial.shape),
        g.gain_two.reshape(mid),
        g.bias_two.reshape(mid),
        g.expand,
        g.gain_three.reshape(wide),
        g.bias_three.reshape(wide),
        g.squeeze,
        g.fine.reshape(w_fine.shape),
        g.coarse.reshape(w_coarse.shape),
        g.excite,
    )


def solution(mesh):
    split = P("clip", "seg")
    whole = P()
    ins = (split, split) + (whole,) * 18 + (split, split)
    outs = (split,) * 3 + (whole,) * 17
    return jax.shard_map(shards, mesh=mesh, in_specs=ins, out_specs=outs, check_vma=False)
```

```python
from functools import partial
from types import SimpleNamespace

import jax
import jax.numpy as jnp
from jax import lax
from jax.experimental import pallas as pl
from jax.experimental.pallas import tpu as pltpu
from jax.sharding import PartitionSpec as P

MESH = pl.DeviceIdType.MESH
F32, BF16 = jnp.float32, jnp.bfloat16
LANES = 128
BLOCK = 64
PAD = 16
TAPS = [(di, dj) for di in (-1, 0, 1) for dj in (-1, 0, 1)]


def dot(a, b):
    return lax.dot_general(a, b, (((1,), (0,)), ((), ())), preferred_element_type=F32)


def dot_bt(a, b):
    return lax.dot_general(a, b, (((1,), (1,)), ((), ())), preferred_element_type=F32)


def dot_at(a, b):
    return lax.dot_general(a, b, (((0,), (0,)), ((), ())), preferred_element_type=F32)


def columns(total, body, step=LANES):
    def go(j, carry):
        body(pl.multiple_of(j * step, step), j)
        return carry

    lax.fori_loop(0, total // step, go, 0)


def log2(power):
    return power.bit_length() - 1


def lanes(start, size=LANES):
    return pl.ds(start, size)


def fold(block):
    return block.reshape(block.shape[0] // 8, 8, LANES).sum(axis=0)


def total_of(part):
    return jnp.sum(part, axis=0, keepdims=True)


class Sems:
    def __init__(self, ref):
        self.ref, self.used = ref, 0

    def take(self):
        self.used += 1
        return self.ref.at[self.used - 1]


class Place:
    def __init__(self, clips, segs):
        self.clips, self.segs = clips, segs
        self.clip, self.seg = lax.axis_index("clip"), lax.axis_index("seg")
        self.near = 2 * segs
        self.far = clips // 2
        self.near_me = lax.rem(self.clip, 2) * segs + self.seg
        self.far_me = self.clip // 2

        self.plane = 8
        self.plane_me = lax.rem(self.clip, 2) * 4 + lax.rem(self.seg, 4)

    def plane_device(self, t):
        return ((self.clip // 2) * 2 + t // 4, (self.seg // 4) * 4 + lax.rem(t, 4))

    def near_device(self, t):
        return ((self.clip // 2) * 2 + t // self.segs, lax.rem(t, self.segs))

    def far_device(self, t):
        return (t * 2 + lax.rem(self.clip, 2), self.seg)

    def bit(self, axis, stride):
        mine = self.seg if axis == "seg" else self.clip
        bit = lax.rem(mine // stride, 2)
        other = mine + stride * (1 - 2 * bit)
        return bit, (self.clip, other) if axis == "seg" else (other, self.seg)

    def greet(self):
        sem = pltpu.get_barrier_semaphore()

        def near(k, carry):
            pl.semaphore_signal(
                sem, inc=1, device_id=self.near_device(lax.rem(self.near_me + k, self.near)), device_id_type=MESH
            )
            return carry

        def far(k, carry):
            pl.semaphore_signal(
                sem, inc=1, device_id=self.far_device(lax.rem(self.far_me + k, self.far)), device_id_type=MESH
            )
            return carry

        lax.fori_loop(1, self.near, near, 0)
        lax.fori_loop(1, self.far, far, 0)

    def greeted(self):
        pl.semaphore_wait(pltpu.get_barrier_semaphore(), self.near + self.far - 2)


def remote(src, dst, sends, recvs, device):
    copy = pltpu.make_async_remote_copy(
        src_ref=src,
        dst_ref=dst,
        send_sem=sends.take(),
        recv_sem=recvs.take(),
        device_id=device,
        device_id_type=MESH,
    )
    copy.start()
    return copy


class Sums:
    def __init__(self, place, near_buf, far_buf, result, sends, recvs):
        self.place, self.near_buf, self.far_buf, self.result = place, near_buf, far_buf, result
        self.sends, self.recvs = sends, recvs

    def put(self, row, at, value):
        self.near_buf[self.place.near_me, row : row + 1, lanes(at, value.shape[1])] = value

    def _send(self, buf, me, count, device):
        mine = buf.at[me]
        return [remote(mine, mine, self.sends, self.recvs, device(lax.rem(me + k, count))) for k in range(1, count)]

    def _add(self, buf, count):
        value = buf[0]
        for k in range(1, count):
            value = value + buf[k]
        return value

    def start(self):
        p = self.place
        self.copies = self._send(self.near_buf, p.near_me, p.near, p.near_device)

    def middle(self):
        p, sent = self.place, self.copies
        for copy in sent:
            copy.wait_recv()
        self.far_buf[p.far_me] = self._add(self.near_buf, p.near)
        self.copies = self._send(self.far_buf, p.far_me, p.far, p.far_device)
        for copy in sent:
            copy.wait_send()

    def finish(self):
        for copy in self.copies:
            copy.wait_recv()
        self.result[...] = self._add(self.far_buf, self.place.far)
        for copy in self.copies:
            copy.wait_send()


def bit_order(clips, segs, letters):
    seg = [("seg", 1 << k) for k in range(segs.bit_length() - 1)]
    clip = [("clip", 1 << k) for k in range(clips.bit_length() - 1)]
    others = seg[2:] + clip[1:]
    named = dict(c=seg[:1], x=clip[:1], y=seg[1:2], p=others[:-1], q=others[-1:])
    return [bit for letter in letters for bit in named[letter]]


class Plan:
    def __init__(self, clips, segs, first, rows, letters, nest, skip=""):
        self.first, self.rows = first, rows
        skip = bit_order(clips, segs, skip)
        held = rows >> len(skip)
        self.block, self.sums, split = held, [], list(skip)
        for bit in bit_order(clips, segs, letters):
            if bit in skip:
                continue
            half = held // 2
            halved = held % 2 == 0 and half % 16 == 0
            held = half if halved else held
            self.sums.append((bit, held, halved))
            if halved:
                split.append(bit)
        self.piece = held
        self.places, size = [], rows
        for bit in bit_order(clips, segs, nest):
            if bit in split:
                size //= 2
                self.places.append((bit, size))
        self.landing_rows = sum(size for _, size, _ in self.sums)
        self.transfers = len(self.sums) + len(self.places)

    def each_piece(self, body):
        bits = [bit for bit, _ in self.places]
        outer, inner = bits[:-3], bits[-3:]

        def some(number, carry):
            values = {bit: lax.rem(number // (1 << k), 2) for k, bit in enumerate(outer)}
            for n in range(1 << len(inner)):
                values.update({bit: (n >> k) % 2 for k, bit in enumerate(inner)})
                body(values)
            return carry

        lax.fori_loop(0, 1 << len(outer), some, 0)

    def packed_at(self, values):
        return sum((values[bit] * size for bit, size in self.places), self.first)

    def summed_at(self, values):
        return sum((values[bit] * size for bit, size, halved in self.sums if halved), 0)


class Job:
    def __init__(self, place, plan, buffers, held, land, sems):
        self.grads, self.landing, self.packed = buffers
        self.local, self.sends, self.recvs = sems
        self.sums, self.places = [], []
        for (axis, stride), size, halved in plan.sums:
            bit, device = place.bit(axis, stride)
            away = held
            if halved:
                away = held + (1 - bit) * size
                held = held + bit * size
            self.sums.append((held, away, size, halved, device, land))
            land += size
        self.held, self.piece, self.land_end = held, plan.piece, land
        first = plan.first
        for (axis, stride), size in plan.places:
            bit, device = place.bit(axis, stride)
            first = first + bit * size
            self.places.append((first, size, device))
        self.first = first
        self.at = self.phase = 0

    def _rows(self, ref, start, size):
        if not isinstance(start, int):
            start = pl.multiple_of(start, 16)
        return ref.at[pl.ds(start, size)]

    def scatter_start(self):
        held, away, size, halved, device, land = self.sums[self.at]
        self.copy = remote(
            self._rows(self.grads, away, size), self._rows(self.landing, land, size), self.sends, self.recvs, device
        )

    def scatter_finish(self):
        held, away, size, halved, device, land = self.sums[self.at]
        sent = self.copy
        sent.wait_recv()
        if not halved:
            sent.wait_send()
        block = 32 if size % 32 == 0 else 16

        def add(k, carry):
            mine = pl.ds(pl.multiple_of(held + k * block, 16), block)
            theirs = pl.ds(pl.multiple_of(land + k * block, 16), block)
            self.grads[mine] = self.grads[mine] + self.landing[theirs]
            return carry

        lax.fori_loop(0, size // block, add, 0)
        self.at += 1
        return [sent] if halved else []

    def own_start(self):
        mine = self._rows(self.grads, self.held, self.piece)
        self.own = pltpu.make_async_copy(mine, self._rows(self.packed, self.first, self.piece), self.local.take())
        self.own.start()
        self.at = len(self.places)
        self.gather_start(mine)

    def gather_start(self, src=None):
        first, size, device = self.places[self.at - 1]
        mine = self._rows(self.packed, first, size)
        self.copy = remote(mine if src is None else src, mine, self.sends, self.recvs, device)

    def gather_finish(self):
        self.at -= 1
        sent = self.copy
        sent.wait_recv()
        if self.at == len(self.places) - 1:
            self.own.wait()
        return [sent]

    def step(self):
        sent = []
        if self.phase == 0:
            self.scatter_start()
            self.phase = 1
        elif self.phase == 1:
            sent = self.scatter_finish()
            if self.at < len(self.sums):
                self.scatter_start()
            else:
                self.own_start()
                self.phase = 2
        elif self.phase == 2:
            sent = self.gather_finish()
            if self.at > 0:
                self.gather_start()
            else:
                self.phase = 3
        for copy in sent:
            copy.wait_send()
        return self.phase


class Stem:
    KERNEL = 7
    COLOURS = 3

    def __init__(self, R, S, images, side, count):
        self.R, self.S, self.images, self.side, self.count = R, S, images, side, count
        self.cells = side // 2
        self.pairs = self.cells // 2
        self.band = side * 8
        self.fine = self.COLOURS * self.band
        self.half_rows = images * self.pairs
        self.depth = S.xx.shape[1]
        self.spread = (self.depth - self.fine) // 3

    def _table(self, q):
        per = self.S.grads.shape[1] // LANES
        table, top = self._part(q // per)
        return table, top, lanes(q % per * LANES)

    def _part(self, n):
        return (self.S.grads, n * self.depth) if n < 2 else (self.S.landing, 0)

    def tables(self):
        R, S = self.R, self.S
        wt, wd = S.wt, S.wd
        tall = 32

        def clear(k, carry):
            for n in range(3):
                table, top = self._part(n)
                table[pl.ds(pl.multiple_of(top + k * tall, tall), tall)] = jnp.zeros((tall, table.shape[1]), BF16)
            return carry

        lax.fori_loop(0, self.depth // tall, clear, 0)
        wt[...] = jnp.zeros(wt.shape, F32)
        wd[...] = jnp.zeros(wd.shape, F32)
        weights = R.stem_w[...].astype(F32)
        for ki in range(self.KERNEL):
            for c in range(self.COLOURS):
                for kj in range(self.KERNEL):
                    at = c * 64 + kj * 8 + ki
                    wt[at : at + 1, 0:64] = weights[ki * self.COLOURS + c, kj : kj + 1]
        for c in range(self.COLOURS):
            for p in range(5):
                block = jnp.zeros((16, LANES), F32)
                if p < 4:
                    block = block + wt[c * 64 + 16 * p : c * 64 + 16 * p + 16, :]
                if p > 0:
                    high = wt[c * 64 + 16 * p - 16 : c * 64 + 16 * p, :]
                    block = block + pltpu.roll(high, 64, 1)
                block = block.astype(BF16)
                for q in range(self.pairs):
                    j = 4 * q - 2 + 2 * p
                    if 0 <= j < self.side:
                        table, top, at = self._table(q)
                        top = top + c * self.band + j * 8
                        table[top : top + 16, at] = block
        weights = R.diff_w[...].astype(F32)
        for t in range(9):
            wd[t * 16 : t * 16 + weights.shape[1], 0:64] = weights[t]
        for ki in range(3):
            for kj in range(3):
                block = wd[(ki * 3 + kj) * 16 : (ki * 3 + kj) * 16 + 16, :]
                block = (block + pltpu.roll(block, 64, 1)).astype(BF16)
                for q in range(self.pairs):
                    j = q + kj - 1
                    if 0 <= j < self.pairs:
                        table, top, at = self._table(q)
                        top = top + self.fine + ki * self.spread + j * 16
                        table[top : top + 16, at] = block

    def patches(self):
        S, side, images = self.S, self.side, self.images
        frames, padded, taps, xx = S.frames, S.padded, S.stem_taps, S.xx
        tall = padded.shape[0] // images
        padded[...] = jnp.zeros(padded.shape, F32)
        taps[...] = jnp.zeros(taps.shape, F32)
        row = lax.broadcasted_iota(jnp.int32, (taps.shape[1], self.band), 0)
        lane = lax.broadcasted_iota(jnp.int32, (taps.shape[1], self.band), 1)
        place = jnp.where(row == (lane & 7) * 64 + (lane >> 3), 1.0, 0.0).astype(BF16)
        for c in range(self.COLOURS):
            for img in range(images):
                plane = frames[(img * 5 + 2) * self.COLOURS + c].astype(F32)
                padded[img * tall + 2 : img * tall + 2 + side, 0:side] = plane
            for ki in range(self.KERNEL):
                for parity in range(2):
                    for img in range(images):
                        start = img * tall + 2 * parity + ki
                        piece = padded[pl.ds(start, self.pairs, stride=4), 0:64]
                        top = parity * self.half_rows + img * self.pairs
                        taps[top : top + self.pairs, ki * 64 : ki * 64 + 64] = piece
            xx[:, lanes(c * self.band, self.band)] = dot(taps[...].astype(BF16), place).astype(BF16)
        row = lax.broadcasted_iota(jnp.int32, (side, self.spread), 0)
        lane = lax.broadcasted_iota(jnp.int32, (side, self.spread), 1)
        inside = (row >> 2) == (lane >> 4)
        channel = lane & 15
        total = None
        for f in range(5):
            for c in range(self.COLOURS):
                sign = jnp.zeros((side, self.spread), F32)
                if f > 0:
                    sign = sign + jnp.where(channel == (f - 1) * self.COLOURS + c, 1.0, 0.0)
                if f < 4:
                    sign = sign - jnp.where(channel == f * self.COLOURS + c, 1.0, 0.0)
                sign = jnp.where(inside, sign, 0.0).astype(BF16)
                planes = jnp.concatenate(
                    [frames[(img * 5 + f) * self.COLOURS + c] for img in range(images)], axis=0
                )
                part = dot(planes, sign)
                total = part if total is None else total + part
        for h in range(self.spread // LANES):
            S.columns[h] = total[:, h * LANES : (h + 1) * LANES]
        pooled = None
        for k in range(4):
            parts = [
                S.columns[h, pl.ds(k, self.half_rows, stride=4), :] for h in range(self.spread // LANES)
            ]
            part = jnp.concatenate(parts, axis=1)
            pooled = part if pooled is None else pooled + part
        pooled = (pooled * 0.0625).astype(BF16).astype(F32)
        row = lax.rem(lax.broadcasted_iota(jnp.int32, pooled.shape, 0), self.pairs)
        for ki in range(3):
            rolled = pltpu.roll(pooled, (1 - ki) % self.half_rows, 0)
            ok = (row + ki - 1 >= 0) & (row + ki - 1 < self.pairs)
            rolled = jnp.where(ok, rolled, 0.0).astype(BF16)
            at = lanes(self.fine + ki * self.spread, self.spread)
            xx[0 : self.half_rows, at] = rolled
            xx[self.half_rows :, at] = rolled

    def forward(self, sums, at):
        S, per = self.S, self.S.grads.shape[1]
        for n in range(self.pairs * LANES // per):
            table, top = self._part(n)
            S.pre[:, lanes(n * per, per)] = dot(S.xx[...], table[top : top + self.depth, :])
        s = q = jnp.zeros((8, LANES), F32)
        for k in range(self.pairs):
            v = S.pre[:, lanes(k * LANES)]
            s, q = s + fold(v), q + fold(v * v)
        self._put(sums, at, s, q)

    def _put(self, sums, at, s, q):
        for row, part in enumerate((s, q)):
            part = total_of(part)
            sums.put(row, at, part + pltpu.roll(part, 64, 1))

    def _norm(self):
        S, inv = self.S, 1.0 / self.count
        mean = S.stem_stat[0:1, :] * inv
        root = lax.rsqrt(S.stem_stat[1:2, :] * inv - mean * mean + 1e-05)
        gain, bias = self.R.stem_gain[...], self.R.stem_bias[...]
        scale = root * jnp.concatenate([gain, gain], axis=1)
        return scale, jnp.concatenate([bias, bias], axis=1) - mean * scale, mean, root

    def rear(self, stat, sums, at):
        S = self.S
        S.stem_stat[...] = stat
        scale, shift, mean, root = self._norm()
        step = 2 * self.cells
        S.stem_wide[:, 0:64] = S.stem_cot[...].astype(F32)
        s = q = jnp.zeros((8, LANES), F32)
        for k in range(self.pairs):
            pre = S.pre[:, lanes(k * LANES)]
            cot = []
            for parity in range(2):
                pieces = [
                    S.stem_wide[pl.ds(parity * self.cells + 2 * k + i, self.half_rows, stride=step), 0:64]
                    for i in range(2)
                ]
                cot.append(jnp.concatenate(pieces, axis=1))
            y = pre * scale + shift
            sg = jax.nn.sigmoid(y)
            out = y * sg
            g = jnp.concatenate(cot, axis=0) * (sg + out * (1.0 - sg))
            S.gpre[:, lanes(k * LANES)] = g
            s, q = s + fold(g), q + fold(g * ((pre - mean) * root))
            swapped = pltpu.roll(out, 64, 1)
            for parity in range(2):
                rows = slice(parity * self.half_rows, (parity + 1) * self.half_rows)
                for i, half in enumerate((out, swapped)):
                    where = pl.ds(parity * self.cells + 2 * k + i, self.half_rows, stride=step)
                    S.stem_wide[where, :] = half[rows]
        S.stem_cot[...] = S.stem_wide[:, 0:64].astype(BF16)
        self._put(sums, at, s, q)

    def back(self, stat, top):
        S, inv = self.S, 1.0 / self.count
        scale, _, mean, root = self._norm()
        gb, gg = stat[0:1, :] * inv, stat[1:2, :] * inv
        bands, spots = S.bands, S.spots
        bands[...] = jnp.zeros(bands.shape, F32)
        spots[...] = jnp.zeros(spots.shape, F32)
        for k in range(self.pairs):
            hat = (S.pre[:, lanes(k * LANES)] - mean) * root
            g = (scale * (S.gpre[:, lanes(k * LANES)] - gb - hat * gg)).astype(BF16)
            S.prod[...] = dot_at(S.xx[...], g)
            for c in range(self.COLOURS):
                for p in range(5):
                    j = 4 * k - 2 + 2 * p
                    if 0 <= j < self.side:
                        here = slice((c * 5 + p) * 16, (c * 5 + p) * 16 + 16)
                        start = c * self.band + j * 8
                        bands[here] = bands[here] + S.prod[start : start + 16]
            for ki in range(3):
                for kj in range(3):
                    j = k + kj - 1
                    if 0 <= j < self.pairs:
                        here = slice((ki * 3 + kj) * 16, (ki * 3 + kj) * 16 + 16)
                        start = self.fine + ki * self.spread + j * 16
                        spots[here] = spots[here] + S.prod[start : start + 16]
        low = lax.broadcasted_iota(jnp.int32, (8, LANES), 1) < 64
        for c in range(self.COLOURS):
            for kj in range(self.KERNEL):
                first = bands[c * 80 + kj * 8 : c * 80 + kj * 8 + 8]
                other = bands[c * 80 + kj * 8 + 16 : c * 80 + kj * 8 + 24]
                at = (c * self.KERNEL + kj) * 8
                S.wt[at : at + 8] = jnp.where(low, first + pltpu.roll(other, 64, 1), 0.0)
        grads = S.grads
        grads[top : top + LANES, :] = jnp.zeros((LANES, grads.shape[1]), BF16)
        rest = S.wt.shape[0] - LANES
        used = self.COLOURS * self.KERNEL * 8
        S.wt[used:] = jnp.zeros((S.wt.shape[0] - used, LANES), F32)
        grads[top : top + LANES, lanes(0)] = S.wt[0:LANES].astype(BF16)
        grads[top : top + rest, lanes(LANES)] = S.wt[LANES:].astype(BF16)
        both = spots[...] + pltpu.roll(spots[...], 64, 1)
        grads[top : top + LANES, lanes(2 * LANES)] = both[0:LANES].astype(BF16)
        grads[top : top + 16, lanes(3 * LANES)] = both[LANES:].astype(BF16)


class Layout:
    def __init__(self, wide, mid, red):
        taps = len(TAPS)
        self.excite = 0
        self.scales = self.excite + red * wide // mid
        self.scale_taps = mid // red
        groups = -(-2 * taps // self.scale_taps)
        self.squeeze = self.scales + groups * red
        self.stem = self.squeeze + wide * red // mid
        self.expand = self.stem + LANES
        self.reduce = self.expand + wide
        self.rows = self.reduce + wide
        self.spatial_in = mid // 2
        self.spatial_block = taps * self.spatial_in
        self.share_rows = 8 * self.spatial_block

    def plans(self, clips, segs):
        quarter = (self.reduce - self.expand) // 4
        half = (self.rows - self.reduce) // 2

        def plan(first, end, letters, nest):
            return Plan(clips, segs, first, end - first, letters, nest)

        bounds = list(range(0, self.expand, 512)) + [self.expand]
        early = [plan(bounds[k], bounds[k + 1], *orders) for k, orders in enumerate(EARLY)]
        middle = [
            plan(self.expand + k * quarter, self.expand + (k + 1) * quarter, *orders)
            for k, orders in enumerate(MIDDLE)
        ]
        late = [plan(self.reduce, self.reduce + half, *LATE[0]), plan(self.reduce + half, self.rows, *LATE[1])]
        return early, middle, late

    def shared_plans(self, clips, segs):
        parts, first = [], 0
        for k, nest in enumerate(SPATIAL):
            count = min(2, len(TAPS) - 2 * k)
            rows = 8 * count * self.spatial_in
            parts.append((2 * k, count, Plan(clips, segs, first, rows, "cxypq", nest, "cxy")))
            first += rows
        return parts


EARLY = (("cypxq", "cxypq"), ("cpqyx", "cyxpq"), ("cxypq", "cyxpq"), ("cyxpq", "cpxqy"))
MIDDLE = (("cyxpq", "cyxpq"), ("cpyqx", "cxypq"), ("cpyxq", "cxpqy"), ("cxpqy", "cyxpq"))
SPATIAL = ("cpxyq", "cyxpq", "cyxpq", "cyxpq", "cxpyq")
LATE = (("cyxpq", "cpyqx"), ("cyxpq", "cxpqy"))
SLOTS = (
    (1, 0),
    (2, 1, 0, 2),
    (1, 0, 2),
    (),
    (),
    (),
    (2, 6, 7, 1, 0, 4, 5),
    (),
    (6, 7, 3, 4, 5, 2, 1, 3, 0),
    (),
    (),
    (6, 7, 1, 4, 3, 5, 2),
    (0, 7, 1, 2),
    (),
    (7, 13, 0, 14),
    (2, 6, 1, 3, 13, 4, 5, 14, 8),
    (2, 7, 9, 3, 0, 4),
    (6, 1, 10, 5, 8),
    (),
    (7, 9, 3, 12, 13, 11, 4, 5),
    (),
    (6, 7, 10, 8),
    (9, 12, 14, 13, 11, 4, 5, 7, 10, 2, 0, 2, 13, 8, 14, 9, 12, 4, 5, 1, 3, 11, 6, 1, 10, 14, 0, 13, 7, 4, 9, 0, 3, 12, 7, 8, 11, 5, 13, 10, 6, 14, 4, 9, 3, 12, 11, 4, 3, 14, 8, 13, 6, 12, 5, 5, 14, 9, 10, 9, 13, 11, 8, 6, 8, 14, 6, 10, 12, 10, 12, 13, 11, 13, 14, 11, 14),
)


def block_kernel(clips, segs, grid, names, sc_names, *refs):
    R = SimpleNamespace(**dict(zip(names, refs[: len(names)])))
    S = SimpleNamespace(**dict(zip(sc_names, refs[len(names) :])))
    rows, wide = S.x.shape
    mid, red = S.f1.shape[1], S.sq.shape[1]
    cells = grid * grid
    images = rows // cells
    lay = Layout(wide, mid, red)
    blocks = range(0, rows, BLOCK)
    ntap = len(TAPS)
    place = Place(clips, segs)
    local, sends, recvs = Sems(S.local), Sems(S.send), Sems(S.recv)

    wfine = S.wfc.at[pl.ds(0, ntap * red)]
    wcoarse = S.wfc.at[pl.ds(ntap * red, ntap * red)]

    def load(src, dst):
        copy = pltpu.make_async_copy(src, dst, local.take())
        copy.start()
        return copy

    x_load, wr_load = load(R.x, S.x), load(R.wr, S.wr)

    def other_loads():
        return SimpleNamespace(
            frames=load(R.frames, S.frames),
            ws=load(R.ws, S.ws),
            we=load(R.we, S.we),
            wq=load(R.wq, S.wq),
            wf=load(R.wf, wfine),
            wc=load(R.wc, wcoarse),
            wx=load(R.wx, S.wx),
            cot=load(R.cot, S.cot),
            stem_cot=load(R.stem_cot, S.stem_cot),
        )

    place.greet()

    groups = R.groups
    total_groups = groups.shape[0]

    def side_of(group):
        return 5 + 2 * group - group // 2

    def area(k, acc):
        side = side_of(groups[k])
        return acc + side * side

    cell = lax.broadcasted_iota(jnp.int32, (cells, LANES), 0)
    ci, cj = cell >> log2(grid), cell & (grid - 1)
    for img in range(images):
        side = side_of(groups[place.clip * images + img])
        S.mask[img * cells : (img + 1) * cells] = jnp.where((ci < side) & (cj < side), 1.0, 0.0).astype(F32)
    half = grid // 2
    mask, tap, tap_small = S.mask, S.tap, S.tap_small

    def parent_of(row):
        i, j = (row & (cells - 1)) >> log2(grid), row & (grid - 1)
        return (row >> log2(cells)) * half * half + (i >> 1) * half + (j >> 1)

    def prepare():
        small = cell & (half * half - 1)
        si, sj = small >> log2(half), small & (half - 1)
        for t, (di, dj) in enumerate(TAPS):
            ok = (ci + di >= 0) & (ci + di < grid) & (cj + dj >= 0) & (cj + dj < grid)
            tap[t] = jnp.where(ok, 1.0, 0.0).astype(F32)
            ok = (si + di >= 0) & (si + di < half) & (sj + dj >= 0) & (sj + dj < half)
            tap_small[t] = jnp.where(ok, 1.0, 0.0).astype(F32)
        shape = (images * half * half, rows)
        here = lax.broadcasted_iota(jnp.int32, shape, 0) == parent_of(lax.broadcasted_iota(jnp.int32, shape, 1))
        S.pool[...] = jnp.where(here, 0.25, 0.0).astype(BF16)
        here = lax.broadcasted_iota(jnp.int32, shape[::-1], 1) == parent_of(
            lax.broadcasted_iota(jnp.int32, shape[::-1], 0)
        )
        S.up[...] = jnp.where(here, 1.0, 0.0).astype(BF16)
        for ref in (S.tmp, S.z, S.tmp_small, S.h1_all):
            ref[:PAD] = jnp.zeros((PAD, ref.shape[1]), F32)
            ref[ref.shape[0] - PAD :] = jnp.zeros((PAD, ref.shape[1]), F32)
        count = lax.fori_loop(0, total_groups, area, jnp.int32(0)) * segs
        return 1.0 / jnp.full((1, LANES), count.astype(F32), F32)

    grads = S.grads

    near = [S.near0, S.near1, S.near2, S.near3, S.near4, S.near5]
    far = [S.far0, S.far1, S.far2, S.far3, S.far4, S.far5]
    stats = [S.res0, S.res1, S.res2, S.res3, S.res4, S.res5]

    def sums(k):
        return Sums(place, near[k], far[k], stats[k], sends, recvs)

    all_sums = [sums(k) for k in range(6)]

    def local_moments(src, width, ar, masked):
        def body(at, j):
            s = q = jnp.zeros((8, LANES), F32)
            for r in blocks:
                v = src[r : r + BLOCK, lanes(at)]
                w = v * mask[r : r + BLOCK] if masked else v
                s, q = s + fold(w), q + fold(w * v)
            ar.put(0, at, total_of(s))
            ar.put(1, at, total_of(q))

        columns(width, body)

    gains = [R.gain_one, R.gain_two, R.gain_three]
    biases = [R.bias_one, R.bias_two, R.bias_three]

    def affine(k, at):
        stat = stats[k]
        mean = stat[0:1, lanes(at)] * inv
        spread = stat[1:2, lanes(at)] * inv - mean * mean
        root = lax.rsqrt(spread + 1e-05)
        scale = root * gains[k][0:1, lanes(at)]
        return scale, biases[k][0:1, lanes(at)] - mean * scale, mean, root

    def spread_taps(tmp, masks, per, count, stride, store):
        for t, (di, dj) in enumerate(TAPS):
            off = PAD + di * stride + dj
            for r in range(0, count, BLOCK):
                v = tmp[r + off : r + off + BLOCK, :] * masks[t, r % per : r % per + BLOCK]
                store(t, r, v)

    def gather_taps(z, width, masks, per, r, stride, at):
        acc = None
        for t, (di, dj) in enumerate(TAPS):
            off = PAD + r + di * stride + dj
            v = z[off : off + BLOCK, lanes((ntap - 1 - t) * width + at)] * masks[t, r % per : r % per + BLOCK]
            acc = v if acc is None else acc + v
        return acc

    stem = Stem(R, S, images, S.frames.shape[1], float(S.stem_cot.shape[0] * clips * segs))
    sems = (local, sends, recvs)
    jobs, land = [], 0
    for plan in [plan for group in lay.plans(clips, segs) for plan in group]:
        job = Job(place, plan, (grads, S.landing, R.packed), plan.first, land, sems)
        land = job.land_end
        jobs.append(job)
    shared, land, held = [], 0, 0
    for _, _, plan in lay.shared_plans(clips, segs):
        job = Job(place, plan, (S.shares, S.share_landing, R.shared), held, land, sems)
        land, held = job.land_end, held + plan.block
        shared.append(job)
    jobs = jobs[:8] + shared + jobs[8:]
    slots = iter(SLOTS)

    def advance():
        for k in next(slots):
            jobs[k].step()

    def plane_send(view, slots):
        me, copies = place.plane_me, []
        for k in range(1, place.plane):
            t = lax.rem(me + k, place.plane)
            copies.append(remote(view(t), slots.at[me], sends, recvs, place.plane_device(t)))
        own = pltpu.make_async_copy(view(me), slots.at[me], local.take())
        own.start()
        return copies + [own]

    x_load.wait()
    x = S.x

    def cut(at, j):
        for r in blocks:
            x[r : r + BLOCK, lanes(at)] = (x[r : r + BLOCK, lanes(at)].astype(F32) * mask[r : r + BLOCK]).astype(BF16)

    columns(wide, cut)

    wr_load.wait()
    S.f1[...] = dot(x[...], S.wr[...])
    local_moments(S.f1, mid, all_sums[0], False)
    place.greeted()
    all_sums[0].start()
    loads = other_loads()
    inv = prepare()
    stem.tables()
    all_sums[0].middle()
    loads.frames.wait()
    stem.patches()
    all_sums[0].finish()

    def hidden_one(at, j):
        scale, shift, _, _ = affine(0, at)
        for r in blocks:
            y = S.f1[r : r + BLOCK, lanes(at)] * scale + shift
            S.tmp[PAD + r : PAD + r + BLOCK, :] = y * jax.nn.sigmoid(y) * mask[r : r + BLOCK]

        def store(t, r, v):
            S.col[r : r + BLOCK, lanes(pl.multiple_of(t * mid + at, LANES))] = v.astype(BF16)

        spread_taps(S.tmp, tap, cells, rows, grid, store)

    columns(mid, hidden_one)
    me, centre = place.plane_me, ntap // 2 * mid
    sibling = me + 1 - 2 * lax.rem(me, 2)

    def half_inputs(t):
        start = pl.multiple_of(centre + t // 4 * lay.spatial_in, lay.spatial_in)
        return S.col.at[:, pl.ds(start, lay.spatial_in)]

    def same_core(k):
        return lax.rem(me // 2 + k, 4) * 2 + lax.rem(me, 2)

    def h1_send():
        copies = [
            remote(half_inputs(same_core(k)), S.h1_in.at[me], sends, recvs, place.plane_device(same_core(k)))
            for k in range(1, 4)
        ]
        own = pltpu.make_async_copy(half_inputs(me), S.h1_in.at[me], local.take())
        own.start()
        return copies, [remote(half_inputs(me), S.h1_in.at[me], sends, recvs, place.plane_device(sibling)), own]

    def h1_relay(copies):
        more = []
        for copy in copies:
            copy.wait()
        for k in range(1, 4):
            block = S.h1_in.at[same_core(k)]
            more.append(remote(block, block, sends, recvs, place.plane_device(sibling)))
        return more
    loads.ws.wait()
    S.f2[...] = dot(S.col[...], S.ws[...])
    local_moments(S.f2, mid, all_sums[1], True)
    all_sums[1].start()
    stem.forward(all_sums[2], wide)
    all_sums[1].middle()
    h1_far, h1_copies = h1_send()
    all_sums[1].finish()

    def hidden_two(at, j):
        scale, shift, _, _ = affine(1, at)
        for r in blocks:
            y = S.f2[r : r + BLOCK, lanes(at)] * scale + shift
            S.h2[r : r + BLOCK, lanes(at)] = (y * jax.nn.sigmoid(y) * mask[r : r + BLOCK]).astype(BF16)

    columns(mid, hidden_two)
    loads.we.wait()
    S.f3[...] = dot(S.h2[...], S.we[...])
    local_moments(S.f3, wide, all_sums[2], False)
    all_sums[2].start()
    all_sums[2].middle()
    h1_copies = h1_copies + h1_relay(h1_far)
    all_sums[2].finish()

    def branch_low(at, j):
        scale, shift, _, _ = affine(2, at)
        for r in blocks:
            y = (S.f3[r : r + BLOCK, lanes(at)] * scale + shift) * mask[r : r + BLOCK]
            S.branch[r : r + BLOCK, lanes(at)] = y.astype(BF16)

    columns(wide, branch_low)
    loads.wq.wait()
    S.sq[...] = dot(S.branch[...], S.wq[...]).astype(BF16)

    def swap(mine, slots):
        after, before = lax.rem(place.seg + 1, segs), lax.rem(place.seg + segs - 1, segs)
        copies = [
            remote(mine, slots.at[0], sends, recvs, (place.clip, after)),
            remote(mine, slots.at[1], sends, recvs, (place.clip, before)),
        ]
        return copies

    has_before = jnp.where(jnp.full((1, LANES), place.seg, jnp.int32) > 0, 1.0, 0.0).astype(F32)
    has_after = jnp.where(jnp.full((1, LANES), place.seg, jnp.int32) < segs - 1, 1.0, 0.0).astype(F32)
    copies = swap(S.sq, S.halo)
    loads.stem_cot.wait()
    stem.rear(stats[2][:, lanes(wide)], all_sums[3], wide)
    stem_copy = pltpu.make_async_copy(S.stem_cot, R.stem_out, local.take())
    stem_copy.start()
    for copy in copies:
        copy.wait()

    diffs = S.diffs
    for r in blocks:
        own = S.sq[r : r + BLOCK].astype(F32)
        later = S.halo[1, r : r + BLOCK].astype(F32) * has_after - own
        earlier = S.halo[0, r : r + BLOCK].astype(F32) * has_before - own
        diffs[r : r + BLOCK, lanes(0, red)] = later.astype(BF16)
        diffs[r : r + BLOCK, lanes(red, red)] = earlier.astype(BF16)
        S.tmp[PAD + r : PAD + r + BLOCK, :] = later.astype(BF16).astype(F32) + earlier.astype(BF16).astype(F32)

    def store_fine(t, r, v):
        S.cc[r : r + BLOCK, lanes(t * red, red)] = v.astype(BF16)

    spread_taps(S.tmp, tap, cells, rows, grid, store_fine)
    pooled = dot(S.pool[...], diffs[...]).astype(BF16).astype(F32)
    small_rows = pooled.shape[0]
    S.tmp_small[PAD : PAD + small_rows, :] = pooled[:, :red] + pooled[:, red:]

    def store_small(t, r, v):
        S.small_col[r : r + BLOCK, lanes(t * red, red)] = v.astype(BF16)

    spread_taps(S.tmp_small, tap_small, cells, small_rows, half, store_small)
    S.cc[:, lanes(ntap * red, ntap * red)] = dot(S.up[...], S.small_col[...]).astype(BF16)
    loads.wf.wait()
    loads.wc.wait()
    S.mo[...] = dot(S.cc[...], S.wfc[...]).astype(BF16)
    loads.wx.wait()
    S.gb[...] = dot(S.mo[...], S.wx[...])
    loads.cot.wait()

    def ends(at, j):
        scale, shift, _, _ = affine(2, at)
        for r in blocks:
            here = (slice(r, r + BLOCK), lanes(at))
            m = mask[r : r + BLOCK]
            branch = (S.f3[here] * scale + shift) * m
            gate = jax.nn.sigmoid(S.gb[here])
            z = x[here].astype(F32) + branch * (1.0 + gate)
            s = jax.nn.sigmoid(z)
            out = z * s
            gz = S.cot[here].astype(F32) * m * (s + out * (1.0 - s))
            S.cot[here] = (out * m).astype(BF16)
            S.gi[here] = gz
            S.gb[here] = gz * (1.0 + gate)
            S.g3[here] = (gz * branch * gate * (1.0 - gate)).astype(BF16)

    columns(wide, ends)
    out_copy = pltpu.make_async_copy(S.cot, R.block_out, local.take())
    out_copy.start()

    S.gm[...] = dot_bt(S.g3[...], S.wx[...]).astype(BF16)
    zf = dot_bt(S.gm[...], S.wfc[0 : ntap * red, :])
    S.z[PAD : PAD + rows, lanes(0, ntap * red)] = zf
    gmc = lax.dot_general(S.up[...], S.gm[...], (((0,), (0,)), ((), ())), preferred_element_type=F32).astype(BF16)
    S.z[PAD : PAD + small_rows, lanes(ntap * red, ntap * red)] = dot_bt(gmc, S.wfc[ntap * red :, :])
    S.z[PAD + small_rows : PAD + small_rows + PAD, lanes(ntap * red, ntap * red)] = jnp.zeros((PAD, ntap * red), F32)
    coarse = gather_taps(S.z, red, tap_small, cells, 0, half, ntap * red)
    coarse = dot_at(S.pool[...], coarse.astype(BF16))
    for r in blocks:
        gd = gather_taps(S.z, red, tap, cells, r, grid, 0) + coarse[r : r + BLOCK]
        S.gd[r : r + BLOCK] = gd
        S.gd_low[r : r + BLOCK] = gd.astype(BF16)
    copies = swap(S.gd_low, S.halo2)
    last = lay.squeeze - red
    grads[last : lay.squeeze] = jnp.zeros((red, mid), BF16)
    for b in range(wide // mid):
        grads[lay.excite + b * red : lay.excite + (b + 1) * red] = dot_at(
            S.mo[...], S.g3[:, lanes(b * mid, mid)]
        ).astype(BF16)
    for t in range(2 * ntap):
        top = lay.scales + t // lay.scale_taps * red
        grads[top : top + red, lanes(t % lay.scale_taps * red, red)] = dot_at(
            S.cc[:, lanes(t * red, red)], S.gm[...]
        ).astype(BF16)
    advance()
    for copy in copies:
        copy.wait()
    for r in blocks:
        g = S.halo2[0, r : r + BLOCK].astype(F32) * has_before + S.halo2[1, r : r + BLOCK].astype(F32) * has_after
        S.gsq[r : r + BLOCK] = (g - 2.0 * S.gd[r : r + BLOCK]).astype(BF16)
    S.z[PAD : PAD + rows, lanes(0, wide)] = dot_bt(S.gsq[...], S.wq[...])

    def branch_grad(at, j):
        _, _, mean, root = affine(2, at)
        s = q = jnp.zeros((8, LANES), F32)
        for r in blocks:
            here = (slice(r, r + BLOCK), lanes(at))
            g = (S.gb[here] + S.z[PAD + r : PAD + r + BLOCK, lanes(at)]) * mask[r : r + BLOCK]
            S.gb[here] = g
            s, q = s + fold(g), q + fold(g * ((S.f3[here] - mean) * root))
        all_sums[3].put(0, at, total_of(s))
        all_sums[3].put(1, at, total_of(q))

    columns(wide, branch_grad)
    all_sums[3].start()
    for b in range(mid // red):
        grads[lay.squeeze : lay.squeeze + mid, lanes(b * red, red)] = dot_at(
            S.branch[:, lanes(b * mid, mid)], S.gsq[...]
        ).astype(BF16)
    advance()
    all_sums[3].middle()
    advance()
    for copy in h1_copies:
        copy.wait()

    def widen(k, carry):
        for r in blocks:
            start = pl.multiple_of(k * rows + r, BLOCK)
            S.h1_all[pl.ds(PAD + start, BLOCK)] = S.h1_in[k, r : r + BLOCK].astype(F32)
        return carry

    lax.fori_loop(0, place.plane, widen, 0)
    all_sums[3].finish()
    advance()

    def through(k, back, src, given, dst, width):
        stat = stats[back]

        def body(at, j):
            scale, _, mean, root = affine(k, at)
            gb, gg = stat[0:1, lanes(at)] * inv, stat[1:2, lanes(at)] * inv
            for r in blocks:
                here = (slice(r, r + BLOCK), lanes(at))
                hat = (src[here] - mean) * root
                dst[here] = (scale * (given[here] - (gb + hat * gg) * mask[r : r + BLOCK])).astype(BF16)

        columns(width, body)

    def act_back(k, ar, src, value, at):
        scale, shift, mean, root = affine(k, at)
        s = q = jnp.zeros((8, LANES), F32)
        for r in blocks:
            here = (slice(r, r + BLOCK), lanes(at))
            a = src[here]
            y = a * scale + shift
            sg = jax.nn.sigmoid(y)
            g = value(r) * mask[r : r + BLOCK] * (sg * (1.0 + y * (1.0 - sg)))
            S.gy[here] = g
            s, q = s + fold(g), q + fold(g * ((a - mean) * root))
        ar.put(0, at, total_of(s))
        ar.put(1, at, total_of(q))

    through(2, 3, S.f3, S.gb, S.g3, wide)
    advance()
    S.gh[...] = dot_bt(S.g3[...], S.we[...])

    def back_two(at, j):
        act_back(1, all_sums[4], S.f2, lambda r: S.gh[r : r + BLOCK, lanes(at)], at)

    columns(mid, back_two)
    advance()
    all_sums[4].start()
    for b in range(wide // mid):
        grads[lay.expand + b * mid : lay.expand + (b + 1) * mid] = dot_at(
            S.h2[...], S.g3[:, lanes(b * mid, mid)]
        ).astype(BF16)
    advance()
    stem.back(stats[3][:, lanes(wide)], lay.stem)
    advance()
    all_sums[4].middle()
    advance()
    all_sums[4].finish()
    advance()
    through(1, 4, S.f2, S.gy, S.g2, mid)

    def output_quarter(ref):
        return lambda t: ref.at[:, pl.ds(pl.multiple_of(lax.rem(t, 4) * LANES, LANES), LANES)]
    S.z[PAD : PAD + rows, :] = dot_bt(S.g2[...], S.ws[...])
    advance()

    def back_one(at, j):
        act_back(
            0,
            all_sums[5],
            S.f1,
            lambda r: gather_taps_at(S.z, mid, tap, cells, r, grid, at),
            at,
        )

    def gather_taps_at(z, width, masks, per, r, stride, at):
        acc = None
        for t, (di, dj) in enumerate(TAPS):
            off = PAD + r + di * stride + dj
            start = pl.multiple_of((ntap - 1 - t) * width + at, LANES)
            v = z[off : off + BLOCK, lanes(start)] * masks[t, r % per : r % per + BLOCK]
            acc = v if acc is None else acc + v
        return acc

    columns(mid, back_one)
    all_sums[5].start()

    g_copies = plane_send(output_quarter(S.g2), S.g2_in)
    advance()
    all_sums[5].middle()
    advance()
    all_sums[5].finish()
    advance()
    through(0, 5, S.f1, S.gy, S.g1, mid)
    for b in range(wide // mid):
        grads[lay.reduce + b * mid : lay.reduce + (b + 1) * mid] = dot_at(
            x[:, lanes(b * mid, mid)], S.g1[...]
        ).astype(BF16)
    advance()
    for copy in g_copies:
        copy.wait()
    all_rows = place.plane * rows
    g_all = S.g2_in[...].reshape(all_rows, LANES)
    for t, (di, dj) in enumerate(TAPS):
        off = PAD + di * grid + dj

        def shifted(k, carry):
            for r in range(0, rows, BLOCK):
                start = pl.multiple_of(k * rows + r, BLOCK)
                for at in range(0, lay.spatial_in, LANES):
                    v = S.h1_all[pl.ds(start, BLOCK + 2 * PAD), at : at + LANES][off : off + BLOCK]
                    v = v * tap[t, r % cells : r % cells + BLOCK]
                    S.h1_tap[pl.ds(start, BLOCK), at : at + LANES] = v.astype(BF16)
            return carry

        lax.fori_loop(0, place.plane, shifted, 0)
        block = dot_at(g_all, S.h1_tap[...])
        S.shares[t * lay.spatial_in : (t + 1) * lay.spatial_in] = block.T.astype(BF16)
        if t % 2 == 1 or t == ntap - 1:
            advance()
    S.z[PAD : PAD + rows, lanes(0, wide)] = dot_bt(S.g1[...], S.wr[...])
    advance()

    def features_grad(at, j):
        for r in blocks:
            here = (slice(r, r + BLOCK), lanes(at))
            g = (S.gi[here] + S.z[PAD + r : PAD + r + BLOCK, lanes(at)]) * mask[r : r + BLOCK]
            S.g3[here] = g.astype(BF16)

    columns(wide, features_grad)
    feat_copy = pltpu.make_async_copy(S.g3, R.grad_features, local.take())
    feat_copy.start()

    advance()
    advance()
    while jobs:
        jobs = [job for job in jobs if job.step() < 3]
    small = R.sums
    at = 0
    for k, width in ((5, mid), (4, mid), (3, wide + LANES)):
        small[:, lanes(at, width)] = stats[k][...]
        at += width
    stem_copy.wait()
    out_copy.wait()
    feat_copy.wait()


def block(clips, segs, feats, cot, res_group, deep, stem):
    (w_reduce, gain_one, bias_one, w_spatial, gain_two, bias_two, w_expand, gain_three, bias_three) = deep[:9]
    w_squeeze, w_fine, w_coarse, w_excite = deep[9:]
    images, _, grid, _, wide = feats.shape
    rows = images * grid * grid
    mid, red = w_reduce.shape[1], w_squeeze.shape[1]
    taps = len(TAPS)
    lay = Layout(wide, mid, red)
    small_rows = rows // 4
    frames, stem_cot, stem_weight, diff_weight, stem_gain, stem_bias = stem
    count, side, colours = frames.shape[2], frames.shape[3], frames.shape[5]
    kernel, channels = stem_weight.shape[0], stem_weight.shape[3]
    stem_cells = images * (side // 2) ** 2
    stem_rows = images * side // 2
    stem_lanes = side // 2 * channels
    depth = colours * side * 8 + 3 * 256
    inputs = dict(
        x=feats.reshape(rows, wide),
        cot=cot.reshape(rows, wide),
        groups=res_group,
        wr=w_reduce,
        ws=w_spatial.reshape(taps * mid, mid),
        we=w_expand,
        wq=w_squeeze,
        wf=w_fine.reshape(taps * red, red),
        wc=w_coarse.reshape(taps * red, red),
        wx=w_excite,
        gain_one=gain_one.reshape(1, mid),
        bias_one=bias_one.reshape(1, mid),
        gain_two=gain_two.reshape(1, mid),
        bias_two=bias_two.reshape(1, mid),
        gain_three=gain_three.reshape(1, wide),
        bias_three=bias_three.reshape(1, wide),
        frames=jnp.transpose(frames, (0, 1, 2, 5, 3, 4)).reshape(images * count * colours, side, side),
        stem_cot=stem_cot.reshape(stem_cells, channels),
        stem_w=jnp.transpose(stem_weight, (0, 2, 1, 3)).reshape(kernel * colours, kernel, channels),
        diff_w=diff_weight.reshape(len(TAPS), diff_weight.shape[2], channels),
        stem_gain=stem_gain.reshape(1, channels),
        stem_bias=stem_bias.reshape(1, channels),
    )
    outputs = dict(
        block_out=jax.ShapeDtypeStruct((rows, wide), BF16),
        grad_features=jax.ShapeDtypeStruct((rows, wide), BF16),
        packed=jax.ShapeDtypeStruct((lay.rows, mid), BF16),
        shared=jax.ShapeDtypeStruct((lay.share_rows, LANES), BF16),
        sums=jax.ShapeDtypeStruct((2, 2 * mid + wide + LANES), F32),
        stem_out=jax.ShapeDtypeStruct((stem_cells, channels), BF16),
    )

    def spec(name):
        if name == "groups":
            return pl.BlockSpec(memory_space=pltpu.SMEM)
        if inputs.get(name, frames).size < 1 << 15 or name == "sums":
            return pl.BlockSpec(memory_space=pltpu.VMEM)
        return pl.BlockSpec(memory_space=pl.ANY)

    plans = [plan for group in lay.plans(clips, segs) for plan in group]
    shared = [plan for _, _, plan in lay.shared_plans(clips, segs)]
    land = sum(plan.landing_rows for plan in plans)
    share_land = sum(plan.landing_rows for plan in shared)
    near, far = 2 * segs, clips // 2
    remote_count = sum(plan.transfers for plan in plans + shared) + 6 * (near + far) + 48
    v = pltpu.VMEM
    scratch = dict(
        x=v((rows, wide), BF16),
        cot=v((rows, wide), BF16),
        wr=v((wide, mid), BF16),
        ws=v((taps * mid, mid), BF16),
        we=v((mid, wide), BF16),
        wq=v((wide, red), BF16),
        wfc=v((2 * taps * red, red), BF16),
        wx=v((red, wide), BF16),
        mask=v((rows, LANES), F32),
        tap=v((taps, grid * grid, LANES), F32),
        tap_small=v((taps, grid * grid, LANES), F32),
        pool=v((small_rows, rows), BF16),
        up=v((rows, small_rows), BF16),
        tmp=v((rows + 2 * PAD, LANES), F32),
        tmp_small=v((small_rows + 2 * PAD, LANES), F32),
        small_col=v((small_rows, taps * red), BF16),
        f1=v((rows, mid), F32),
        f2=v((rows, mid), F32),
        f3=v((rows, wide), F32),
        col=v((rows, taps * mid), BF16),
        h2=v((rows, mid), BF16),
        branch=v((rows, wide), BF16),
        sq=v((rows, red), BF16),
        halo=v((2, rows, red), BF16),
        halo2=v((2, rows, red), BF16),
        diffs=v((rows, 2 * red), BF16),
        cc=v((rows, 2 * taps * red), BF16),
        mo=v((rows, red), BF16),
        gm=v((rows, red), BF16),
        gd=v((rows, red), F32),
        gd_low=v((rows, red), BF16),
        gsq=v((rows, red), BF16),
        gb=v((rows, wide), F32),
        gi=v((rows, wide), F32),
        g3=v((rows, wide), BF16),
        gh=v((rows, mid), F32),
        gy=v((rows, mid), F32),
        g2=v((rows, mid), BF16),
        g1=v((rows, mid), BF16),
        z=v((rows + 2 * PAD, taps * mid), F32),
        grads=v((lay.rows, mid), BF16),
        landing=v((land, mid), BF16),
        shares=v((lay.spatial_block, LANES), BF16),
        share_landing=v((share_land, LANES), BF16),
        h1_in=v((8, rows, lay.spatial_in), BF16),
        h1_all=v((8 * rows + 2 * PAD, lay.spatial_in), F32),
        h1_tap=v((8 * rows, lay.spatial_in), BF16),
        g2_in=v((8, rows, LANES), BF16),
        frames=v((images * count * colours, side, side), BF16),
        stem_cot=v((stem_cells, channels), BF16),
        stem_wide=v((stem_cells, LANES), F32),
        stem_stat=v((2, LANES), F32),
        padded=v((images * (side + 8), LANES), F32),
        stem_taps=v((stem_rows, 512), F32),
        columns=v((2, images * side, LANES), F32),
        xx=v((stem_rows, depth), BF16),
        pre=v((stem_rows, stem_lanes), F32),
        gpre=v((stem_rows, stem_lanes), F32),
        prod=v((depth, LANES), F32),
        bands=v((240, LANES), F32),
        spots=v((144, LANES), F32),
        wt=v((192, LANES), F32),
        wd=v((144, LANES), F32),
    )
    for k, width in enumerate((mid, mid, wide + LANES, wide + LANES, mid, mid)):
        scratch[f"near{k}"] = v((near, 2, width), F32)
        scratch[f"far{k}"] = v((far, 2, width), F32)
        scratch[f"res{k}"] = v((2, width), F32)
    scratch.update(
        local=pltpu.SemaphoreType.DMA((32,)),
        send=pltpu.SemaphoreType.DMA((remote_count,)),
        recv=pltpu.SemaphoreType.DMA((remote_count,)),
    )
    names = list(inputs) + list(outputs)
    result = pl.pallas_call(
        partial(block_kernel, clips, segs, grid, names, list(scratch)),
        out_shape=list(outputs.values()),
        in_specs=[spec(name) for name in inputs],
        out_specs=[spec(name) for name in outputs],
        scratch_shapes=list(scratch.values()),
        compiler_params=pltpu.CompilerParams(
            collective_id=0, has_side_effects=True, vmem_limit_bytes=VMEM_LIMIT
        ),
        name="block",
    )(*inputs.values())
    return result


VMEM_LIMIT = 62 << 20


AHEAD = 16


def spread_kernel(lay, plans, shared_plans, mid, red, wide, ins, outs, names, *refs):
    R = SimpleNamespace(**dict(zip(ins + outs + names, refs)))
    taps = len(TAPS)
    copies, out = [], []

    def read(src, dst):
        copies.append(pltpu.make_async_copy(src, dst, R.reads.at[len(copies)]))

    arrived = iter(range(len(plans) + len(shared_plans) + 3))

    def arrive():
        k = next(arrived)
        if k == 0:
            for copy in copies[:AHEAD]:
                copy.start()
        copies[k].wait()
        if k + AHEAD < len(copies):
            copies[k + AHEAD].start()

    def write(src, dst):
        copy = pltpu.make_async_copy(src, dst, R.writes.at[len(out)])
        copy.start()
        out.append(copy)

    for plan in plans[:8] + [plan for _, _, plan in shared_plans] + plans[8:]:
        here = pl.ds(plan.first, plan.rows)
        if plan in plans:
            read(R.packed.at[here], R.held.at[here])
        else:
            read(R.shared.at[here], R.shares.at[here])
    passed = [
        (R.block_out, R.block_held, R.out_block),
        (R.grad_features, R.features_held, R.out_features),
        (R.stem_out, R.stem_held, R.out_stem),
    ]
    for src, here, _ in passed:
        read(src, here)
    at = 0
    for bias, gain in (
        (R.bias_one, R.gain_one),
        (R.bias_two, R.gain_two),
        (R.bias_three, R.gain_three),
        (R.stem_bias, R.stem_gain),
    ):
        width = bias.shape[1]
        bias[...] = R.sums[0:1, at : at + width]
        gain[...] = R.sums[1:2, at : at + width]
        at += width
    full = R.full

    def wait_and_convert(plan):
        arrive()

        def convert(values):
            src = plan.packed_at(values)
            dst = plan.first + plan.summed_at(values)
            for r in range(0, plan.piece, 16):
                here = pl.ds(pl.multiple_of(dst + r, 16), 16)
                full[here] = R.held[pl.ds(pl.multiple_of(src + r, 16), 16)].astype(F32)

        plan.each_piece(convert)

    for plan in plans[:4]:
        wait_and_convert(plan)
    for b in range(wide // mid):
        write(full.at[pl.ds(lay.excite + b * red, red)], R.excite.at[:, pl.ds(b * mid, mid)])
    for t in range(2 * taps):
        top, at = lay.scales + t // lay.scale_taps * red, t % lay.scale_taps * red
        write(full.at[pl.ds(top, red), pl.ds(at, red)], (R.fine if t < taps else R.coarse).at[pl.ds(t % taps * red, red)])
    for b in range(mid // red):
        write(full.at[pl.ds(lay.squeeze, mid), pl.ds(b * red, red)], R.squeeze.at[pl.ds(b * mid, mid)])
    for k, plan in enumerate(plans[4:8]):
        wait_and_convert(plan)
        write(full.at[pl.ds(plan.first, mid)], R.expand.at[:, pl.ds(k * mid, mid)])

    for tap, count, plan in shared_plans:
        arrive()

        def convert(values):
            src, row = plan.packed_at(values), plan.summed_at(values)
            x, y, core = values[("clip", 1)], values[("seg", 2)], values[("seg", 1)]
            dst = (tap + row // lay.spatial_in) * mid + x * lay.spatial_in + row % lay.spatial_in
            at = lanes(pl.multiple_of((y * 2 + core) * LANES, LANES))
            for r in range(0, plan.piece, 16):
                here = pl.ds(pl.multiple_of(dst + r, 16), 16)
                R.full_spatial[here, at] = R.shares[pl.ds(pl.multiple_of(src + r, 16), 16)].astype(F32)

        plan.each_piece(convert)
        here = pl.ds(tap * mid, count * mid)
        write(R.full_spatial.at[here], R.spatial.at[here])
    for plan in plans[8:]:
        wait_and_convert(plan)
        write(full.at[pl.ds(plan.first, plan.rows)], R.reduce.at[pl.ds(plan.first - lay.reduce, plan.rows)])
    for _, here, dst in passed:
        arrive()
        write(here, dst)
    kernel, channels = R.stem_w.shape[1], R.stem_w.shape[2]
    colours = R.stem_w.shape[0] // kernel
    rest = R.rows.shape[0] - LANES
    R.rows[0:LANES] = full[lay.stem : lay.stem + LANES, lanes(0)]
    R.rows[LANES:] = full[lay.stem : lay.stem + rest, lanes(LANES)]
    for ki in range(kernel):
        for c in range(colours):
            part = R.rows[pl.ds(c * kernel * 8 + ki, kernel, stride=8), :]
            R.stem_w[ki * colours + c] = part[:, 0:channels]
    for t in range(taps):
        top, at = (lay.stem + t * 16, 2 * LANES) if t < 8 else (lay.stem, 3 * LANES)
        R.diff_w[t] = full[top : top + R.diff_w.shape[1], at : at + channels]
    for copy in out:
        copy.wait()


def spread(clips, segs, given, sizes):
    mid, red, wide, kernel, colours, channels, differences = sizes
    lay = Layout(wide, mid, red)
    taps = len(TAPS)
    plans = [plan for group in lay.plans(clips, segs) for plan in group]
    shared_plans = lay.shared_plans(clips, segs)

    def f32(*shape):
        return jax.ShapeDtypeStruct(shape, F32)

    outs = dict(
        out_block=given["block_out"],
        out_features=given["grad_features"],
        out_stem=given["stem_out"],
        reduce=f32(wide, mid),
        spatial=f32(taps * mid, mid),
        expand=f32(mid, wide),
        squeeze=f32(wide, red),
        fine=f32(taps * red, red),
        coarse=f32(taps * red, red),
        excite=f32(red, wide),
    )
    outs = {name: jax.ShapeDtypeStruct(out.shape, out.dtype) for name, out in outs.items()}
    small = dict(
        stem_w=f32(kernel * colours, kernel, channels),
        diff_w=f32(taps, differences, channels),
        bias_one=f32(1, mid),
        gain_one=f32(1, mid),
        bias_two=f32(1, mid),
        gain_two=f32(1, mid),
        bias_three=f32(1, wide),
        gain_three=f32(1, wide),
        stem_bias=f32(1, channels),
        stem_gain=f32(1, channels),
    )
    scratch = dict(
        held=pltpu.VMEM((lay.rows, mid), BF16),
        shares=pltpu.VMEM((lay.share_rows, LANES), BF16),
        full=pltpu.VMEM((lay.rows, mid), F32),
        full_spatial=pltpu.VMEM((taps * mid, mid), F32),
        rows=pltpu.VMEM((176, LANES), F32),
        block_held=pltpu.VMEM(given["block_out"].shape, BF16),
        features_held=pltpu.VMEM(given["grad_features"].shape, BF16),
        stem_held=pltpu.VMEM(given["stem_out"].shape, BF16),
        reads=pltpu.SemaphoreType.DMA((32,)),
        writes=pltpu.SemaphoreType.DMA((64,)),
    )
    here, anywhere = pl.BlockSpec(memory_space=pltpu.VMEM), pl.BlockSpec(memory_space=pl.ANY)
    names = list(outs) + list(small)
    results = pl.pallas_call(
        partial(
            spread_kernel, lay, plans, shared_plans, mid, red, wide, list(given), names, list(scratch)
        ),
        out_shape=list(outs.values()) + list(small.values()),
        in_specs=[here if array.size < 1 << 15 else anywhere for array in given.values()],
        out_specs=[anywhere] * len(outs) + [here] * len(small),
        scratch_shapes=list(scratch.values()),
        compiler_params=pltpu.CompilerParams(vmem_limit_bytes=VMEM_LIMIT),
        name="spread",
    )(*given.values())
    return SimpleNamespace(**dict(zip(names, results)))


def shards(
    frames,
    features,
    res_group,
    stem_weight,
    diff_weight,
    stem_gain,
    stem_bias,
    w_reduce,
    gain_one,
    bias_one,
    w_spatial,
    gain_two,
    bias_two,
    w_expand,
    gain_three,
    bias_three,
    w_squeeze,
    w_fine,
    w_coarse,
    w_excite,
    stem_cotangent,
    block_cotangent,
):
    clips, segs = lax.axis_size("clip"), lax.axis_size("seg")
    wide, mid, red = w_reduce.shape[0], w_reduce.shape[1], w_squeeze.shape[1]
    deep = (
        w_reduce, gain_one, bias_one, w_spatial, gain_two, bias_two, w_expand, gain_three, bias_three,
        w_squeeze, w_fine, w_coarse, w_excite,
    )
    stem = (frames, stem_cotangent, stem_weight, diff_weight, stem_gain, stem_bias)
    block_out, grad_feats, packed, shared, sums, stem_out = block(
        clips, segs, features, block_cotangent, res_group, deep, stem
    )
    kernel, colours, channels = stem_weight.shape[0], stem_weight.shape[2], stem_weight.shape[3]
    given = dict(
        packed=packed, shared=shared, sums=sums, block_out=block_out, grad_features=grad_feats, stem_out=stem_out
    )
    sizes = (mid, red, wide, kernel, colours, channels, diff_weight.shape[2])
    g = spread(clips, segs, given, sizes)
    g_stem_w = jnp.transpose(g.stem_w.reshape(kernel, colours, kernel, channels), (0, 2, 1, 3))
    return (
        g.out_stem.reshape(stem_cotangent.shape),
        g.out_block.reshape(features.shape),
        g.out_features.reshape(features.shape),
        g_stem_w,
        g.diff_w.reshape(diff_weight.shape),
        g.stem_gain.reshape(channels),
        g.stem_bias.reshape(channels),
        g.reduce,
        g.gain_one.reshape(mid),
        g.bias_one.reshape(mid),
        g.spatial.reshape(w_spatial.shape),
        g.gain_two.reshape(mid),
        g.bias_two.reshape(mid),
        g.expand,
        g.gain_three.reshape(wide),
        g.bias_three.reshape(wide),
        g.squeeze,
        g.fine.reshape(w_fine.shape),
        g.coarse.reshape(w_coarse.shape),
        g.excite,
    )


def solution(mesh):
    split = P("clip", "seg")
    whole = P()
    ins = (split, split) + (whole,) * 18 + (split, split)
    outs = (split,) * 3 + (whole,) * 17
    return jax.shard_map(shards, mesh=mesh, in_specs=ins, out_specs=outs, check_vma=False)
```
